256 devices in a mesh: ctx: 64 (over x, z, core), mp: 4 (over y).
Axes of the slice: x: 4, y: 4, z: 8, core: 2. Of those that a mesh axis runs over, the one named last changes fastest.
Arguments:
- hidden: bfloat16 [131072, 512], P('ctx', 'mp'), may hold values from -6 to 6
- w_x: bfloat16 [512, 1024], P(None, 'mp'), may hold values from -0.25 to 0.25
- w_z: bfloat16 [512, 1024], P(None, 'mp'), may hold values from -0.25 to 0.25
- w_bc: bfloat16 [512, 256], replicated, may hold values from -0.25 to 0.25
- w_dt: bfloat16 [512, 16], P(None, 'mp'), may hold values from -0.25 to 0.25
- conv_x: float32 [4, 1024], P(None, 'mp'), may hold values from -3 to 3
- conv_bc: float32 [4, 256], replicated, may hold values from -3 to 3
- dt_bias: float32 [16], P('mp'), may hold values from -5 to -3
- decay_rate: float32 [16], P('mp'), may hold values from 2e-06 to 2
- skip_gain: float32 [16], P('mp'), may hold values from 0.1 to 1.9
- norm_gain: float32 [1024], P('mp'), may hold values from 0.1 to 1.9
- w_out: bfloat16 [1024, 512], P('mp'), may hold values from -0.1875 to 0.1875
- piece_lengths: int32 [16], replicated, may hold values from 1 to 65536, 131072 in all
Outputs:
- layer_out: bfloat16 [131072, 512], P('ctx', 'mp')
The draws below stay inside these ranges and needn't reach their ends.
Inputs may be any that keep to these rules, and one draw needn't show every extreme that they name: `piece_lengths`: the piece lengths add up to 131072, and the longest is exactly 65536.
All inputs are finite; a program needn't handle non-finite values.
Results may differ from the reference program's by a relative error of at most 0.015.
Values may be sent and summed in bfloat16 or wider, within the bound.
No kernel may reach another device: no remote copies, remote signals or barrier semaphores. Data moves between devices by JAX's collectives and lax.ppermute only.
A program may use at most 128 MiB of HBM per device.

```python
import math
import jax
import jax.numpy as jnp
import numpy as np
from jax import lax

D = 512
E = 1024
HEAD_DIM = 64
HEADS = 16
NSTATE = 128
BLOCK = 256
TOK_DEV = 2048
TOKENS = 131072
PIECES = 16
MOST = 65536


def draw_hidden(key, part):
    key = jax.random.fold_in(key, 11)
    key_noise = jax.random.fold_in(key, 1)
    key_offset = jax.random.fold_in(key, 2)
    block_total = TOKENS // TOK_DEV
    offset = 0.4 * jax.random.normal(key_offset, (block_total, 1, D), jnp.float32)
    noise = jax.random.normal(key_noise, (block_total, TOK_DEV, D), jnp.float32)
    values = jnp.clip(noise + offset, -6.0, 6.0)
    return values.reshape(TOKENS, D).astype(jnp.bfloat16)


def block_scale(own_key, extent, pieces, least, high):
    level = 1.0
    for dim, blocks in pieces:
        steps = jax.random.uniform(jax.random.fold_in(jax.random.fold_in(own_key, 6), dim), (blocks,), jnp.float32, least / len(pieces), high / len(pieces))
        level = level * jnp.repeat(jnp.exp(steps), extent[dim] // blocks).reshape((-1,) + (1,) * (len(extent) - 1 - dim))
    return level


def profile(count, total, reach, lean):
    portions = [(1 << 20) // math.isqrt(grade ** lean) + 1 for grade in range(2, count + 1)]
    surplus, counts = total - reach - (count - 1), [1] * (count - 1)
    while surplus > 0:
        movable = [i for i in range(count - 1) if counts[i] < reach]
        mass, remaining = sum([portions[i] for i in movable]), surplus
        for i in movable:
            more = min(reach - counts[i], max(1, remaining * portions[i] // mass), surplus)
            counts[i] = counts[i] + more
            surplus = surplus - more
    return np.array([reach] + counts)


def uneven(own_key, number_of, total, most, lean):
    if number_of == 2:
        one = jax.random.randint(own_key, (), max(1, total - most), min(most, total - 1) + 1)
        return jnp.stack([one, total - one])
    tallies = jnp.asarray(profile(number_of, total, most, lean), jnp.int32)
    pairs = (number_of - 1) // 2
    donor, taker = tallies[1:1 + 2 * pairs:2], tallies[2:2 + 2 * pairs:2]
    room = jnp.minimum(donor - 1, most - taker)
    moved = jax.random.randint(jax.random.fold_in(own_key, 1), (pairs,), 0, 1 << 20) % (room + 1)
    tallies = tallies.at[1:1 + 2 * pairs:2].set(donor - moved).at[2:2 + 2 * pairs:2].set(taker + moved)
    return tallies[jax.random.permutation(jax.random.fold_in(own_key, 2), number_of)]


def gaussian(rng, dims, spread, most, cuts=(), held_as=jnp.bfloat16):
    factor_of = block_scale(rng, dims, cuts, -0.22, 0.18) if cuts else 1.0
    result = jax.random.normal(rng, dims, jnp.float32) * spread * factor_of
    return jnp.minimum(jnp.maximum(result, -most), most).astype(held_as)


def setup_inputs(seed: int = 0) -> dict:
    seeds = jax.random.split(jax.random.key(seed), 14)
    return {
        "hidden": draw_hidden(jax.random.fold_in(seeds[13], 71), 0),
        "w_x": gaussian(seeds[1], (D, E), D ** -0.5, 0.25, ((1, 4),)),
        "w_z": gaussian(seeds[2], (D, E), D ** -0.5, 0.25, ((1, 4),)),
        "w_bc": gaussian(seeds[3], (D, 2 * NSTATE), D ** -0.5, 0.25),
        "w_dt": gaussian(seeds[4], (D, HEADS), D ** -0.5, 0.25, ((1, 4),)),
        "conv_x": gaussian(seeds[5], (4, E), 4 ** -0.5, 3.0, ((1, 4),), jnp.float32),
        "conv_bc": gaussian(seeds[6], (4, 2 * NSTATE), 4 ** -0.5, 3.0, (), jnp.float32),
        "dt_bias": jnp.clip(-5.0 + 2.0 * jax.random.uniform(seeds[7], (HEADS,), jnp.float32) ** block_scale(seeds[7], (HEADS,), ((0, 4),), -0.2, 0.2), -5.0, -3.0),
        "decay_rate": jnp.clip(jnp.exp(math.log(2.0) - 13.815511 * jax.random.uniform(seeds[8], (HEADS,), jnp.float32) ** block_scale(seeds[8], (HEADS,), ((0, 4),), -0.2, 0.2)), 1.9999999949504854e-06, 2.0),
        "skip_gain": jnp.clip(1.0 + 0.18 * jax.random.normal(seeds[9], (HEADS,), jnp.float32), 0.1, 1.9),
        "norm_gain": jnp.clip(1.0 + 0.18 * jax.random.normal(seeds[10], (E,), jnp.float32), 0.1, 1.9),
        "w_out": gaussian(seeds[11], (E, D), E ** -0.5, 0.1875, ((0, 4),)),
        "piece_lengths": uneven(seeds[12], PIECES, TOKENS, MOST, 2).astype(jnp.int32),
    }


HIGHEST_PREC = lax.Precision.HIGHEST
EPSILON = 1e-05

def piece_ids(first_pos, length, piece_lengths):
    boundary = jnp.cumsum(piece_lengths).astype(jnp.int32)
    position = first_pos + jnp.arange(length, dtype=jnp.int32)
    return lax.optimization_barrier(jnp.sum((position[:, None] >= boundary[None, :]).astype(jnp.int32), axis=1)).astype(jnp.int32)

def conv_pieces(conv_in, window_seg, conv_w):
    row_count = conv_in.shape[0] - 3
    summed = jnp.zeros((row_count, conv_in.shape[1]), jnp.float32)
    for tap_index in range(4):
        same_piece = (window_seg[tap_index:tap_index + row_count] == window_seg[3:]).astype(jnp.float32)
        summed = summed + conv_in[tap_index:tap_index + row_count].astype(jnp.float32) * conv_w[tap_index][None, :].astype(jnp.float32) * same_piece[:, None]
    return jax.nn.silu(summed).astype(jnp.bfloat16)

def scan_block(carry_state, inputs_x, b_rows, c_rows, step_dt, decay_rate, block_seg, seg_before):
    width_q = inputs_x.shape[0]
    log_decay = -step_dt * decay_rate[None, :]
    cumulated = jnp.cumsum(log_decay, axis=0)
    position = jnp.arange(width_q)
    causal = (block_seg[:, None] == block_seg[None, :]) & (position[:, None] >= position[None, :])
    scores = jnp.dot(c_rows, b_rows.T, preferred_element_type=jnp.float32)
    by_head = cumulated.T
    log_gap = by_head[:, :, None] - by_head[:, None, :]
    decays = jnp.where(causal[None], jnp.exp(jnp.where(causal[None], log_gap, 0.0)), 0.0)
    block_weights = (decays * scores[None] * step_dt.T[:, None, :]).astype(jnp.bfloat16)
    intra_part = jnp.einsum('hts,shp->thp', block_weights.astype(jnp.float32), inputs_x.astype(jnp.float32), precision=HIGHEST_PREC)
    from_start = jnp.exp(cumulated) * (block_seg == seg_before).astype(jnp.float32)[:, None]
    c_scaled = c_rows.astype(jnp.float32)[:, None, :] * from_start[:, :, None]
    inter_part = jnp.einsum('thn,hpn->thp', c_scaled, carry_state, precision=HIGHEST_PREC)
    to_end = jnp.exp(cumulated[-1][None, :] - cumulated) * (block_seg == block_seg[-1]).astype(jnp.float32)[:, None] * step_dt
    state_weights = (b_rows.astype(jnp.float32)[:, None, :] * to_end[:, :, None]).astype(jnp.bfloat16)
    state_added = jnp.einsum('shn,shp->hpn', state_weights.astype(jnp.float32), inputs_x.astype(jnp.float32), precision=HIGHEST_PREC)
    whole_decay = jnp.exp(cumulated[-1]) * (block_seg[-1] == seg_before).astype(jnp.float32)
    new_state = whole_decay[:, None, None] * carry_state + state_added
    return (new_state, intra_part + inter_part, cumulated)

def run_stream(stream_rows, stream_seg, w_in, conv_w, dt_bias, decay_rate, skip_gain, norm_gain, w_out):
    padded = jnp.concatenate([jnp.zeros((3, D), jnp.bfloat16), stream_rows], axis=0)
    seg_pad = jnp.concatenate([jnp.full((3,), -1, jnp.int32), stream_seg.astype(jnp.int32)], axis=0)
    mixing = E + 2 * NSTATE

    def advance(carry_state, block_index):
        offset = (block_index * BLOCK).astype(jnp.int32)
        window = lax.dynamic_slice_in_dim(padded, offset, BLOCK + 3, 0)
        window_seg = lax.dynamic_slice_in_dim(seg_pad, offset, BLOCK + 3, 0)
        projected = jnp.dot(window, w_in, preferred_element_type=jnp.float32).astype(jnp.bfloat16)
        conv_out = conv_pieces(projected[:, :mixing], window_seg, conv_w)
        gate_in = projected[3:, mixing:mixing + E]
        raw_dt = projected[3:, mixing + E:]
        step_dt = jax.nn.softplus(raw_dt.astype(jnp.float32) + dt_bias[None, :])
        inputs_x = conv_out[:, :E].reshape(BLOCK, HEADS, HEAD_DIM)
        b_rows = conv_out[:, E:E + NSTATE]
        c_rows = conv_out[:, E + NSTATE:]
        new_state, mixed_heads, cumulated = scan_block(carry_state, inputs_x, b_rows, c_rows, step_dt, decay_rate, window_seg[3:], window_seg[2])
        mixed_heads = mixed_heads + skip_gain[None, :, None] * inputs_x.astype(jnp.float32)
        gated = mixed_heads.reshape(BLOCK, E) * jax.nn.silu(gate_in.astype(jnp.float32))
        normed = (gated * lax.rsqrt(lax.optimization_barrier(jnp.mean(gated * gated, axis=1, keepdims=True)) + EPSILON) * norm_gain[None, :]).astype(jnp.bfloat16)
        return (new_state, jnp.dot(normed, w_out, preferred_element_type=jnp.float32))
    start_state = jnp.zeros((HEADS, HEAD_DIM, NSTATE), jnp.float32)
    final_state, outputs = lax.scan(advance, start_state, jnp.arange(TOKENS // BLOCK, dtype=jnp.int32))
    return outputs.reshape(TOKENS, D)

def reference(hidden, w_x, w_z, w_bc, w_dt, conv_x, conv_bc, dt_bias, decay_rate, skip_gain, norm_gain, w_out, piece_lengths):
    w_in = jnp.concatenate([w_x, w_bc, w_z, w_dt], axis=1)
    conv_w = jnp.concatenate([conv_x, conv_bc], axis=1)
    seq_piece = piece_ids(0, TOKENS, piece_lengths)
    forward = run_stream(hidden, seq_piece, w_in, conv_w, dt_bias, decay_rate, skip_gain, norm_gain, w_out)
    backward = run_stream(hidden[::-1, ::-1], seq_piece[::-1], w_in, conv_w, dt_bias, decay_rate, skip_gain, norm_gain, w_out)
    return (forward + backward[::-1, ::-1]).astype(jnp.bfloat16)
```

```python
import functools

import jax
import jax.numpy as jnp
import numpy as np
from jax import lax
from jax.experimental import pallas as pl
from jax.experimental.pallas import tpu as pltpu
from jax.sharding import PartitionSpec as P

E = 1024
HEAD_DIM = 64
NSTATE = 128
BLOCK = 256
HEADS_HERE = 4
INNER = HEADS_HERE * HEAD_DIM
PIECES = 16
EPSILON = 1e-05
FAR = -1e30
EDGE = 16
MIX = INNER + NSTATE
PAY = NSTATE + 16
VMEM_BYTES = 56 * 1024 * 1024

bf16 = jnp.bfloat16
f32 = jnp.float32


def head_spread():
    out = np.zeros((16, 2 * INNER), np.float32)
    for part in range(2):
        for stream in range(2):
            for h in range(HEADS_HERE):
                first = stream * INNER + h * HEAD_DIM
                out[part * 8 + stream * 4 + h, first : first + HEAD_DIM] = 1.0
    return out


def whole(shape):
    return pl.BlockSpec(shape, lambda *_: (0,) * len(shape))


SMEM = pl.BlockSpec(memory_space=pltpu.SMEM)


def params():
    return pltpu.CompilerParams(
        dimension_semantics=("arbitrary",), vmem_limit_bytes=VMEM_BYTES
    )


def cost(flops, nbytes):
    return pl.CostEstimate(flops=int(flops), bytes_accessed=int(nbytes), transcendentals=0)


def bounds_of(pieces_ref):
    total = pieces_ref[0]
    ends = [total]
    for k in range(1, PIECES):
        total = total + pieces_ref[k]
        ends.append(total)
    return ends


def seg_rows(ends, first):
    shape = (8, BLOCK)
    pos = (
        first - 3 + lax.broadcasted_iota(jnp.int32, shape, 0)
        + lax.broadcasted_iota(jnp.int32, shape, 1)
    )
    seg = jnp.zeros(shape, jnp.int32)
    for end in ends:
        seg = seg + (pos >= end).astype(jnp.int32)
    return seg.astype(f32)


def has_boundary(ends, first):
    found = jnp.int32(0)
    for end in ends:
        found = found + ((end > first - 3) & (end <= first + BLOCK + 2)).astype(jnp.int32)
    return found > 0


def split2(rows):
    high = rows.astype(bf16)
    return jnp.concatenate([high, (rows - high.astype(f32)).astype(bf16)], axis=0)


def rows_to_cols(rows, spread):
    return lax.dot_general(
        split2(rows), spread, (((0,), (0,)), ((), ())), preferred_element_type=f32
    )


def load_block(hs, lo, hi, g, n_blocks):
    base = pl.multiple_of(g * BLOCK, BLOCK)
    before_at = pl.multiple_of(jnp.maximum(base - EDGE, 0), EDGE)
    after_at = pl.multiple_of(jnp.minimum(base + BLOCK, n_blocks * BLOCK - EDGE), EDGE)
    block = jnp.concatenate([h[pl.ds(base, BLOCK), :] for h in hs], axis=1)
    before = jnp.concatenate([h[pl.ds(before_at, EDGE), :] for h in hs], axis=1)
    after = jnp.concatenate([h[pl.ds(after_at, EDGE), :] for h in hs], axis=1)
    before = jnp.where(g == 0, lo, before)
    after = jnp.where(g == n_blocks - 1, hi, after)
    return block, before, after


def silu(v):
    return v * (1.0 / (1.0 + jnp.exp(-v)))


def conv_rows(scratch, taps, width, reverse, masked, masks):
    total = None
    for back in range(4):
        first = back if reverse else EDGE - back
        term = scratch[pl.ds(first, BLOCK), pl.ds(0, width)] * taps[3 - back][None, :]
        if masked and back:
            row = 3 + back if reverse else 3 - back
            term = term * masks[:, row : row + 1]
        total = term if total is None else total + term
    return silu(total).astype(bf16)


def k1_body(
    n_blocks, pieces, origin, h0, h1, h2, h3, edges, w_f, w_r, wdt, taps, dt_bias, rate, spread,
    xb_f, xb_r, cum_o, dt_o, fs_o, start_o, decay_o, pay_o,
    sf, sr, added, blockdec,
):
    g = pl.program_id(0)
    ends = bounds_of(pieces)
    first = origin[0] + g * BLOCK
    lo = jnp.concatenate([edges[s, 0:EDGE, :] for s in range(4)], axis=1)
    hi = jnp.concatenate([edges[s, EDGE : 2 * EDGE, :] for s in range(4)], axis=1)
    block, before, after = load_block((h0, h1, h2, h3), lo, hi, g, n_blocks)
    proj_f = jnp.dot(jnp.concatenate([before, block], axis=0), w_f[...], preferred_element_type=f32)
    proj_r = jnp.dot(jnp.concatenate([block, after], axis=0), w_r[...], preferred_element_type=f32)
    sf[...] = proj_f.astype(bf16).astype(f32)
    sr[...] = proj_r.astype(bf16).astype(f32)
    seg = seg_rows(ends, first)
    same = (seg == seg[3:4, :]).astype(f32)
    crosses = has_boundary(ends, first)

    @pl.when(crosses)
    def _():
        masks = same.T
        xb_f[...] = conv_rows(sf, taps, MIX, False, True, masks)
        xb_r[...] = conv_rows(sr, taps, MIX, True, True, masks)

    @pl.when(jnp.logical_not(crosses))
    def _():
        xb_f[...] = conv_rows(sf, taps, MIX, False, False, None)
        xb_r[...] = conv_rows(sr, taps, MIX, True, False, None)

    raw = lax.dot_general(
        wdt[...], block, (((1,), (1,)), ((), ())), preferred_element_type=f32
    ).astype(bf16).astype(f32)
    v = raw + dt_bias[...]
    dt = jnp.maximum(v, 0.0) + jnp.log1p(jnp.exp(-jnp.abs(v)))
    logd = -dt * rate[...]
    row_at = lax.broadcasted_iota(jnp.int32, (BLOCK, BLOCK), 0)
    col_at = lax.broadcasted_iota(jnp.int32, (BLOCK, BLOCK), 1)
    upper = (row_at <= col_at).astype(f32)
    lower = (row_at >= col_at).astype(f32)
    forward = lax.broadcasted_iota(jnp.int32, (8, BLOCK), 0) < HEADS_HERE
    cum = jnp.where(
        forward,
        jnp.dot(logd, upper, precision=lax.Precision.HIGHEST, preferred_element_type=f32),
        jnp.dot(logd, lower, precision=lax.Precision.HIGHEST, preferred_element_type=f32),
    )
    own = jnp.broadcast_to(seg[3:4, :], (8, BLOCK))
    seg_first, seg_last = seg[3:4, 0:1], seg[3:4, BLOCK - 1 : BLOCK]
    seg_pre, seg_post = seg[2:3, 0:1], seg[4:5, BLOCK - 1 : BLOCK]
    seg_end = jnp.where(forward, seg_last, seg_first)
    seg_in = jnp.where(forward, seg_pre, seg_post)
    total = jnp.where(forward, cum[:, BLOCK - 1 : BLOCK], cum[:, 0:1])
    to_end = jnp.exp(total - cum) * (own == seg_end).astype(f32) * dt
    from_start = jnp.exp(cum) * (own == seg_in).astype(f32)
    block_decay = jnp.exp(total) * (seg_end == seg_in).astype(f32)
    cum_o[...] = cum
    dt_o[...] = dt
    fs_o[...] = from_start
    wide = rows_to_cols(to_end, spread[...])
    decay_row = jnp.sum(
        jnp.concatenate([block_decay, block_decay], axis=1) * spread[0:8, :].astype(f32),
        axis=0, keepdims=True,
    )
    blockdec[g] = jnp.broadcast_to(decay_row, (8, 2 * INNER))
    for stream, ref in ((0, xb_f), (1, xb_r)):
        x = ref[:, 0:INNER].astype(f32) * wide[:, stream * INNER : (stream + 1) * INNER]
        added[stream, g] = lax.dot_general(
            ref[:, INNER:MIX], x.astype(bf16), (((0,), (0,)), ((), ())), preferred_element_type=f32
        )

    @pl.when(g == n_blocks - 1)
    def _():
        for stream in range(2):
            state = jnp.zeros((NSTATE, INNER), f32)
            decay = jnp.ones((1, INNER), f32)
            for step in range(n_blocks):
                b = step if stream == 0 else n_blocks - 1 - step
                start_o[stream, b] = state
                decay_o[stream, b] = jnp.broadcast_to(decay, (8, INNER))
                d = blockdec[b, 0:1, stream * INNER : (stream + 1) * INNER]
                state = d * state + added[stream, b]
                decay = decay * d
            pay_o[stream, 0:NSTATE, :] = state.astype(bf16)
            high = decay.astype(bf16)
            low = (decay - high.astype(f32)).astype(bf16)
            at = lax.broadcasted_iota(jnp.int32, (16, INNER), 0)
            pay_o[stream, NSTATE:PAY, :] = jnp.where(
                at == 0, high.astype(f32), jnp.where(at == 1, low.astype(f32), 0.0)
            ).astype(bf16)


def local_states(pieces, origin, hs, edges, w_f, w_r, wdt, taps, dt_bias, rate, spread):
    rows = hs[0].shape[0]
    n = rows // BLOCK
    col = pl.BlockSpec((8, BLOCK), lambda g: (0, g))
    row = pl.BlockSpec((BLOCK, MIX), lambda g: (g, 0))
    return pl.pallas_call(
        functools.partial(k1_body, n),
        grid=(n,),
        in_specs=[SMEM, SMEM] + [whole(h.shape) for h in hs]
        + [whole(a.shape) for a in (edges, w_f, w_r, wdt, taps, dt_bias, rate, spread)],
        out_specs=[row, row, col, col, col]
        + [whole((2, n, NSTATE, INNER)), whole((2, n, 8, INNER)), whole((2, PAY, INNER))],
        out_shape=[
            jax.ShapeDtypeStruct((rows, MIX), bf16),
            jax.ShapeDtypeStruct((rows, MIX), bf16),
            jax.ShapeDtypeStruct((8, rows), f32),
            jax.ShapeDtypeStruct((8, rows), f32),
            jax.ShapeDtypeStruct((8, rows), f32),
            jax.ShapeDtypeStruct((2, n, NSTATE, INNER), f32),
            jax.ShapeDtypeStruct((2, n, 8, INNER), f32),
            jax.ShapeDtypeStruct((2, PAY, INNER), bf16),
        ],
        scratch_shapes=[
            pltpu.VMEM((EDGE + BLOCK, MIX), f32),
            pltpu.VMEM((EDGE + BLOCK, MIX), f32),
            pltpu.VMEM((2, n, NSTATE, INNER), f32),
            pltpu.VMEM((n, 8, 2 * INNER), f32),
        ],
        compiler_params=params(),
        cost_estimate=cost(rows * 6e6, rows * 4000),
        name="local_states",
    )(pieces, origin, *hs, edges, w_f, w_r, wdt, taps, dt_bias, rate, spread)


def k2_body(
    n_blocks, base, pieces, origin, h0, h1, h2, h3, edges, w_f, w_r, taps, skip, xb_f, xb_r, cum_i, dt_i,
    c_f, c_r, y_f, y_r, z_f, z_r,
    sf, sr, open_mask,
):
    step = pl.program_id(0)
    g = step + base
    ends = bounds_of(pieces)
    first = origin[0] + g * BLOCK
    row_at = lax.broadcasted_iota(jnp.int32, (BLOCK, BLOCK), 0)
    col_at = lax.broadcasted_iota(jnp.int32, (BLOCK, BLOCK), 1)

    @pl.when(step == 0)
    def _():
        open_mask[0] = jnp.where(row_at >= col_at, 0.0, FAR)
        open_mask[1] = jnp.where(row_at <= col_at, 0.0, FAR)

    lo = jnp.concatenate([edges[s, 0:EDGE, :] for s in range(4)], axis=1)
    hi = jnp.concatenate([edges[s, EDGE : 2 * EDGE, :] for s in range(4)], axis=1)
    block, before, after = load_block((h0, h1, h2, h3), lo, hi, g, n_blocks)
    proj_f = jnp.dot(jnp.concatenate([before, block], axis=0), w_f[...], preferred_element_type=f32)
    proj_r = jnp.dot(jnp.concatenate([block, after], axis=0), w_r[...], preferred_element_type=f32)
    sf[...] = proj_f[:, 0:NSTATE].astype(bf16).astype(f32)
    sr[...] = proj_r[:, 0:NSTATE].astype(bf16).astype(f32)
    z_f[...] = silu(proj_f[EDGE:, NSTATE:].astype(bf16).astype(f32))
    z_r[...] = silu(proj_r[0:BLOCK, NSTATE:].astype(bf16).astype(f32))
    seg = seg_rows(ends, first)
    crosses = has_boundary(ends, first)
    cum = cum_i[...]
    cum_t = cum.T

    @pl.when(crosses)
    def _():
        masks = (seg == seg[3:4, :]).astype(f32).T
        c_f[...] = conv_rows(sf, taps, NSTATE, False, True, masks)
        c_r[...] = conv_rows(sr, taps, NSTATE, True, True, masks)
        together = seg.T[:, 3:4] == seg[3:4, :]
        open_mask[2] = jnp.where(together & (row_at >= col_at), 0.0, FAR)
        open_mask[3] = jnp.where(together & (row_at <= col_at), 0.0, FAR)

    @pl.when(jnp.logical_not(crosses))
    def _():
        c_f[...] = conv_rows(sf, taps, NSTATE, False, False, None)
        c_r[...] = conv_rows(sr, taps, NSTATE, True, False, None)

    which = jnp.where(crosses, 2, 0)
    log_dt = jnp.log(dt_i[...]) - cum
    lane_head = lax.broadcasted_iota(jnp.int32, (BLOCK, INNER), 1) // HEAD_DIM
    half = BLOCK // 2
    for stream, xb, c_ref, y_ref in ((0, xb_f, c_f, y_f), (1, xb_r, c_r, y_r)):
        x = xb[:, 0:INNER]
        b = xb[:, INNER:MIX]
        heads = [jnp.where(lane_head == h, x, jnp.zeros_like(x)) for h in range(HEADS_HERE)]
        for part in range(2):
            rows = slice(part * half, (part + 1) * half)
            if stream == 0:
                cols = slice(0, half) if part == 0 else slice(0, BLOCK)
            else:
                cols = slice(0, BLOCK) if part == 0 else slice(half, BLOCK)
            scores = lax.dot_general(
                c_ref[rows, :], b[cols, :], (((1,), (1,)), ((), ())), preferred_element_type=f32
            )
            mask = open_mask[which + stream, rows, cols]
            total = x[rows, :].astype(f32) * skip[...]
            for h in range(HEADS_HERE):
                at = stream * HEADS_HERE + h
                gap = (cum_t[rows, at : at + 1] + log_dt[at : at + 1, cols]) + mask
                weight = (jnp.exp(gap) * scores).astype(bf16)
                total = total + jnp.dot(weight, heads[h][cols, :], preferred_element_type=f32)
            y_ref[rows, :] = total


def intra(part, n_parts, pieces, origin, hs, edges, w_f, w_r, taps, skip, xb_f, xb_r, cum, dt):
    rows = hs[0].shape[0]
    n = rows // BLOCK
    here = n // n_parts
    base = part * here
    col = pl.BlockSpec((8, BLOCK), lambda g: (0, g + base))
    mixed = pl.BlockSpec((BLOCK, MIX), lambda g: (g + base, 0))
    c_out = pl.BlockSpec((BLOCK, NSTATE), lambda g: (g, 0))
    y_out = pl.BlockSpec((BLOCK, INNER), lambda g: (g, 0))
    m = here * BLOCK
    return pl.pallas_call(
        functools.partial(k2_body, n, base),
        grid=(here,),
        in_specs=[SMEM, SMEM] + [whole(h.shape) for h in hs]
        + [whole(a.shape) for a in (edges, w_f, w_r, taps, skip)] + [mixed, mixed, col, col],
        out_specs=[c_out, c_out, y_out, y_out, y_out, y_out],
        out_shape=[
            jax.ShapeDtypeStruct((m, NSTATE), bf16),
            jax.ShapeDtypeStruct((m, NSTATE), bf16),
            jax.ShapeDtypeStruct((m, INNER), f32),
            jax.ShapeDtypeStruct((m, INNER), f32),
            jax.ShapeDtypeStruct((m, INNER), f32),
            jax.ShapeDtypeStruct((m, INNER), f32),
        ],
        scratch_shapes=[
            pltpu.VMEM((EDGE + BLOCK, NSTATE), f32),
            pltpu.VMEM((EDGE + BLOCK, NSTATE), f32),
            pltpu.VMEM((4, BLOCK, BLOCK), f32),
        ],
        compiler_params=params(),
        cost_estimate=cost(m * 5e6, m * 5000),
        name="intra",
    )(pieces, origin, *hs, edges, w_f, w_r, taps, skip, xb_f, xb_r, cum, dt)


def combine_body(last, digit_ref, own, r1, r2, r3, s_in, a_in, *outs):
    digit = digit_ref[0]
    for stream in range(2):
        def part(ref):
            rows = ref[stream, NSTATE:PAY, :].astype(f32)
            return ref[stream, 0:NSTATE, :].astype(f32), rows[0:1, :] + rows[1:2, :]

        got = [None] + [part(r) for r in (r1, r2, r3)]
        place = digit if stream == 0 else 3 - digit
        pick = (lambda s: got[s]) if stream == 0 else (lambda s: got[4 - s])
        low_s, low_a = jnp.zeros((NSTATE, INNER), f32), jnp.ones((1, INNER), f32)
        for s in (1, 2, 3):
            there = (s <= place).astype(f32)
            state, decay = pick(s)
            low_s = low_s + (low_a * there) * state
            low_a = low_a * (decay * there + (1.0 - there))
        old_s, old_a = s_in[stream], a_in[stream, 0:1, :]
        outs[0][stream] = old_a * low_s + old_s
        if last:
            continue
        outs[1][stream] = jnp.broadcast_to(old_a * low_a, (8, INNER))
        own_s, own_a = part(own)
        total_s, total_a = own_a * low_s + own_s, own_a * low_a
        for s in (3, 2, 1):
            there = (s > place).astype(f32)
            state, decay = pick(s)
            keep = decay * there + (1.0 - there)
            total_s = keep * total_s + there * state
            total_a = keep * total_a
        outs[2][stream, 0:NSTATE, :] = total_s.astype(bf16)
        high = total_a.astype(bf16)
        low = (total_a - high.astype(f32)).astype(bf16)
        at = lax.broadcasted_iota(jnp.int32, (16, INNER), 0)
        outs[2][stream, NSTATE:PAY, :] = jnp.where(
            at == 0, high.astype(f32), jnp.where(at == 1, low.astype(f32), 0.0)
        ).astype(bf16)


def combine(last, digit, own, received, s_in, a_in):
    shapes = [jax.ShapeDtypeStruct((2, NSTATE, INNER), f32)]
    if not last:
        shapes += [
            jax.ShapeDtypeStruct((2, 8, INNER), f32),
            jax.ShapeDtypeStruct((2, PAY, INNER), bf16),
        ]
    return pl.pallas_call(
        functools.partial(combine_body, last),
        grid=(1,),
        in_specs=[SMEM] + [whole(own.shape)] * 4 + [whole(s_in.shape), whole(a_in.shape)],
        out_specs=[whole(s.shape) for s in shapes],
        out_shape=shapes,
        compiler_params=params(),
        cost_estimate=cost(2e6, 1.5e6),
        name="combine",
    )(digit, own, *received, s_in, a_in)


def k3_body(c_f, c_r, y_f, y_r, z_f, z_r, fs, starts, decays, s_in, gain, spread, g_f, g_r, sums):
    wide = rows_to_cols(fs[...], spread[...])
    out = []
    for stream, c_ref, y_ref, z_ref, g_ref in ((0, c_f, y_f, z_f, g_f), (1, c_r, y_r, z_r, g_r)):
        state = starts[stream, 0] + decays[stream, 0, 0:1, :] * s_in[stream]
        carried = jnp.dot(c_ref[...], state.astype(bf16), preferred_element_type=f32)
        mixed = y_ref[...] + carried * wide[:, stream * INNER : (stream + 1) * INNER]
        gated = mixed * z_ref[...]
        square = gated * gated
        out.append(jnp.sum((square[:, 0:128] + square[:, 128:256]).T, axis=0, keepdims=True))
        g_ref[...] = (gated * gain[...]).astype(bf16)
    sums[...] = jnp.concatenate(out, axis=0)


def gate(part, n_parts, locals_, fs, starts, decays, s_in, gain, spread):
    c_f, c_r, y_f, y_r, z_f, z_r = locals_
    n = starts.shape[1]
    here = n // n_parts
    base = part * here
    m = here * BLOCK
    c_in = pl.BlockSpec((BLOCK, NSTATE), lambda g: (g, 0))
    y_in = pl.BlockSpec((BLOCK, INNER), lambda g: (g, 0))
    return pl.pallas_call(
        k3_body,
        grid=(here,),
        in_specs=[c_in, c_in, y_in, y_in, y_in, y_in,
                  pl.BlockSpec((8, BLOCK), lambda g: (0, g + base)),
                  pl.BlockSpec((2, 1, NSTATE, INNER), lambda g: (0, g + base, 0, 0)),
                  pl.BlockSpec((2, 1, 8, INNER), lambda g: (0, g + base, 0, 0)),
                  whole(s_in.shape), whole(gain.shape), whole(spread.shape)],
        out_specs=[y_in, y_in, pl.BlockSpec((2, BLOCK), lambda g: (0, g))],
        out_shape=[
            jax.ShapeDtypeStruct((m, INNER), bf16),
            jax.ShapeDtypeStruct((m, INNER), bf16),
            jax.ShapeDtypeStruct((2, m), f32),
        ],
        compiler_params=params(),
        cost_estimate=cost(m * 5e5, m * 6000),
        name="gate",
    )(c_f, c_r, y_f, y_r, z_f, z_r, fs, starts, decays, s_in, gain, spread)


def k4_body(g_f, g_r, s0, s1, s2, s3, w_f, w_r, spread, o0, o1, o2, o3):
    total = (s0[...] + s1[...]) + (s2[...] + s3[...])
    scale = lax.rsqrt(total / E + EPSILON)
    scale = jnp.concatenate([scale, jnp.zeros((6, BLOCK), f32)], axis=0)
    wide = rows_to_cols(scale, spread[...])
    out_f = jnp.dot(g_f[...], w_f[...], preferred_element_type=f32)
    out_r = jnp.dot(g_r[...], w_r[...], preferred_element_type=f32)
    for s, ref in enumerate((o0, o1, o2, o3)):
        cols = slice(s * 128, (s + 1) * 128)
        part = out_f[:, cols] * wide[:, 0:128] + out_r[:, cols] * wide[:, 128:256]
        ref[...] = part.astype(ref.dtype)


def project_out(g_f, g_r, sums, w_f, w_r, spread):
    m = g_f.shape[0]
    n = m // BLOCK
    g_in = pl.BlockSpec((BLOCK, INNER), lambda g: (g, 0))
    s_in = pl.BlockSpec((2, BLOCK), lambda g: (0, g))
    o = pl.BlockSpec((BLOCK, 128), lambda g: (g, 0))
    return pl.pallas_call(
        k4_body,
        grid=(n,),
        in_specs=[g_in, g_in] + [s_in] * 4 + [whole(w_f.shape), whole(w_r.shape), whole(spread.shape)],
        out_specs=[o] * 4,
        out_shape=[jax.ShapeDtypeStruct((m, 128), f32)] + [jax.ShapeDtypeStruct((m, 128), bf16)] * 3,
        compiler_params=params(),
        cost_estimate=cost(m * 1e6, m * 3000),
        name="project_out",
    )(g_f, g_r, *sums, w_f, w_r, spread)


def row_spread():
    out = np.zeros((16, 256), np.float32)
    for part in range(2):
        out[part * 8, 0:128] = 1.0
        out[part * 8 + 1, 128:256] = 1.0
    return out


def around(array, axis, count, shift):
    return lax.ppermute(array, axis, [(i, (i + shift) % count) for i in range(count)])


def digit_perm(count, stride, shift):
    pairs = []
    for i in range(count):
        d = (i // stride) % 4
        pairs.append((i, i + (((d + shift) % 4) - d) * stride))
    return pairs


N_PARTS = 2


def shards(
    hidden, w_x, w_z, w_bc, w_dt, conv_x, conv_bc, dt_bias, decay_rate, skip_gain, norm_gain, w_out,
    piece_lengths,
):
    rows = hidden.shape[0]
    ctx, mp = lax.axis_index("ctx"), lax.axis_index("mp")
    n_ctx, n_mp = lax.axis_size("ctx"), lax.axis_size("mp")

    hs = [hidden] + [around(hidden, "mp", n_mp, s) for s in range(1, n_mp)]
    low = lax.ppermute(hidden[rows - EDGE :], "ctx", [(i, i + 1) for i in range(n_ctx - 1)])
    high = lax.ppermute(hidden[:EDGE], "ctx", [(i + 1, i) for i in range(n_ctx - 1)])
    edge = jnp.concatenate([low, high], axis=0)
    edges = jnp.stack([edge] + [around(edge, "mp", n_mp, s) for s in range(1, n_mp)])

    width = w_x.shape[0]
    here = width // n_mp
    at = jnp.arange(width, dtype=jnp.int32)
    place = ((mp - at // here) % n_mp) * here + at % here
    pick_f = (place[:, None] == at[None, :]).astype(bf16)
    pick_r = (width - 1 - place[:, None] == at[None, :]).astype(bf16)
    w_1 = jnp.concatenate([w_x, w_bc[:, :NSTATE]], axis=1)
    w_2 = jnp.concatenate([w_bc[:, NSTATE:], w_z], axis=1)
    w_1f, w_1r, w_2f, w_2r = (
        jnp.dot(pick, w, preferred_element_type=f32).astype(bf16)
        for w in (w_1, w_2) for pick in (pick_f, pick_r)
    )
    wdt = jnp.concatenate(
        [jnp.dot(pick, w_dt, preferred_element_type=f32).astype(bf16).T for pick in (pick_f, pick_r)], axis=0
    )
    goal = ((mp + at // here) % n_mp) * here + at % here
    out_pick_f = (goal[None, :] == at[:, None]).astype(bf16)
    out_pick_r = (width - 1 - goal[None, :] == at[:, None]).astype(bf16)
    w_of = jnp.dot(w_out, out_pick_f, preferred_element_type=f32).astype(bf16)
    w_or = jnp.dot(w_out, out_pick_r, preferred_element_type=f32).astype(bf16)

    taps_1 = jnp.concatenate([conv_x, conv_bc[:, :NSTATE]], axis=1)
    taps_2 = conv_bc[:, NSTATE:]
    bias = jnp.broadcast_to(jnp.concatenate([dt_bias, dt_bias])[:, None], (8, BLOCK))
    rate = jnp.broadcast_to(jnp.concatenate([decay_rate, decay_rate])[:, None], (8, BLOCK))
    skip = jnp.repeat(skip_gain, HEAD_DIM)[None, :]
    gain = norm_gain[None, :]
    spread = jnp.asarray(head_spread(), bf16)
    spread_rows = jnp.asarray(row_spread(), bf16)
    origin = (ctx * rows)[None].astype(jnp.int32)

    xb_f, xb_r, cum, dt, fs, starts, decays, pay = local_states(
        piece_lengths, origin, hs, edges, w_1f, w_1r, wdt, taps_1, bias, rate, spread
    )

    s_in = jnp.zeros((2, NSTATE, INNER), f32)
    a_in = jnp.ones((2, 8, INNER), f32)
    for level, stride in enumerate((1, 4, 16)):
        received = [lax.ppermute(pay, "ctx", digit_perm(n_ctx, stride, s)) for s in (1, 2, 3)]
        digit = ((ctx // stride) % 4)[None].astype(jnp.int32)
        last = level == 2
        outs = combine(last, digit, pay, received, s_in, a_in)
        if last:
            s_in = outs[0]
        else:
            s_in, a_in, pay = outs

    locals_ = [
        intra(p, N_PARTS, piece_lengths, origin, hs, edges, w_2f, w_2r, taps_2, skip, xb_f, xb_r, cum, dt)
        for p in range(N_PARTS)
    ]
    out = []
    for p in range(N_PARTS):
        g_f, g_r, sums = gate(p, N_PARTS, locals_[p], fs, starts, decays, s_in, gain, spread)
        all_sums = [sums] + [around(sums, "mp", n_mp, s) for s in range(1, n_mp)]
        own, *sent = project_out(g_f, g_r, all_sums, w_of, w_or, spread_rows)
        got = [around(piece, "mp", n_mp, s + 1) for s, piece in enumerate(sent)]
        total = own
        for piece in got:
            total = total + piece.astype(f32)
        out.append(total.astype(bf16))
    return jnp.concatenate(out, axis=0)


def solution(mesh):
    return jax.shard_map(
        shards,
        mesh=mesh,
        in_specs=(
            P("ctx", "mp"),
            P(None, "mp"),
            P(None, "mp"),
            P(),
            P(None, "mp"),
            P(None, "mp"),
            P(),
            P("mp"),
            P("mp"),
            P("mp"),
            P("mp"),
            P("mp", None),
            P(),
        ),
        out_specs=P("ctx", "mp"),
        check_vma=False,
    )
```

```python
import functools

import jax
import jax.numpy as jnp
import numpy as np
from jax import lax
from jax.experimental import pallas as pl
from jax.experimental.pallas import tpu as pltpu
from jax.sharding import PartitionSpec as P

E = 1024
HEAD_DIM = 64
NSTATE = 128
BLOCK = 256
HEADS_HERE = 4
INNER = HEADS_HERE * HEAD_DIM
PIECES = 16
EPSILON = 1e-05
FAR = -1e30
EDGE = 16
MIX = INNER + NSTATE
QUARTER = NSTATE // 4
PAY = 2 * QUARTER + 16

bf16 = jnp.bfloat16
f32 = jnp.float32


def head_spread():
    out = np.zeros((16, 2 * INNER), np.float32)
    for part in range(2):
        for stream in range(2):
            for h in range(HEADS_HERE):
                first = stream * INNER + h * HEAD_DIM
                out[part * 8 + stream * 4 + h, first : first + HEAD_DIM] = 1.0
    return out


def whole(shape):
    return pl.BlockSpec(shape, lambda *_: (0,) * len(shape))


SMEM = pl.BlockSpec(memory_space=pltpu.SMEM)


def params(mib):
    return pltpu.CompilerParams(
        dimension_semantics=("arbitrary",), vmem_limit_bytes=mib * 1024 * 1024
    )


def cost(flops, nbytes):
    return pl.CostEstimate(flops=int(flops), bytes_accessed=int(nbytes), transcendentals=0)


def bounds_of(pieces_ref):
    total = pieces_ref[0]
    ends = [total]
    for k in range(1, PIECES):
        total = total + pieces_ref[k]
        ends.append(total)
    return ends


def seg_rows(ends, first):
    shape = (8, BLOCK)
    pos = (
        first - 3 + lax.broadcasted_iota(jnp.int32, shape, 0)
        + lax.broadcasted_iota(jnp.int32, shape, 1)
    )
    seg = jnp.zeros(shape, jnp.int32)
    for end in ends:
        seg = seg + (pos >= end).astype(jnp.int32)
    return seg.astype(f32)


def has_boundary(ends, first):
    found = jnp.int32(0)
    for end in ends:
        found = found + ((end > first - 3) & (end <= first + BLOCK + 2)).astype(jnp.int32)
    return found > 0


def split2(rows):
    high = rows.astype(bf16)
    return jnp.concatenate([high, (rows - high.astype(f32)).astype(bf16)], axis=0)


def rows_to_cols(rows, spread):
    return lax.dot_general(
        split2(rows), spread, (((0,), (0,)), ((), ())), preferred_element_type=f32
    )


def load_block(hs, lo, hi, g, n_blocks):
    base = pl.multiple_of(g * BLOCK, BLOCK)
    before_at = pl.multiple_of(jnp.maximum(base - EDGE, 0), EDGE)
    after_at = pl.multiple_of(jnp.minimum(base + BLOCK, n_blocks * BLOCK - EDGE), EDGE)
    block = jnp.concatenate([h[pl.ds(base, BLOCK), :] for h in hs], axis=1)
    before = jnp.concatenate([h[pl.ds(before_at, EDGE), :] for h in hs], axis=1)
    after = jnp.concatenate([h[pl.ds(after_at, EDGE), :] for h in hs], axis=1)
    before = jnp.where(g == 0, lo, before)
    after = jnp.where(g == n_blocks - 1, hi, after)
    return block, before, after


def silu(v):
    half = 0.5 * v
    return half + half * jnp.tanh(half)


def tap_rows(conv_x, conv_bc):
    return [conv_x[:, 0:128], conv_x[:, 128:256], conv_bc[:, 0:128], conv_bc[:, 128:256]]


def conv_tile(scratch, tile, taps, reverse, masks):
    total = None
    for back in range(4):
        first = back if reverse else EDGE - back
        term = scratch[tile, pl.ds(first, BLOCK), :] * taps[3 - back : 4 - back, :]
        if masks is not None and back:
            row = 3 + back if reverse else 3 - back
            term = term * masks[:, row : row + 1]
        total = term if total is None else total + term
    return silu(total).astype(bf16)


def keep_rounded(scratch, proj):
    for tile in range(scratch.shape[0]):
        scratch[tile] = proj[:, tile * 128 : (tile + 1) * 128].astype(bf16).astype(f32)


def per_head(scalars, shape, axis, width):
    head = lax.broadcasted_iota(jnp.int32, shape, axis) // width % HEADS_HERE
    out = jnp.full(shape, scalars[0], f32)
    for h in range(1, HEADS_HERE):
        out = jnp.where(head == h, scalars[h], out)
    return out


def split_rows(decays):
    at = lax.broadcasted_iota(jnp.int32, (16, INNER), 0)
    out = jnp.zeros((16, INNER), f32)
    for k, decay in enumerate(decays):
        high = decay.astype(bf16).astype(f32)
        out = jnp.where(at == 2 * k, high, jnp.where(at == 2 * k + 1, decay - high, out))
    return out.astype(bf16)


def decays_of(rows):
    wide = rows.astype(f32)
    return [wide[2 * k : 2 * k + 1, :] + wide[2 * k + 1 : 2 * k + 2, :] for k in range(2)]


def row_quantities(
    n_blocks, ends, origin, hs, wdt, dt_bias, rate, spread, cum_o, dt_o, fs_o, same_s, te_s, blockdec
):
    raw = []
    for b in range(n_blocks):
        block = jnp.concatenate([h[b * BLOCK : (b + 1) * BLOCK, :] for h in hs], axis=1)
        raw.append(
            lax.dot_general(wdt[...], block, (((1,), (1,)), ((), ())), preferred_element_type=f32)
        )
    shape = (8 * n_blocks, BLOCK)
    v = jnp.concatenate(raw, axis=0).astype(bf16).astype(f32) + per_head(dt_bias, shape, 0, 1)
    dt = jnp.maximum(v, 0.0) + jnp.log1p(jnp.exp(-jnp.abs(v)))
    logd = -dt * per_head(rate, shape, 0, 1)
    high = logd.astype(bf16)
    rest = logd - high.astype(f32)
    middle = rest.astype(bf16)
    low = (rest - middle.astype(f32)).astype(bf16)
    row_at = lax.broadcasted_iota(jnp.int32, (BLOCK, BLOCK), 0)
    col_at = lax.broadcasted_iota(jnp.int32, (BLOCK, BLOCK), 1)
    summed = []
    for keep in (row_at <= col_at, row_at >= col_at):
        ones = keep.astype(f32).astype(bf16)
        summed.append(sum(jnp.dot(p, ones, preferred_element_type=f32) for p in (low, middle, high)))
    forward = lax.broadcasted_iota(jnp.int32, (8, BLOCK), 0) < HEADS_HERE
    spread_f = spread[0:8, :].astype(f32)
    for b in range(n_blocks):
        rows = slice(b * 8, (b + 1) * 8)
        cols = slice(b * BLOCK, (b + 1) * BLOCK)
        cum = jnp.where(forward, summed[0][rows], summed[1][rows])
        dt_b = dt[rows]
        seg = seg_rows(ends, origin + b * BLOCK)
        same_s[b] = (seg == seg[3:4, :]).astype(f32)
        own = jnp.broadcast_to(seg[3:4, :], (8, BLOCK))
        seg_end = jnp.where(forward, seg[3:4, BLOCK - 1 : BLOCK], seg[3:4, 0:1])
        seg_in = jnp.where(forward, seg[2:3, 0:1], seg[4:5, BLOCK - 1 : BLOCK])
        total = jnp.where(forward, cum[:, BLOCK - 1 : BLOCK], cum[:, 0:1])
        to_end = jnp.exp(total - cum) * (own == seg_end).astype(f32) * dt_b
        block_decay = jnp.exp(total) * (seg_end == seg_in).astype(f32)
        cum_o[:, cols] = cum
        dt_o[:, cols] = dt_b
        fs_o[:, cols] = jnp.exp(cum) * (own == seg_in).astype(f32)
        te_s[b] = split2(to_end)
        decay_row = jnp.sum(
            jnp.concatenate([block_decay, block_decay], axis=1) * spread_f, axis=0, keepdims=True
        )
        blockdec[b] = jnp.broadcast_to(decay_row, (8, 2 * INNER))


def k1_body(
    n_blocks, pieces, meta, dt_bias, rate, h0, h1, h2, h3, e0, e1, e2, e3, w_f, w_r, wdt, conv_x, conv_bc,
    spread,
    xb_f, xb_r, cum_o, dt_o, fs_o, start_o, decay_o, p0, p1, p2, p3,
    sf, sr, added, blockdec, same_s, te_s, total_s,
):
    g = pl.program_id(0)
    ends = bounds_of(pieces)
    first = meta[0] + g * BLOCK
    hs, edges = (h0, h1, h2, h3), (e0, e1, e2, e3)

    @pl.when(g == 0)
    def _():
        row_quantities(
            n_blocks, ends, meta[0], hs, wdt, dt_bias, rate, spread, cum_o, dt_o, fs_o, same_s, te_s, blockdec
        )

    crosses = has_boundary(ends, first)

    def states(masked):
        lo = jnp.concatenate([e[0:EDGE, :] for e in edges], axis=1)
        hi = jnp.concatenate([e[EDGE : 2 * EDGE, :] for e in edges], axis=1)
        block, before, after = load_block(hs, lo, hi, g, n_blocks)
        masks = same_s[g].T if masked else None
        taps = tap_rows(conv_x, conv_bc)
        wide = lax.dot_general(
            te_s[g], spread[...], (((0,), (0,)), ((), ())), preferred_element_type=f32
        )
        keep_rounded(
            sf, jnp.dot(jnp.concatenate([before, block], axis=0), w_f[...], preferred_element_type=f32)
        )
        keep_rounded(
            sr, jnp.dot(jnp.concatenate([block, after], axis=0), w_r[...], preferred_element_type=f32)
        )
        for stream, scratch, ref in ((0, sf, xb_f), (1, sr, xb_r)):
            scaled = []
            for tile in (0, 1):
                x = conv_tile(scratch, tile, taps[tile], stream == 1, masks)
                ref[:, tile * 128 : (tile + 1) * 128] = x
                at = stream * INNER + tile * 128
                scaled.append((x.astype(f32) * wide[:, at : at + 128]).astype(bf16))
            b = conv_tile(scratch, 2, taps[2], stream == 1, masks)
            ref[:, INNER:MIX] = b
            added[stream, g] = lax.dot_general(
                b, jnp.concatenate(scaled, axis=1), (((0,), (0,)), ((), ())), preferred_element_type=f32
            )

    pl.when(crosses)(lambda: states(True))
    pl.when(jnp.logical_not(crosses))(lambda: states(False))

    @pl.when(g == n_blocks - 1)
    def _():
        decays = []
        for stream in range(2):
            state = jnp.zeros((NSTATE, INNER), f32)
            decay = jnp.ones((1, INNER), f32)
            for step in range(n_blocks):
                b = step if stream == 0 else n_blocks - 1 - step
                start_o[stream, b] = state
                decay_o[stream, b] = jnp.broadcast_to(decay, (8, INNER))
                d = blockdec[b, 0:1, stream * INNER : (stream + 1) * INNER]
                state = d * state + added[stream, b]
                decay = decay * d
            total_s[stream] = state
            decays.append(decay)
        rows = split_rows(decays)
        for s, ref in enumerate((p0, p1, p2, p3)):
            at = pl.multiple_of(lax.rem(meta[1] + s, 4) * QUARTER, QUARTER)
            ref[0:QUARTER, :] = total_s[0, pl.ds(at, QUARTER), :].astype(bf16)
            ref[QUARTER : 2 * QUARTER, :] = total_s[1, pl.ds(at, QUARTER), :].astype(bf16)
            ref[2 * QUARTER : PAY, :] = rows


def local_states(pieces, meta, dt_bias, rate, hs, edges, w_f, w_r, wdt, conv_x, conv_bc, spread):
    rows = hs[0].shape[0]
    n = rows // BLOCK
    row = pl.BlockSpec((BLOCK, MIX), lambda g: (g, 0))
    fixed = [*hs, *edges, w_f, w_r, wdt, conv_x, conv_bc, spread]
    shapes = [
        jax.ShapeDtypeStruct((rows, MIX), bf16),
        jax.ShapeDtypeStruct((rows, MIX), bf16),
        jax.ShapeDtypeStruct((8, rows), f32),
        jax.ShapeDtypeStruct((8, rows), f32),
        jax.ShapeDtypeStruct((8, rows), f32),
        jax.ShapeDtypeStruct((2, n, NSTATE, INNER), f32),
        jax.ShapeDtypeStruct((2, n, 8, INNER), f32),
    ] + [jax.ShapeDtypeStruct((PAY, INNER), bf16)] * 4
    return pl.pallas_call(
        functools.partial(k1_body, n),
        grid=(n,),
        in_specs=[SMEM] * 4 + [whole(a.shape) for a in fixed],
        out_specs=[row, row] + [whole(s.shape) for s in shapes[2:]],
        out_shape=shapes,
        scratch_shapes=[
            pltpu.VMEM((MIX // 128, EDGE + BLOCK, 128), f32),
            pltpu.VMEM((MIX // 128, EDGE + BLOCK, 128), f32),
            pltpu.VMEM((2, n, NSTATE, INNER), f32),
            pltpu.VMEM((n, 8, 2 * INNER), f32),
            pltpu.VMEM((n, 8, BLOCK), f32),
            pltpu.VMEM((n, 16, BLOCK), bf16),
            pltpu.VMEM((2, NSTATE, INNER), f32),
        ],
        compiler_params=params(28),
        cost_estimate=cost(rows * 6e6, rows * 4000),
        name="local_states",
    )(pieces, meta, dt_bias, rate, *fixed)


def k2_body(
    n_blocks, base, n_alias, pieces, meta, skip_gain, h0, h1, h2, h3, e0, e1, e2, e3, w_f, w_r, conv_x, conv_bc,
    xb_f, xb_r, cum_i, dt_i, *rest,
):
    c_f, c_r, y_f, y_r, z_f, z_r, sf, sr, open_mask = rest[n_alias:]
    step = pl.program_id(0)
    g = step + base
    ends = bounds_of(pieces)
    first = meta[0] + g * BLOCK
    row_at = lax.broadcasted_iota(jnp.int32, (BLOCK, BLOCK), 0)
    col_at = lax.broadcasted_iota(jnp.int32, (BLOCK, BLOCK), 1)
    half = BLOCK // 2

    @pl.when(step == 0)
    def _():
        open_mask[0] = jnp.where(row_at >= col_at, 0.0, FAR)
        open_mask[1] = jnp.where(row_at <= col_at, 0.0, FAR)

    crosses = has_boundary(ends, first)

    @pl.when(crosses)
    def _():
        seg = seg_rows(ends, first)
        together = seg.T[:, 3:4] == seg[3:4, :]
        open_mask[2] = jnp.where(together & (row_at >= col_at), 0.0, FAR)
        open_mask[3] = jnp.where(together & (row_at <= col_at), 0.0, FAR)

    def mix(masked):
        lo = jnp.concatenate([e[0:EDGE, :] for e in (e0, e1, e2, e3)], axis=1)
        hi = jnp.concatenate([e[EDGE : 2 * EDGE, :] for e in (e0, e1, e2, e3)], axis=1)
        block, before, after = load_block((h0, h1, h2, h3), lo, hi, g, n_blocks)
        masks = None
        if masked:
            seg = seg_rows(ends, first)
            masks = (seg == seg[3:4, :]).astype(f32).T
        proj_f = jnp.dot(jnp.concatenate([before, block], axis=0), w_f[...], preferred_element_type=f32)
        proj_r = jnp.dot(jnp.concatenate([block, after], axis=0), w_r[...], preferred_element_type=f32)
        keep_rounded(sf, proj_f)
        keep_rounded(sr, proj_r)
        z_f[...] = silu(proj_f[EDGE:, NSTATE:].astype(bf16).astype(f32))
        z_r[...] = silu(proj_r[0:BLOCK, NSTATE:].astype(bf16).astype(f32))
        taps = tap_rows(conv_x, conv_bc)[3]
        cum = cum_i[...]
        cum_t = cum.T
        log_dt = jnp.log(dt_i[...]) - cum
        lane_head = lax.broadcasted_iota(jnp.int32, (BLOCK, INNER), 1) // HEAD_DIM
        skip = per_head(skip_gain, (1, INNER), 1, HEAD_DIM)
        for stream, xb, scratch, c_ref, y_ref in ((0, xb_f, sf, c_f, y_f), (1, xb_r, sr, c_r, y_r)):
            c_rows = conv_tile(scratch, 0, taps, stream == 1, masks)
            c_ref[...] = c_rows
            x = xb[:, 0:INNER]
            b = xb[:, INNER:MIX]
            heads = [jnp.where(lane_head == h, x, jnp.zeros_like(x)) for h in range(HEADS_HERE)]
            for part in range(2):
                rows = slice(part * half, (part + 1) * half)
                if stream == 0:
                    cols = slice(0, half) if part == 0 else slice(0, BLOCK)
                else:
                    cols = slice(0, BLOCK) if part == 0 else slice(half, BLOCK)
                scores = lax.dot_general(
                    c_rows[rows, :], b[cols, :], (((1,), (1,)), ((), ())), preferred_element_type=f32
                )
                mask = open_mask[(2 if masked else 0) + stream, rows, cols]
                total = x[rows, :].astype(f32) * skip
                for h in range(HEADS_HERE):
                    at = stream * HEADS_HERE + h
                    gap = (cum_t[rows, at : at + 1] + log_dt[at : at + 1, cols]) + mask
                    weight = (jnp.exp(gap) * scores).astype(bf16)
                    total = total + jnp.dot(weight, heads[h][cols, :], preferred_element_type=f32)
                y_ref[rows, :] = total

    pl.when(crosses)(lambda: mix(True))
    pl.when(jnp.logical_not(crosses))(lambda: mix(False))


def intra(part, n_parts, pieces, meta, skip_gain, hs, edges, w_f, w_r, conv_x, conv_bc, xb_f, xb_r, cum, dt, before):
    rows = hs[0].shape[0]
    n = rows // BLOCK
    here = n // n_parts
    base = part * here
    col = pl.BlockSpec((8, BLOCK), lambda g: (0, g + base))
    mixed = pl.BlockSpec((BLOCK, MIX), lambda g: (g + base, 0))
    c_out = pl.BlockSpec((BLOCK, NSTATE), lambda g: (g + base, 0))
    y_out = pl.BlockSpec((BLOCK, INNER), lambda g: (g + base, 0))
    fixed = [*hs, *edges, w_f, w_r, conv_x, conv_bc]
    before = list(before)
    n_in = 3 + len(fixed) + 4
    return pl.pallas_call(
        functools.partial(k2_body, n, base, len(before)),
        grid=(here,),
        in_specs=[SMEM] * 3 + [whole(a.shape) for a in fixed] + [mixed, mixed, col, col]
        + [pl.BlockSpec(memory_space=pl.ANY)] * len(before),
        out_specs=[c_out, c_out, y_out, y_out, y_out, y_out],
        out_shape=[jax.ShapeDtypeStruct((rows, NSTATE), bf16)] * 2
        + [jax.ShapeDtypeStruct((rows, INNER), f32)] * 4,
        input_output_aliases={n_in + k: k for k in range(len(before))},
        scratch_shapes=[
            pltpu.VMEM((1, EDGE + BLOCK, 128), f32),
            pltpu.VMEM((1, EDGE + BLOCK, 128), f32),
            pltpu.VMEM((4, BLOCK, BLOCK), f32),
        ],
        compiler_params=params(24),
        cost_estimate=cost(here * BLOCK * 5e6, here * BLOCK * 5000),
        name="intra",
    )(pieces, meta, skip_gain, *fixed, xb_f, xb_r, cum, dt, *before)


def state_rows(ref, stream):
    return ref[stream * QUARTER : (stream + 1) * QUARTER, :].astype(f32)


def put_payload(ref, states, decays):
    for stream in range(2):
        ref[stream * QUARTER : (stream + 1) * QUARTER, :] = states[stream].astype(bf16)
    ref[2 * QUARTER : PAY, :] = split_rows(decays)


def group_body(meta, own, r1, r2, r3, pre_s, pre_a, pay, stage):
    me = meta[1]
    for s, ref in enumerate((own, r1, r2, r3)):
        stage[lax.rem(me - s + 4, 4)] = ref[...]
    states, decays = [], []
    for stream in range(2):
        state = jnp.zeros((QUARTER, INNER), f32)
        decay = jnp.ones((1, INNER), f32)
        for step in range(4):
            k = step if stream == 0 else 3 - step
            pre_s[k, stream] = state
            pre_a[k, stream] = jnp.broadcast_to(decay, (8, INNER))
            one = stage[k]
            d = decays_of(one[2 * QUARTER :])[stream]
            state = d * state + one[stream * QUARTER : (stream + 1) * QUARTER].astype(f32)
            decay = decay * d
        states.append(state)
        decays.append(decay)
    put_payload(pay, states, decays)


def before_digit(place, stream, got):
    low_s, low_a = jnp.zeros((QUARTER, INNER), f32), jnp.ones((1, INNER), f32)
    for s in (1, 2, 3):
        there = s <= place
        state, decay = got[s if stream == 0 else 4 - s]
        low_s = jnp.where(there, low_s + low_a * state, low_s)
        low_a = jnp.where(there, low_a * decay, low_a)
    return low_s, low_a


def middle_body(meta, own, r1, r2, r3, low_o, low_ao, pay):
    digit = meta[2]
    states, decays = [], []
    rows = [decays_of(r[2 * QUARTER : PAY, :]) for r in (own, r1, r2, r3)]
    for stream in range(2):
        got = [(state_rows(r, stream), rows[s][stream]) for s, r in enumerate((own, r1, r2, r3))]
        place = digit if stream == 0 else 3 - digit
        low_s, low_a = before_digit(place, stream, got)
        low_o[stream] = low_s
        low_ao[stream] = jnp.broadcast_to(low_a, (8, INNER))
        total_s, total_a = got[0][1] * low_s + got[0][0], got[0][1] * low_a
        for s in (3, 2, 1):
            there = s > place
            state, decay = got[s if stream == 0 else 4 - s]
            total_s = jnp.where(there, decay * total_s + state, total_s)
            total_a = jnp.where(there, decay * total_a, total_a)
        states.append(total_s)
        decays.append(total_a)
    put_payload(pay, states, decays)


def top_body(meta, r1, r2, r3, low_i, low_ai, pre_s, pre_a, *outs):
    digit = meta[3]
    rows = [None] + [decays_of(r[2 * QUARTER : PAY, :]) for r in (r1, r2, r3)]
    for stream in range(2):
        got = [None] + [
            (state_rows(r, stream), rows[s + 1][stream]) for s, r in enumerate((r1, r2, r3))
        ]
        place = digit if stream == 0 else 3 - digit
        top_s, _ = before_digit(place, stream, got)
        group_s = low_ai[stream, 0:1, :] * top_s + low_i[stream]
        for s, ref in enumerate(outs):
            k = lax.rem(meta[1] + s, 4)
            member = pre_a[k, stream][0:1, :] * group_s + pre_s[k, stream]
            ref[stream * QUARTER : (stream + 1) * QUARTER, :] = member.astype(bf16)


def small_call(body, name, meta, arrays, shapes, scratch=()):
    return pl.pallas_call(
        body,
        grid=(1,),
        in_specs=[SMEM] + [whole(a.shape) for a in arrays],
        out_specs=[whole(s.shape) for s in shapes],
        out_shape=shapes,
        scratch_shapes=list(scratch),
        compiler_params=params(6),
        cost_estimate=cost(2e6, 1e6),
        name=name,
    )(meta, *arrays)


PAYLOAD = jax.ShapeDtypeStruct((PAY, INNER), bf16)


def join_group(meta, arrays):
    shapes = [
        jax.ShapeDtypeStruct((4, 2, QUARTER, INNER), f32),
        jax.ShapeDtypeStruct((4, 2, 8, INNER), f32),
        PAYLOAD,
    ]
    return small_call(group_body, "join_group", meta, arrays, shapes, [pltpu.VMEM((4, PAY, INNER), bf16)])


def join_middle(meta, arrays):
    shapes = [
        jax.ShapeDtypeStruct((2, QUARTER, INNER), f32),
        jax.ShapeDtypeStruct((2, 8, INNER), f32),
        PAYLOAD,
    ]
    return small_call(middle_body, "join_middle", meta, arrays, shapes)


def join_top(meta, arrays):
    shapes = [jax.ShapeDtypeStruct((2 * QUARTER, INNER), bf16)] * 4
    return small_call(top_body, "join_top", meta, arrays, shapes)


def k3_body(meta, c_f, c_r, y_f, y_r, z_f, z_r, fs, starts, decays, q0, q1, q2, q3, gain, spread, g_f, g_r, sums, s_in):
    @pl.when(pl.program_id(0) == 0)
    def _():
        for s, ref in enumerate((q0, q1, q2, q3)):
            at = pl.multiple_of(lax.rem(meta[1] - s + 4, 4) * QUARTER, QUARTER)
            for stream in range(2):
                s_in[stream, pl.ds(at, QUARTER), :] = state_rows(ref, stream)

    wide = rows_to_cols(fs[...], spread[...])
    out = []
    for stream, c_ref, y_ref, z_ref, g_ref in ((0, c_f, y_f, z_f, g_f), (1, c_r, y_r, z_r, g_r)):
        state = starts[stream, 0] + decays[stream, 0, 0:1, :] * s_in[stream]
        carried = jnp.dot(c_ref[...], state.astype(bf16), preferred_element_type=f32)
        mixed = y_ref[...] + carried * wide[:, stream * INNER : (stream + 1) * INNER]
        gated = mixed * z_ref[...]
        square = gated * gated
        out.append(jnp.sum((square[:, 0:128] + square[:, 128:256]).T, axis=0, keepdims=True))
        g_ref[...] = (gated * gain[...]).astype(bf16)
    sums[...] = jnp.concatenate(out, axis=0)


def gate(part, n_parts, meta, locals_, fs, starts, decays, quarters, gain, spread):
    n = starts.shape[1]
    here = n // n_parts
    base = part * here
    m = here * BLOCK
    c_in = pl.BlockSpec((BLOCK, NSTATE), lambda g: (g + base, 0))
    y_in = pl.BlockSpec((BLOCK, INNER), lambda g: (g + base, 0))
    y_out = pl.BlockSpec((BLOCK, INNER), lambda g: (g, 0))
    return pl.pallas_call(
        k3_body,
        grid=(here,),
        in_specs=[SMEM, c_in, c_in, y_in, y_in, y_in, y_in,
                  pl.BlockSpec((8, BLOCK), lambda g: (0, g + base)),
                  pl.BlockSpec((2, 1, NSTATE, INNER), lambda g: (0, g + base, 0, 0)),
                  pl.BlockSpec((2, 1, 8, INNER), lambda g: (0, g + base, 0, 0))]
        + [whole(a.shape) for a in (*quarters, gain, spread)],
        out_specs=[y_out, y_out, pl.BlockSpec((2, BLOCK), lambda g: (0, g))],
        out_shape=[
            jax.ShapeDtypeStruct((m, INNER), bf16),
            jax.ShapeDtypeStruct((m, INNER), bf16),
            jax.ShapeDtypeStruct((2, m), f32),
        ],
        scratch_shapes=[pltpu.VMEM((2, NSTATE, INNER), f32)],
        compiler_params=params(16),
        cost_estimate=cost(m * 5e5, m * 6000),
        name="gate",
    )(meta, *locals_, fs, starts, decays, *quarters, gain, spread)


def k4_body(g_f, g_r, s0, s1, s2, s3, w_f, w_r, spread, o0, o1, o2, o3):
    total = (s0[...] + s1[...]) + (s2[...] + s3[...])
    scale = lax.rsqrt(total / E + EPSILON)
    scale = jnp.concatenate([scale, jnp.zeros((6, BLOCK), f32)], axis=0)
    wide = rows_to_cols(scale, spread[...])
    out_f = jnp.dot(g_f[...], w_f[...], preferred_element_type=f32)
    out_r = jnp.dot(g_r[...], w_r[...], preferred_element_type=f32)
    for s, ref in enumerate((o0, o1, o2, o3)):
        cols = slice(s * 128, (s + 1) * 128)
        part = out_f[:, cols] * wide[:, 0:128] + out_r[:, cols] * wide[:, 128:256]
        ref[...] = part.astype(ref.dtype)


def project_out(g_f, g_r, sums, w_f, w_r, spread):
    m = g_f.shape[0]
    n = m // BLOCK
    g_in = pl.BlockSpec((BLOCK, INNER), lambda g: (g, 0))
    s_in = pl.BlockSpec((2, BLOCK), lambda g: (0, g))
    o = pl.BlockSpec((BLOCK, 128), lambda g: (g, 0))
    return pl.pallas_call(
        k4_body,
        grid=(n,),
        in_specs=[g_in, g_in] + [s_in] * 4 + [whole(w_f.shape), whole(w_r.shape), whole(spread.shape)],
        out_specs=[o] * 4,
        out_shape=[jax.ShapeDtypeStruct((m, 128), f32)] + [jax.ShapeDtypeStruct((m, 128), bf16)] * 3,
        compiler_params=params(16),
        cost_estimate=cost(m * 1e6, m * 3000),
        name="project_out",
    )(g_f, g_r, *sums, w_f, w_r, spread)


def row_spread():
    out = np.zeros((16, 256), np.float32)
    for part in range(2):
        out[part * 8, 0:128] = 1.0
        out[part * 8 + 1, 128:256] = 1.0
    return out


def around(array, axis, count, shift):
    return lax.ppermute(array, axis, [(i, (i + shift) % count) for i in range(count)])


def digit_perm(count, stride, shift):
    pairs = []
    for i in range(count):
        d = (i // stride) % 4
        pairs.append((i, i + (((d + shift) % 4) - d) * stride))
    return pairs


N_PARTS = 2
INTRA_PARTS = 4


def shards(
    hidden, w_x, w_z, w_bc, w_dt, conv_x, conv_bc, dt_bias, decay_rate, skip_gain, norm_gain, w_out,
    piece_lengths,
):
    rows = hidden.shape[0]
    ctx, mp = lax.axis_index("ctx"), lax.axis_index("mp")
    n_ctx, n_mp = lax.axis_size("ctx"), lax.axis_size("mp")

    hs = [hidden] + [around(hidden, "mp", n_mp, s) for s in range(1, n_mp)]
    low = lax.ppermute(hidden[rows - EDGE :], "ctx", [(i, i + 1) for i in range(n_ctx - 1)])
    high = lax.ppermute(hidden[:EDGE], "ctx", [(i + 1, i) for i in range(n_ctx - 1)])
    edge = jnp.concatenate([low, high], axis=0)
    edges = [edge] + [around(edge, "mp", n_mp, s) for s in range(1, n_mp)]

    width = w_x.shape[0]
    here = width // n_mp
    at = jnp.arange(width, dtype=jnp.int32)
    place = ((mp - at // here) % n_mp) * here + at % here
    pick_f = (place[:, None] == at[None, :]).astype(bf16)
    pick_r = (width - 1 - place[:, None] == at[None, :]).astype(bf16)
    w_1 = jnp.concatenate([w_x, w_bc[:, :NSTATE]], axis=1)
    w_2 = jnp.concatenate([w_bc[:, NSTATE:], w_z], axis=1)
    w_1f, w_1r, w_2f, w_2r = (
        jnp.dot(pick, w, preferred_element_type=f32).astype(bf16)
        for w in (w_1, w_2) for pick in (pick_f, pick_r)
    )
    wdt = jnp.concatenate(
        [jnp.dot(pick, w_dt, preferred_element_type=f32).astype(bf16).T for pick in (pick_f, pick_r)], axis=0
    )
    goal = ((mp + at // here) % n_mp) * here + at % here
    out_pick_f = (goal[None, :] == at[:, None]).astype(bf16)
    out_pick_r = (width - 1 - goal[None, :] == at[:, None]).astype(bf16)
    w_of = jnp.dot(w_out, out_pick_f, preferred_element_type=f32).astype(bf16)
    w_or = jnp.dot(w_out, out_pick_r, preferred_element_type=f32).astype(bf16)

    gain = norm_gain[None, :]
    spread = jnp.asarray(head_spread(), bf16)
    spread_rows = jnp.asarray(row_spread(), bf16)
    meta = jnp.stack([ctx * rows, ctx % 4, (ctx // 4) % 4, (ctx // 16) % 4]).astype(jnp.int32)

    xb_f, xb_r, cum, dt, fs, starts, decays, *pays = local_states(
        piece_lengths, meta, dt_bias, decay_rate, hs, edges, w_1f, w_1r, wdt, conv_x, conv_bc, spread
    )

    locals_ = ()

    def beside(part, received):
        nonlocal locals_
        locals_ = intra(
            part, INTRA_PARTS, piece_lengths, meta, skip_gain, hs, edges, w_2f, w_2r, conv_x, conv_bc,
            xb_f, xb_r, cum, dt, locals_,
        )
        received, locals_ = lax.optimization_barrier((received, tuple(locals_)))
        return received

    def moved(arrays, stride):
        return [lax.ppermute(a, "ctx", digit_perm(n_ctx, stride, s)) for s, a in zip((1, 2, 3), arrays)]

    pre_s, pre_a, pay = join_group(meta, [pays[0]] + beside(0, moved(pays[1:], 1)))
    low_s, low_a, top = join_middle(meta, [pay] + beside(1, moved([pay] * 3, 4)))
    back = join_top(meta, beside(2, moved([top] * 3, 16)) + [low_s, low_a, pre_s, pre_a])
    quarters = [back[0]] + beside(3, moved(back[1:], 1))

    out = []
    for p in range(N_PARTS):
        g_f, g_r, sums = gate(p, N_PARTS, meta, locals_, fs, starts, decays, quarters, gain, spread)
        all_sums = [sums] + [around(sums, "mp", n_mp, s) for s in range(1, n_mp)]
        own, *sent = project_out(g_f, g_r, all_sums, w_of, w_or, spread_rows)
        got = [around(piece, "mp", n_mp, s + 1) for s, piece in enumerate(sent)]
        total = own
        for piece in got:
            total = total + piece.astype(f32)
        out.append(total.astype(bf16))
    return jnp.concatenate(out, axis=0)


def solution(mesh):
    return jax.shard_map(
        shards,
        mesh=mesh,
        in_specs=(
            P("ctx", "mp"),
            P(None, "mp"),
            P(None, "mp"),
            P(),
            P(None, "mp"),
            P(None, "mp"),
            P(),
            P("mp"),
            P("mp"),
            P("mp"),
            P("mp"),
            P("mp", None),
            P(),
        ),
        out_specs=P("ctx", "mp"),
        check_vma=False,
    )
```

```python
import functools

import jax
import jax.numpy as jnp
import numpy as np
from jax import lax
from jax.experimental import pallas as pl
from jax.experimental.pallas import tpu as pltpu
from jax.sharding import PartitionSpec as P

E = 1024
HEAD_DIM = 64
NSTATE = 128
BLOCK = 256
HEADS_HERE = 4
INNER = HEADS_HERE * HEAD_DIM
PIECES = 16
EPSILON = 1e-05
FAR = -1e30
EDGE = 16
MIX = INNER + NSTATE
QUARTER = NSTATE // 4
RUN = (4, 2)
HERE = 4
BLOCKS = 2 * HERE
PAY = 2 * QUARTER + 16

bf16 = jnp.bfloat16
f32 = jnp.float32


def head_spread():
    out = np.zeros((16, 2 * INNER), np.float32)
    for part in range(2):
        for stream in range(2):
            for h in range(HEADS_HERE):
                first = stream * INNER + h * HEAD_DIM
                out[part * 8 + stream * 4 + h, first : first + HEAD_DIM] = 1.0
    return out


def whole(shape):
    return pl.BlockSpec(shape, lambda *_: (0,) * len(shape))


SMEM = pl.BlockSpec(memory_space=pltpu.SMEM)


def params(mib):
    return pltpu.CompilerParams(
        dimension_semantics=("arbitrary",), vmem_limit_bytes=mib * 1024 * 1024
    )


def cost(flops, nbytes):
    return pl.CostEstimate(flops=int(flops), bytes_accessed=int(nbytes), transcendentals=0)


def bounds_of(pieces_ref):
    total = pieces_ref[0]
    ends = [total]
    for k in range(1, PIECES):
        total = total + pieces_ref[k]
        ends.append(total)
    return ends


def seg_rows(ends, first):
    shape = (8, BLOCK)
    pos = (
        first - 3 + lax.broadcasted_iota(jnp.int32, shape, 0)
        + lax.broadcasted_iota(jnp.int32, shape, 1)
    )
    seg = jnp.zeros(shape, jnp.int32)
    for end in ends:
        seg = seg + (pos >= end).astype(jnp.int32)
    return seg.astype(f32)


def has_boundary(ends, first):
    found = jnp.int32(0)
    for end in ends:
        found = found + ((end > first - 3) & (end <= first + BLOCK + 2)).astype(jnp.int32)
    return found > 0


def split2(rows):
    high = rows.astype(bf16)
    return jnp.concatenate([high, (rows - high.astype(f32)).astype(bf16)], axis=0)


def rows_to_cols(rows, spread):
    return lax.dot_general(
        split2(rows), spread, (((0,), (0,)), ((), ())), preferred_element_type=f32
    )


def row_of(chunk, g):
    return EDGE + g * BLOCK + (g // RUN[chunk]) * 2 * EDGE


def block_of(chunk, g):
    return g + 2 if chunk == 0 else g + 4 * (g // 2)


def load_window(hs, chunk, g):
    at = pl.multiple_of(row_of(chunk, g) - EDGE, EDGE)
    return jnp.concatenate([h[pl.ds(at, BLOCK + 2 * EDGE), :] for h in hs], axis=1)


def silu(v):
    half = 0.5 * v
    return half + half * jnp.tanh(half)


def tap_rows(conv_x, conv_bc):
    return [conv_x[:, 0:128], conv_x[:, 128:256], conv_bc[:, 0:128], conv_bc[:, 128:256]]


def conv_tile(scratch, tile, taps, reverse, masks):
    total = None
    for back in range(4):
        first = back if reverse else EDGE - back
        term = scratch[tile, pl.ds(first, BLOCK), :] * taps[3 - back : 4 - back, :]
        if masks is not None and back:
            row = 3 + back if reverse else 3 - back
            term = term * masks[:, row : row + 1]
        total = term if total is None else total + term
    return silu(total).astype(bf16)


def keep_rounded(scratch, proj):
    for tile in range(scratch.shape[0]):
        scratch[tile] = proj[:, tile * 128 : (tile + 1) * 128].astype(bf16).astype(f32)


def per_head(scalars, shape, axis, width):
    head = lax.broadcasted_iota(jnp.int32, shape, axis) // width % HEADS_HERE
    out = jnp.full(shape, scalars[0], f32)
    for h in range(1, HEADS_HERE):
        out = jnp.where(head == h, scalars[h], out)
    return out


def split_rows(decays):
    at = lax.broadcasted_iota(jnp.int32, (16, INNER), 0)
    out = jnp.zeros((16, INNER), f32)
    for k, decay in enumerate(decays):
        high = decay.astype(bf16).astype(f32)
        out = jnp.where(at == 2 * k, high, jnp.where(at == 2 * k + 1, decay - high, out))
    return out.astype(bf16)


def decays_of(rows):
    wide = rows.astype(f32)
    return [wide[2 * k : 2 * k + 1, :] + wide[2 * k + 1 : 2 * k + 2, :] for k in range(2)]


def row_quantities(
    chunk, ends, origin, hs, wdt, dt_bias, rate, spread, cum_o, dt_o, fs_o, same_s, te_s, blockdec
):
    raw = []
    for b in range(HERE):
        at = row_of(chunk, b)
        block = jnp.concatenate([h[at : at + BLOCK, :] for h in hs], axis=1)
        raw.append(
            lax.dot_general(wdt[...], block, (((1,), (1,)), ((), ())), preferred_element_type=f32)
        )
    shape = (8 * HERE, BLOCK)
    v = jnp.concatenate(raw, axis=0).astype(bf16).astype(f32) + per_head(dt_bias, shape, 0, 1)
    dt = jnp.maximum(v, 0.0) + jnp.log1p(jnp.exp(-jnp.abs(v)))
    logd = -dt * per_head(rate, shape, 0, 1)
    high = logd.astype(bf16)
    rest = logd - high.astype(f32)
    middle = rest.astype(bf16)
    low = (rest - middle.astype(f32)).astype(bf16)
    row_at = lax.broadcasted_iota(jnp.int32, (BLOCK, BLOCK), 0)
    col_at = lax.broadcasted_iota(jnp.int32, (BLOCK, BLOCK), 1)
    summed = []
    for keep in (row_at <= col_at, row_at >= col_at):
        ones = keep.astype(f32).astype(bf16)
        summed.append(sum(jnp.dot(p, ones, preferred_element_type=f32) for p in (low, middle, high)))
    forward = lax.broadcasted_iota(jnp.int32, (8, BLOCK), 0) < HEADS_HERE
    spread_f = spread[0:8, :].astype(f32)
    for b in range(HERE):
        rows = slice(b * 8, (b + 1) * 8)
        cols = slice(b * BLOCK, (b + 1) * BLOCK)
        cum = jnp.where(forward, summed[0][rows], summed[1][rows])
        dt_b = dt[rows]
        seg = seg_rows(ends, origin + block_of(chunk, b) * BLOCK)
        same_s[b] = (seg == seg[3:4, :]).astype(f32)
        own = jnp.broadcast_to(seg[3:4, :], (8, BLOCK))
        seg_end = jnp.where(forward, seg[3:4, BLOCK - 1 : BLOCK], seg[3:4, 0:1])
        seg_in = jnp.where(forward, seg[2:3, 0:1], seg[4:5, BLOCK - 1 : BLOCK])
        total = jnp.where(forward, cum[:, BLOCK - 1 : BLOCK], cum[:, 0:1])
        to_end = jnp.exp(total - cum) * (own == seg_end).astype(f32) * dt_b
        block_decay = jnp.exp(total) * (seg_end == seg_in).astype(f32)
        cum_o[:, cols] = cum
        dt_o[:, cols] = dt_b
        fs_o[:, cols] = jnp.exp(cum) * (own == seg_in).astype(f32)
        te_s[b] = split2(to_end)
        decay_row = jnp.sum(
            jnp.concatenate([block_decay, block_decay], axis=1) * spread_f, axis=0, keepdims=True
        )
        blockdec[b] = jnp.broadcast_to(decay_row, (8, 2 * INNER))


def k1_body(chunk, pieces, meta, dt_bias, rate, h0, h1, h2, h3, w_f, w_r, wdt, conv_x, conv_bc, spread, *rest):
    if chunk == 0:
        xb_f, xb_r, cum_o, dt_o, fs_o, added, blockdec, sf, sr, same_s, te_s = rest
    else:
        added_0, blockdec_0, *rest = rest
        xb_f, xb_r, cum_o, dt_o, fs_o, start_o, decay_o, p0, p1, p2, p3 = rest[:11]
        sf, sr, same_s, te_s, added, blockdec, total_s = rest[11:]
    g = pl.program_id(0)
    ends = bounds_of(pieces)
    first = meta[0] + block_of(chunk, g) * BLOCK
    hs = (h0, h1, h2, h3)

    @pl.when(g == 0)
    def _():
        row_quantities(
            chunk, ends, meta[0], hs, wdt, dt_bias, rate, spread, cum_o, dt_o, fs_o, same_s, te_s, blockdec
        )

    crosses = has_boundary(ends, first)

    def states(masked):
        window = load_window(hs, chunk, g)
        masks = same_s[g].T if masked else None
        taps = tap_rows(conv_x, conv_bc)
        wide = lax.dot_general(
            te_s[g], spread[...], (((0,), (0,)), ((), ())), preferred_element_type=f32
        )
        keep_rounded(sf, jnp.dot(window[: EDGE + BLOCK], w_f[...], preferred_element_type=f32))
        keep_rounded(sr, jnp.dot(window[EDGE:], w_r[...], preferred_element_type=f32))
        for stream, scratch, ref in ((0, sf, xb_f), (1, sr, xb_r)):
            scaled = []
            for tile in (0, 1):
                x = conv_tile(scratch, tile, taps[tile], stream == 1, masks)
                ref[:, tile * 128 : (tile + 1) * 128] = x
                at = stream * INNER + tile * 128
                scaled.append((x.astype(f32) * wide[:, at : at + 128]).astype(bf16))
            b = conv_tile(scratch, 2, taps[2], stream == 1, masks)
            ref[:, INNER:MIX] = b
            added[stream, g] = lax.dot_general(
                b, jnp.concatenate(scaled, axis=1), (((0,), (0,)), ((), ())), preferred_element_type=f32
            )

    pl.when(crosses)(lambda: states(True))
    pl.when(jnp.logical_not(crosses))(lambda: states(False))
    if chunk == 0:
        return

    @pl.when(g == HERE - 1)
    def _():
        sources = {block_of(0, k): (added_0, blockdec_0, k) for k in range(HERE)}
        sources.update({block_of(1, k): (added, blockdec, k) for k in range(HERE)})
        decays = []
        for stream in range(2):
            state = jnp.zeros((NSTATE, INNER), f32)
            decay = jnp.ones((1, INNER), f32)
            for step in range(BLOCKS):
                b = step if stream == 0 else BLOCKS - 1 - step
                start_o[stream, b] = state
                decay_o[stream, b] = jnp.broadcast_to(decay, (8, INNER))
                states_ref, decays_ref, k = sources[b]
                d = decays_ref[k, 0:1, stream * INNER : (stream + 1) * INNER]
                state = d * state + states_ref[stream, k]
                decay = decay * d
            total_s[stream] = state
            decays.append(decay)
        rows = split_rows(decays)
        for s, ref in enumerate((p0, p1, p2, p3)):
            at = pl.multiple_of(lax.rem(meta[1] + s, 4) * QUARTER, QUARTER)
            ref[0:QUARTER, :] = total_s[0, pl.ds(at, QUARTER), :].astype(bf16)
            ref[QUARTER : 2 * QUARTER, :] = total_s[1, pl.ds(at, QUARTER), :].astype(bf16)
            ref[2 * QUARTER : PAY, :] = rows


def local_states(chunk, pieces, meta, dt_bias, rate, hs, w_f, w_r, wdt, conv_x, conv_bc, spread, others=()):
    rows = HERE * BLOCK
    row = pl.BlockSpec((BLOCK, MIX), lambda g: (g, 0))
    fixed = [*hs, w_f, w_r, wdt, conv_x, conv_bc, spread, *others]
    added = jax.ShapeDtypeStruct((2, HERE, NSTATE, INNER), f32)
    blockdec = jax.ShapeDtypeStruct((HERE, 8, 2 * INNER), f32)
    shapes = [
        jax.ShapeDtypeStruct((rows, MIX), bf16),
        jax.ShapeDtypeStruct((rows, MIX), bf16),
        jax.ShapeDtypeStruct((8, rows), f32),
        jax.ShapeDtypeStruct((8, rows), f32),
        jax.ShapeDtypeStruct((8, rows), f32),
    ]
    scratch = [
        pltpu.VMEM((MIX // 128, EDGE + BLOCK, 128), f32),
        pltpu.VMEM((MIX // 128, EDGE + BLOCK, 128), f32),
        pltpu.VMEM((HERE, 8, BLOCK), f32),
        pltpu.VMEM((HERE, 16, BLOCK), bf16),
    ]
    if chunk == 0:
        shapes += [added, blockdec]
    else:
        shapes += [
            jax.ShapeDtypeStruct((2, BLOCKS, NSTATE, INNER), f32),
            jax.ShapeDtypeStruct((2, BLOCKS, 8, INNER), f32),
        ] + [jax.ShapeDtypeStruct((PAY, INNER), bf16)] * 4
        scratch += [pltpu.VMEM(a.shape, f32) for a in (added, blockdec)]
        scratch += [pltpu.VMEM((2, NSTATE, INNER), f32)]
    return pl.pallas_call(
        functools.partial(k1_body, chunk),
        grid=(HERE,),
        in_specs=[SMEM] * 4 + [whole(a.shape) for a in fixed],
        out_specs=[row, row] + [whole(s.shape) for s in shapes[2:]],
        out_shape=shapes,
        scratch_shapes=scratch,
        compiler_params=params(24),
        cost_estimate=cost(rows * 6e6, rows * 4000),
        name="local_states",
    )(pieces, meta, dt_bias, rate, *fixed)


def k2_body(
    chunk, base, n_alias, pieces, meta, skip_gain, h0, h1, h2, h3, w_f, w_r, conv_x, conv_bc,
    xb_f, xb_r, cum_i, dt_i, *rest,
):
    c_f, c_r, y_f, y_r, z_f, z_r, sf, sr, open_mask = rest[n_alias:]
    step = pl.program_id(0)
    g = step + base
    ends = bounds_of(pieces)
    first = meta[0] + block_of(chunk, g) * BLOCK
    row_at = lax.broadcasted_iota(jnp.int32, (BLOCK, BLOCK), 0)
    col_at = lax.broadcasted_iota(jnp.int32, (BLOCK, BLOCK), 1)
    half = BLOCK // 2

    @pl.when(step == 0)
    def _():
        open_mask[0] = jnp.where(row_at >= col_at, 0.0, FAR)
        open_mask[1] = jnp.where(row_at <= col_at, 0.0, FAR)

    crosses = has_boundary(ends, first)

    @pl.when(crosses)
    def _():
        seg = seg_rows(ends, first)
        together = seg.T[:, 3:4] == seg[3:4, :]
        open_mask[2] = jnp.where(together & (row_at >= col_at), 0.0, FAR)
        open_mask[3] = jnp.where(together & (row_at <= col_at), 0.0, FAR)

    def mix(masked):
        window = load_window((h0, h1, h2, h3), chunk, g)
        masks = None
        if masked:
            seg = seg_rows(ends, first)
            masks = (seg == seg[3:4, :]).astype(f32).T
        proj_f = jnp.dot(window[: EDGE + BLOCK], w_f[...], preferred_element_type=f32)
        proj_r = jnp.dot(window[EDGE:], w_r[...], preferred_element_type=f32)
        keep_rounded(sf, proj_f)
        keep_rounded(sr, proj_r)
        z_f[...] = silu(proj_f[EDGE:, NSTATE:].astype(bf16).astype(f32))
        z_r[...] = silu(proj_r[0:BLOCK, NSTATE:].astype(bf16).astype(f32))
        taps = tap_rows(conv_x, conv_bc)[3]
        cum = cum_i[...]
        cum_t = cum.T
        log_dt = jnp.log(dt_i[...]) - cum
        lane_head = lax.broadcasted_iota(jnp.int32, (BLOCK, INNER), 1) // HEAD_DIM
        skip = per_head(skip_gain, (1, INNER), 1, HEAD_DIM)
        for stream, xb, scratch, c_ref, y_ref in ((0, xb_f, sf, c_f, y_f), (1, xb_r, sr, c_r, y_r)):
            c_rows = conv_tile(scratch, 0, taps, stream == 1, masks)
            c_ref[...] = c_rows
            x = xb[:, 0:INNER]
            b = xb[:, INNER:MIX]
            heads = [jnp.where(lane_head == h, x, jnp.zeros_like(x)) for h in range(HEADS_HERE)]
            for part in range(2):
                rows = slice(part * half, (part + 1) * half)
                if stream == 0:
                    cols = slice(0, half) if part == 0 else slice(0, BLOCK)
                else:
                    cols = slice(0, BLOCK) if part == 0 else slice(half, BLOCK)
                scores = lax.dot_general(
                    c_rows[rows, :], b[cols, :], (((1,), (1,)), ((), ())), preferred_element_type=f32
                )
                mask = open_mask[(2 if masked else 0) + stream, rows, cols]
                total = x[rows, :].astype(f32) * skip
                for h in range(HEADS_HERE):
                    at = stream * HEADS_HERE + h
                    gap = (cum_t[rows, at : at + 1] + log_dt[at : at + 1, cols]) + mask
                    weight = (jnp.exp(gap) * scores).astype(bf16)
                    total = total + jnp.dot(weight, heads[h][cols, :], preferred_element_type=f32)
                y_ref[rows, :] = total

    pl.when(crosses)(lambda: mix(True))
    pl.when(jnp.logical_not(crosses))(lambda: mix(False))


def intra(chunk, part, n_parts, pieces, meta, skip_gain, hs, w_f, w_r, conv_x, conv_bc, xb_f, xb_r, cum, dt, before):
    rows = HERE * BLOCK
    here = HERE // n_parts
    base = part * here
    col = pl.BlockSpec((8, BLOCK), lambda g: (0, g + base))
    mixed = pl.BlockSpec((BLOCK, MIX), lambda g: (g + base, 0))
    c_out = pl.BlockSpec((BLOCK, NSTATE), lambda g: (g + base, 0))
    y_out = pl.BlockSpec((BLOCK, INNER), lambda g: (g + base, 0))
    fixed = [*hs, w_f, w_r, conv_x, conv_bc]
    before = list(before)
    n_in = 3 + len(fixed) + 4
    return pl.pallas_call(
        functools.partial(k2_body, chunk, base, len(before)),
        grid=(here,),
        in_specs=[SMEM] * 3 + [whole(a.shape) for a in fixed] + [mixed, mixed, col, col]
        + [pl.BlockSpec(memory_space=pl.ANY)] * len(before),
        out_specs=[c_out, c_out, y_out, y_out, y_out, y_out],
        out_shape=[jax.ShapeDtypeStruct((rows, NSTATE), bf16)] * 2
        + [jax.ShapeDtypeStruct((rows, INNER), f32)] * 4,
        input_output_aliases={n_in + k: k for k in range(len(before))},
        scratch_shapes=[
            pltpu.VMEM((1, EDGE + BLOCK, 128), f32),
            pltpu.VMEM((1, EDGE + BLOCK, 128), f32),
            pltpu.VMEM((4, BLOCK, BLOCK), f32),
        ],
        compiler_params=params(24),
        cost_estimate=cost(here * BLOCK * 5e6, here * BLOCK * 5000),
        name="intra",
    )(pieces, meta, skip_gain, *fixed, xb_f, xb_r, cum, dt, *before)


def state_rows(ref, stream):
    return ref[stream * QUARTER : (stream + 1) * QUARTER, :].astype(f32)


def put_payload(ref, states, decays):
    for stream in range(2):
        ref[stream * QUARTER : (stream + 1) * QUARTER, :] = states[stream].astype(bf16)
    ref[2 * QUARTER : PAY, :] = split_rows(decays)


def group_body(meta, own, r1, r2, r3, pre_s, pre_a, pay, stage):
    me = meta[1]
    for s, ref in enumerate((own, r1, r2, r3)):
        stage[lax.rem(me - s + 4, 4)] = ref[...]
    states, decays = [], []
    for stream in range(2):
        state = jnp.zeros((QUARTER, INNER), f32)
        decay = jnp.ones((1, INNER), f32)
        for step in range(4):
            k = step if stream == 0 else 3 - step
            pre_s[k, stream] = state
            pre_a[k, stream] = jnp.broadcast_to(decay, (8, INNER))
            one = stage[k]
            d = decays_of(one[2 * QUARTER :])[stream]
            state = d * state + one[stream * QUARTER : (stream + 1) * QUARTER].astype(f32)
            decay = decay * d
        states.append(state)
        decays.append(decay)
    put_payload(pay, states, decays)


def before_digit(place, stream, got):
    low_s, low_a = jnp.zeros((QUARTER, INNER), f32), jnp.ones((1, INNER), f32)
    for s in (1, 2, 3):
        there = s <= place
        state, decay = got[s if stream == 0 else 4 - s]
        low_s = jnp.where(there, low_s + low_a * state, low_s)
        low_a = jnp.where(there, low_a * decay, low_a)
    return low_s, low_a


def middle_body(meta, own, r1, r2, r3, low_o, low_ao, pay):
    digit = meta[2]
    states, decays = [], []
    rows = [decays_of(r[2 * QUARTER : PAY, :]) for r in (own, r1, r2, r3)]
    for stream in range(2):
        got = [(state_rows(r, stream), rows[s][stream]) for s, r in enumerate((own, r1, r2, r3))]
        place = digit if stream == 0 else 3 - digit
        low_s, low_a = before_digit(place, stream, got)
        low_o[stream] = low_s
        low_ao[stream] = jnp.broadcast_to(low_a, (8, INNER))
        total_s, total_a = got[0][1] * low_s + got[0][0], got[0][1] * low_a
        for s in (3, 2, 1):
            there = s > place
            state, decay = got[s if stream == 0 else 4 - s]
            total_s = jnp.where(there, decay * total_s + state, total_s)
            total_a = jnp.where(there, decay * total_a, total_a)
        states.append(total_s)
        decays.append(total_a)
    put_payload(pay, states, decays)


def top_body(meta, r1, r2, r3, low_i, low_ai, pre_s, pre_a, *outs):
    digit = meta[3]
    rows = [None] + [decays_of(r[2 * QUARTER : PAY, :]) for r in (r1, r2, r3)]
    for stream in range(2):
        got = [None] + [
            (state_rows(r, stream), rows[s + 1][stream]) for s, r in enumerate((r1, r2, r3))
        ]
        place = digit if stream == 0 else 3 - digit
        top_s, _ = before_digit(place, stream, got)
        group_s = low_ai[stream, 0:1, :] * top_s + low_i[stream]
        for s, ref in enumerate(outs):
            k = lax.rem(meta[1] + s, 4)
            member = pre_a[k, stream][0:1, :] * group_s + pre_s[k, stream]
            ref[stream * QUARTER : (stream + 1) * QUARTER, :] = member.astype(bf16)


def small_call(body, name, meta, arrays, shapes, scratch=()):
    return pl.pallas_call(
        body,
        grid=(1,),
        in_specs=[SMEM] + [whole(a.shape) for a in arrays],
        out_specs=[whole(s.shape) for s in shapes],
        out_shape=shapes,
        scratch_shapes=list(scratch),
        compiler_params=params(6),
        cost_estimate=cost(2e6, 1e6),
        name=name,
    )(meta, *arrays)


PAYLOAD = jax.ShapeDtypeStruct((PAY, INNER), bf16)


def join_group(meta, arrays):
    shapes = [
        jax.ShapeDtypeStruct((4, 2, QUARTER, INNER), f32),
        jax.ShapeDtypeStruct((4, 2, 8, INNER), f32),
        PAYLOAD,
    ]
    return small_call(group_body, "join_group", meta, arrays, shapes, [pltpu.VMEM((4, PAY, INNER), bf16)])


def join_middle(meta, arrays):
    shapes = [
        jax.ShapeDtypeStruct((2, QUARTER, INNER), f32),
        jax.ShapeDtypeStruct((2, 8, INNER), f32),
        PAYLOAD,
    ]
    return small_call(middle_body, "join_middle", meta, arrays, shapes)


def join_top(meta, arrays):
    shapes = [jax.ShapeDtypeStruct((2 * QUARTER, INNER), bf16)] * 4
    return small_call(top_body, "join_top", meta, arrays, shapes)


def k3_body(meta, c_f, c_r, y_f, y_r, z_f, z_r, fs, starts, decays, q0, q1, q2, q3, gain, spread, *rest):
    g_f, g_r, sums, s_in = rest[-4:]

    @pl.when(pl.program_id(0) == 0)
    def _():
        for s, ref in enumerate((q0, q1, q2, q3)):
            at = pl.multiple_of(lax.rem(meta[1] - s + 4, 4) * QUARTER, QUARTER)
            for stream in range(2):
                s_in[stream, pl.ds(at, QUARTER), :] = state_rows(ref, stream)

    wide = rows_to_cols(fs[...], spread[...])
    out = []
    for stream, c_ref, y_ref, z_ref, g_ref in ((0, c_f, y_f, z_f, g_f), (1, c_r, y_r, z_r, g_r)):
        state = starts[stream, 0] + decays[stream, 0, 0:1, :] * s_in[stream]
        carried = jnp.dot(c_ref[...], state.astype(bf16), preferred_element_type=f32)
        mixed = y_ref[...] + carried * wide[:, stream * INNER : (stream + 1) * INNER]
        gated = mixed * z_ref[...]
        square = gated * gated
        out.append(jnp.sum((square[:, 0:128] + square[:, 128:256]).T, axis=0, keepdims=True))
        g_ref[...] = (gated * gain[...]).astype(bf16)
    sums[...] = jnp.concatenate(out, axis=0)


def gate(chunk, meta, locals_, fs, starts, decays, quarters, gain, spread, before):
    base = chunk * HERE
    m = BLOCKS * BLOCK
    c_in = pl.BlockSpec((BLOCK, NSTATE), lambda g: (g, 0))
    y_in = pl.BlockSpec((BLOCK, INNER), lambda g: (g, 0))
    y_out = pl.BlockSpec((BLOCK, INNER), lambda g: (g + base, 0))
    fixed = [*quarters, gain, spread]
    before = list(before)
    n_in = 1 + 6 + 3 + len(fixed)
    return pl.pallas_call(
        k3_body,
        grid=(HERE,),
        in_specs=[SMEM, c_in, c_in, y_in, y_in, y_in, y_in,
                  pl.BlockSpec((8, BLOCK), lambda g: (0, g)),
                  pl.BlockSpec((2, 1, NSTATE, INNER), lambda g: (0, block_of(chunk, g), 0, 0)),
                  pl.BlockSpec((2, 1, 8, INNER), lambda g: (0, block_of(chunk, g), 0, 0))]
        + [whole(a.shape) for a in fixed] + [pl.BlockSpec(memory_space=pl.ANY)] * len(before),
        out_specs=[y_out, y_out, pl.BlockSpec((2, BLOCK), lambda g: (0, g + base))],
        out_shape=[
            jax.ShapeDtypeStruct((m, INNER), bf16),
            jax.ShapeDtypeStruct((m, INNER), bf16),
            jax.ShapeDtypeStruct((2, m), f32),
        ],
        input_output_aliases={n_in + k: k for k in range(len(before))},
        scratch_shapes=[pltpu.VMEM((2, NSTATE, INNER), f32)],
        compiler_params=params(16),
        cost_estimate=cost(m * 3e5, m * 3000),
        name="gate",
    )(meta, *locals_, fs, starts, decays, *fixed, *before)


def k4_body(g_f, g_r, s0, s1, s2, s3, w_f, w_r, spread, o0, o1, o2, o3):
    total = (s0[...] + s1[...]) + (s2[...] + s3[...])
    scale = lax.rsqrt(total / E + EPSILON)
    scale = jnp.concatenate([scale, jnp.zeros((6, BLOCK), f32)], axis=0)
    wide = rows_to_cols(scale, spread[...])
    out_f = jnp.dot(g_f[...], w_f[...], preferred_element_type=f32)
    out_r = jnp.dot(g_r[...], w_r[...], preferred_element_type=f32)
    for s, ref in enumerate((o0, o1, o2, o3)):
        cols = slice(s * 128, (s + 1) * 128)
        part = out_f[:, cols] * wide[:, 0:128] + out_r[:, cols] * wide[:, 128:256]
        ref[...] = part.astype(ref.dtype)


def project_out(g_f, g_r, sums, w_f, w_r, spread):
    m = g_f.shape[0]
    n = m // BLOCK
    g_in = pl.BlockSpec((BLOCK, INNER), lambda g: (g, 0))
    s_in = pl.BlockSpec((2, BLOCK), lambda g: (0, g))
    o = pl.BlockSpec(
        (BLOCK, 128), lambda g: (jnp.where(g < HERE, block_of(0, g), block_of(1, g - HERE)), 0)
    )
    return pl.pallas_call(
        k4_body,
        grid=(n,),
        in_specs=[g_in, g_in] + [s_in] * 4 + [whole(w_f.shape), whole(w_r.shape), whole(spread.shape)],
        out_specs=[o] * 4,
        out_shape=[jax.ShapeDtypeStruct((m, 128), f32)] + [jax.ShapeDtypeStruct((m, 128), bf16)] * 3,
        compiler_params=params(16),
        cost_estimate=cost(m * 1e6, m * 3000),
        name="project_out",
    )(g_f, g_r, *sums, w_f, w_r, spread)


def row_spread():
    out = np.zeros((16, 256), np.float32)
    for part in range(2):
        out[part * 8, 0:128] = 1.0
        out[part * 8 + 1, 128:256] = 1.0
    return out


def around(array, axis, count, shift):
    return lax.ppermute(array, axis, [(i, (i + shift) % count) for i in range(count)])


def digit_perm(count, stride, shift):
    pairs = []
    for i in range(count):
        d = (i // stride) % 4
        pairs.append((i, i + (((d + shift) % 4) - d) * stride))
    return pairs


INTRA_PARTS = 2


def shards(
    hidden, w_x, w_z, w_bc, w_dt, conv_x, conv_bc, dt_bias, decay_rate, skip_gain, norm_gain, w_out,
    piece_lengths,
):
    rows = hidden.shape[0]
    ctx, mp = lax.axis_index("ctx"), lax.axis_index("mp")
    n_ctx, n_mp = lax.axis_size("ctx"), lax.axis_size("mp")

    run = rows // 4
    middle = hidden[run - EDGE : 3 * run + EDGE]
    hs_0 = [middle] + [around(middle, "mp", n_mp, s) for s in range(1, n_mp)]
    low = lax.ppermute(hidden[rows - EDGE :], "ctx", [(i, i + 1) for i in range(n_ctx - 1)])
    high = lax.ppermute(hidden[:EDGE], "ctx", [(i + 1, i) for i in range(n_ctx - 1)])
    outer = jnp.concatenate([low, hidden[: run + EDGE], hidden[3 * run - EDGE :], high], axis=0)
    hs_1 = [outer] + [around(outer, "mp", n_mp, s) for s in range(1, n_mp)]

    width = w_x.shape[0]
    here = width // n_mp
    at = jnp.arange(width, dtype=jnp.int32)
    place = ((mp - at // here) % n_mp) * here + at % here
    pick_f = (place[:, None] == at[None, :]).astype(bf16)
    pick_r = (width - 1 - place[:, None] == at[None, :]).astype(bf16)
    w_1 = jnp.concatenate([w_x, w_bc[:, :NSTATE]], axis=1)
    w_2 = jnp.concatenate([w_bc[:, NSTATE:], w_z], axis=1)
    w_1f, w_1r, w_2f, w_2r = (
        jnp.dot(pick, w, preferred_element_type=f32).astype(bf16)
        for w in (w_1, w_2) for pick in (pick_f, pick_r)
    )
    wdt = jnp.concatenate(
        [jnp.dot(pick, w_dt, preferred_element_type=f32).astype(bf16).T for pick in (pick_f, pick_r)], axis=0
    )
    goal = ((mp + at // here) % n_mp) * here + at % here
    out_pick_f = (goal[None, :] == at[:, None]).astype(bf16)
    out_pick_r = (width - 1 - goal[None, :] == at[:, None]).astype(bf16)
    w_of = jnp.dot(w_out, out_pick_f, preferred_element_type=f32).astype(bf16)
    w_or = jnp.dot(w_out, out_pick_r, preferred_element_type=f32).astype(bf16)

    gain = norm_gain[None, :]
    spread = jnp.asarray(head_spread(), bf16)
    spread_rows = jnp.asarray(row_spread(), bf16)
    meta = jnp.stack([ctx * rows, ctx % 4, (ctx // 4) % 4, (ctx // 16) % 4]).astype(jnp.int32)

    first = (piece_lengths, meta, dt_bias, decay_rate)
    weights_1 = (w_1f, w_1r, wdt, conv_x, conv_bc, spread)
    weights_2 = (w_2f, w_2r, conv_x, conv_bc)

    xb_f, xb_r, cum, dt, fs_0, *middle_states = local_states(0, *first, hs_0, *weights_1)
    locals_0 = intra(
        0, 0, 1, piece_lengths, meta, skip_gain, hs_0, *weights_2, xb_f, xb_r, cum, dt, ()
    )
    hs_1, locals_0 = lax.optimization_barrier((tuple(hs_1), tuple(locals_0)))
    xb_f, xb_r, cum, dt, fs_1, starts, decays, *pays = local_states(
        1, *first, hs_1, *weights_1, middle_states
    )
    locals_1 = ()

    def beside(part, received):
        nonlocal locals_1
        locals_1 = intra(
            1, part, INTRA_PARTS, piece_lengths, meta, skip_gain, hs_1, *weights_2, xb_f, xb_r, cum, dt, locals_1
        )
        received, locals_1 = lax.optimization_barrier((received, tuple(locals_1)))
        return received

    def moved(arrays, stride):
        return [lax.ppermute(a, "ctx", digit_perm(n_ctx, stride, s)) for s, a in zip((1, 2, 3), arrays)]

    pre_s, pre_a, pay = join_group(meta, [pays[0]] + beside(0, moved(pays[1:], 1)))
    low_s, low_a, top = join_middle(meta, [pay] + beside(1, moved([pay] * 3, 4)))
    back = join_top(meta, moved([top] * 3, 16) + [low_s, low_a, pre_s, pre_a])
    quarters = [back[0]] + moved(back[1:], 1)

    gated = gate(0, meta, locals_0, fs_0, starts, decays, quarters, gain, spread, ())
    g_f, g_r, sums = gate(1, meta, locals_1, fs_1, starts, decays, quarters, gain, spread, gated)
    all_sums = [sums] + [around(sums, "mp", n_mp, s) for s in range(1, n_mp)]
    total, *sent = project_out(g_f, g_r, all_sums, w_of, w_or, spread_rows)
    for s, piece in enumerate(sent):
        total = total + around(piece, "mp", n_mp, s + 1).astype(f32)
    return total.astype(bf16)


def solution(mesh):
    return jax.shard_map(
        shards,
        mesh=mesh,
        in_specs=(
            P("ctx", "mp"),
            P(None, "mp"),
            P(None, "mp"),
            P(),
            P(None, "mp"),
            P(None, "mp"),
            P(),
            P("mp"),
            P("mp"),
            P("mp"),
            P("mp"),
            P("mp", None),
            P(),
        ),
        out_specs=P("ctx", "mp"),
        check_vma=False,
    )
```

```python
import functools

import jax
import jax.numpy as jnp
import numpy as np
from jax import lax
from jax.experimental import pallas as pl
from jax.experimental.pallas import tpu as pltpu
from jax.sharding import PartitionSpec as P

E = 1024
HEAD_DIM = 64
NSTATE = 128
BLOCK = 256
HEADS_HERE = 4
INNER = HEADS_HERE * HEAD_DIM
PIECES = 16
EPSILON = 1e-05
FAR = -1e30
EDGE = 16
MIX = INNER + NSTATE
QUARTER = NSTATE // 4
RUN = (4, 2)
HERE = 4
BLOCKS = 2 * HERE
PAY = 2 * QUARTER + 16

bf16 = jnp.bfloat16
f32 = jnp.float32


def head_spread():
    out = np.zeros((16, 2 * INNER), np.float32)
    for part in range(2):
        for stream in range(2):
            for h in range(HEADS_HERE):
                first = stream * INNER + h * HEAD_DIM
                out[part * 8 + stream * 4 + h, first : first + HEAD_DIM] = 1.0
    return out


def whole(shape):
    return pl.BlockSpec(shape, lambda *_: (0,) * len(shape))


SMEM = pl.BlockSpec(memory_space=pltpu.SMEM)


def params(mib):
    return pltpu.CompilerParams(
        dimension_semantics=("arbitrary",), vmem_limit_bytes=mib * 1024 * 1024
    )


def cost(flops, nbytes):
    return pl.CostEstimate(flops=int(flops), bytes_accessed=int(nbytes), transcendentals=0)


def bounds_of(pieces_ref):
    total = pieces_ref[0]
    ends = [total]
    for k in range(1, PIECES):
        total = total + pieces_ref[k]
        ends.append(total)
    return ends


def seg_rows(ends, first):
    shape = (8, BLOCK)
    pos = (
        first - 3 + lax.broadcasted_iota(jnp.int32, shape, 0)
        + lax.broadcasted_iota(jnp.int32, shape, 1)
    )
    seg = jnp.zeros(shape, jnp.int32)
    for end in ends:
        seg = seg + (pos >= end).astype(jnp.int32)
    return seg.astype(f32)


def has_boundary(ends, first):
    found = jnp.int32(0)
    for end in ends:
        found = found + ((end > first - 3) & (end <= first + BLOCK + 2)).astype(jnp.int32)
    return found > 0


def split2(rows):
    high = rows.astype(bf16)
    return jnp.concatenate([high, (rows - high.astype(f32)).astype(bf16)], axis=0)


def rows_to_cols(rows, spread):
    return lax.dot_general(
        split2(rows), spread, (((0,), (0,)), ((), ())), preferred_element_type=f32
    )


def row_of(chunk, g):
    return EDGE + g * BLOCK + (g // RUN[chunk]) * 2 * EDGE


def block_of(chunk, g):
    return g + 2 if chunk == 0 else g + 4 * (g // 2)


def load_window(hs, chunk, g):
    at = pl.multiple_of(row_of(chunk, g) - EDGE, EDGE)
    return jnp.concatenate([h[pl.ds(at, BLOCK + 2 * EDGE), :] for h in hs], axis=1)


def silu(v):
    half = 0.5 * v
    return half + half * jnp.tanh(half)


def tap_rows(conv_x, conv_bc):
    return [conv_x[:, 0:128], conv_x[:, 128:256], conv_bc[:, 0:128], conv_bc[:, 128:256]]


def conv_tile(scratch, tile, taps, reverse, masks):
    total = None
    for back in range(4):
        first = back if reverse else EDGE - back
        term = scratch[tile, pl.ds(first, BLOCK), :] * taps[3 - back : 4 - back, :]
        if masks is not None and back:
            row = 3 + back if reverse else 3 - back
            term = term * masks[:, row : row + 1]
        total = term if total is None else total + term
    return silu(total).astype(bf16)


def keep_rounded(scratch, proj):
    for tile in range(scratch.shape[0]):
        scratch[tile] = proj[:, tile * 128 : (tile + 1) * 128].astype(bf16).astype(f32)


def per_head(scalars, shape, axis, width):
    head = lax.broadcasted_iota(jnp.int32, shape, axis) // width % HEADS_HERE
    out = jnp.full(shape, scalars[0], f32)
    for h in range(1, HEADS_HERE):
        out = jnp.where(head == h, scalars[h], out)
    return out


def split_rows(decays):
    at = lax.broadcasted_iota(jnp.int32, (16, INNER), 0)
    out = jnp.zeros((16, INNER), f32)
    for k, decay in enumerate(decays):
        high = decay.astype(bf16).astype(f32)
        out = jnp.where(at == 2 * k, high, jnp.where(at == 2 * k + 1, decay - high, out))
    return out.astype(bf16)


def decays_of(rows):
    wide = rows.astype(f32)
    return [wide[2 * k : 2 * k + 1, :] + wide[2 * k + 1 : 2 * k + 2, :] for k in range(2)]


def row_quantities(
    chunk, ends, origin, hs, wdt, dt_bias, rate, spread, cum_o, dt_o, fs_o, same_s, te_s, blockdec
):
    raw = []
    for b in range(HERE):
        at = row_of(chunk, b)
        block = jnp.concatenate([h[at : at + BLOCK, :] for h in hs], axis=1)
        raw.append(
            lax.dot_general(wdt[...], block, (((1,), (1,)), ((), ())), preferred_element_type=f32)
        )
    shape = (8 * HERE, BLOCK)
    v = jnp.concatenate(raw, axis=0).astype(bf16).astype(f32) + per_head(dt_bias, shape, 0, 1)
    dt = jnp.maximum(v, 0.0) + jnp.log1p(jnp.exp(-jnp.abs(v)))
    logd = -dt * per_head(rate, shape, 0, 1)
    high = logd.astype(bf16)
    rest = logd - high.astype(f32)
    middle = rest.astype(bf16)
    low = (rest - middle.astype(f32)).astype(bf16)
    row_at = lax.broadcasted_iota(jnp.int32, (BLOCK, BLOCK), 0)
    col_at = lax.broadcasted_iota(jnp.int32, (BLOCK, BLOCK), 1)
    summed = []
    for keep in (row_at <= col_at, row_at >= col_at):
        ones = keep.astype(f32).astype(bf16)
        summed.append(sum(jnp.dot(p, ones, preferred_element_type=f32) for p in (low, middle, high)))
    forward = lax.broadcasted_iota(jnp.int32, (8, BLOCK), 0) < HEADS_HERE
    spread_f = spread[0:8, :].astype(f32)
    for b in range(HERE):
        rows = slice(b * 8, (b + 1) * 8)
        cols = slice(b * BLOCK, (b + 1) * BLOCK)
        cum = jnp.where(forward, summed[0][rows], summed[1][rows])
        dt_b = dt[rows]
        seg = seg_rows(ends, origin + block_of(chunk, b) * BLOCK)
        same_s[b] = (seg == seg[3:4, :]).astype(f32)
        own = jnp.broadcast_to(seg[3:4, :], (8, BLOCK))
        seg_end = jnp.where(forward, seg[3:4, BLOCK - 1 : BLOCK], seg[3:4, 0:1])
        seg_in = jnp.where(forward, seg[2:3, 0:1], seg[4:5, BLOCK - 1 : BLOCK])
        total = jnp.where(forward, cum[:, BLOCK - 1 : BLOCK], cum[:, 0:1])
        to_end = jnp.exp(total - cum) * (own == seg_end).astype(f32) * dt_b
        block_decay = jnp.exp(total) * (seg_end == seg_in).astype(f32)
        cum_o[:, cols] = cum
        dt_o[:, cols] = dt_b
        fs_o[:, cols] = jnp.exp(cum) * (own == seg_in).astype(f32)
        te_s[b] = split2(to_end)
        decay_row = jnp.sum(
            jnp.concatenate([block_decay, block_decay], axis=1) * spread_f, axis=0, keepdims=True
        )
        blockdec[b] = jnp.broadcast_to(decay_row, (8, 2 * INNER))


def k1_body(chunk, pieces, meta, dt_bias, rate, h0, h1, h2, h3, w_f, w_r, wdt, conv_x, conv_bc, spread, *rest):
    if chunk == 0:
        xb_f, xb_r, cum_o, dt_o, fs_o, added, blockdec, sf, sr, same_s, te_s = rest
    else:
        added_0, blockdec_0, *rest = rest
        xb_f, xb_r, cum_o, dt_o, fs_o, start_o, decay_o, p0, p1, p2, p3 = rest[:11]
        sf, sr, same_s, te_s, added, blockdec, total_s = rest[11:]
    g = pl.program_id(0)
    ends = bounds_of(pieces)
    first = meta[0] + block_of(chunk, g) * BLOCK
    hs = (h0, h1, h2, h3)

    @pl.when(g == 0)
    def _():
        row_quantities(
            chunk, ends, meta[0], hs, wdt, dt_bias, rate, spread, cum_o, dt_o, fs_o, same_s, te_s, blockdec
        )

    crosses = has_boundary(ends, first)

    def states(masked):
        window = load_window(hs, chunk, g)
        masks = same_s[g].T if masked else None
        taps = tap_rows(conv_x, conv_bc)
        wide = lax.dot_general(
            te_s[g], spread[...], (((0,), (0,)), ((), ())), preferred_element_type=f32
        )
        keep_rounded(sf, jnp.dot(window[: EDGE + BLOCK], w_f[...], preferred_element_type=f32))
        keep_rounded(sr, jnp.dot(window[EDGE:], w_r[...], preferred_element_type=f32))
        for stream, scratch, ref in ((0, sf, xb_f), (1, sr, xb_r)):
            scaled = []
            for tile in (0, 1):
                x = conv_tile(scratch, tile, taps[tile], stream == 1, masks)
                ref[:, tile * 128 : (tile + 1) * 128] = x
                at = stream * INNER + tile * 128
                scaled.append((x.astype(f32) * wide[:, at : at + 128]).astype(bf16))
            b = conv_tile(scratch, 2, taps[2], stream == 1, masks)
            ref[:, INNER:MIX] = b
            added[stream, g] = lax.dot_general(
                b, jnp.concatenate(scaled, axis=1), (((0,), (0,)), ((), ())), preferred_element_type=f32
            )

    pl.when(crosses)(lambda: states(True))
    pl.when(jnp.logical_not(crosses))(lambda: states(False))
    if chunk == 0:
        return

    @pl.when(g == HERE - 1)
    def _():
        sources = {block_of(0, k): (added_0, blockdec_0, k) for k in range(HERE)}
        sources.update({block_of(1, k): (added, blockdec, k) for k in range(HERE)})
        decays = []
        for stream in range(2):
            state = jnp.zeros((NSTATE, INNER), f32)
            decay = jnp.ones((1, INNER), f32)
            for step in range(BLOCKS):
                b = step if stream == 0 else BLOCKS - 1 - step
                start_o[stream, b] = state
                decay_o[stream, b] = jnp.broadcast_to(decay, (8, INNER))
                states_ref, decays_ref, k = sources[b]
                d = decays_ref[k, 0:1, stream * INNER : (stream + 1) * INNER]
                state = d * state + states_ref[stream, k]
                decay = decay * d
            total_s[stream] = state
            decays.append(decay)
        rows = split_rows(decays)
        for s, ref in enumerate((p0, p1, p2, p3)):
            at = pl.multiple_of(lax.rem(meta[1] + s, 4) * QUARTER, QUARTER)
            ref[0:QUARTER, :] = total_s[0, pl.ds(at, QUARTER), :].astype(bf16)
            ref[QUARTER : 2 * QUARTER, :] = total_s[1, pl.ds(at, QUARTER), :].astype(bf16)
            ref[2 * QUARTER : PAY, :] = rows


def local_states(chunk, pieces, meta, dt_bias, rate, hs, w_f, w_r, wdt, conv_x, conv_bc, spread, others=()):
    rows = HERE * BLOCK
    row = pl.BlockSpec((BLOCK, MIX), lambda g: (g, 0))
    fixed = [*hs, w_f, w_r, wdt, conv_x, conv_bc, spread, *others]
    added = jax.ShapeDtypeStruct((2, HERE, NSTATE, INNER), f32)
    blockdec = jax.ShapeDtypeStruct((HERE, 8, 2 * INNER), f32)
    shapes = [
        jax.ShapeDtypeStruct((rows, MIX), bf16),
        jax.ShapeDtypeStruct((rows, MIX), bf16),
        jax.ShapeDtypeStruct((8, rows), f32),
        jax.ShapeDtypeStruct((8, rows), f32),
        jax.ShapeDtypeStruct((8, rows), f32),
    ]
    scratch = [
        pltpu.VMEM((MIX // 128, EDGE + BLOCK, 128), f32),
        pltpu.VMEM((MIX // 128, EDGE + BLOCK, 128), f32),
        pltpu.VMEM((HERE, 8, BLOCK), f32),
        pltpu.VMEM((HERE, 16, BLOCK), bf16),
    ]
    if chunk == 0:
        shapes += [added, blockdec]
    else:
        shapes += [
            jax.ShapeDtypeStruct((2, BLOCKS, NSTATE, INNER), f32),
            jax.ShapeDtypeStruct((2, BLOCKS, 8, INNER), f32),
        ] + [jax.ShapeDtypeStruct((PAY, INNER), bf16)] * 4
        scratch += [pltpu.VMEM(a.shape, f32) for a in (added, blockdec)]
        scratch += [pltpu.VMEM((2, NSTATE, INNER), f32)]
    return pl.pallas_call(
        functools.partial(k1_body, chunk),
        grid=(HERE,),
        in_specs=[SMEM] * 4 + [whole(a.shape) for a in fixed],
        out_specs=[row, row] + [whole(s.shape) for s in shapes[2:]],
        out_shape=shapes,
        scratch_shapes=scratch,
        compiler_params=params(24),
        cost_estimate=cost(rows * 6e6, rows * 4000),
        name="local_states",
    )(pieces, meta, dt_bias, rate, *fixed)


def k2_body(
    chunk, base, n_alias, pieces, meta, skip_gain, h0, h1, h2, h3, w_f, w_r, conv_x, conv_bc,
    xb_f, xb_r, cum_i, dt_i, *rest,
):
    c_f, c_r, y_f, y_r, z_f, z_r, sf, sr, open_mask = rest[n_alias:]
    step = pl.program_id(0)
    g = step + base
    ends = bounds_of(pieces)
    first = meta[0] + block_of(chunk, g) * BLOCK
    row_at = lax.broadcasted_iota(jnp.int32, (BLOCK, BLOCK), 0)
    col_at = lax.broadcasted_iota(jnp.int32, (BLOCK, BLOCK), 1)
    half = BLOCK // 2

    @pl.when(step == 0)
    def _():
        open_mask[0] = jnp.where(row_at >= col_at, 0.0, FAR)
        open_mask[1] = jnp.where(row_at <= col_at, 0.0, FAR)

    crosses = has_boundary(ends, first)

    @pl.when(crosses)
    def _():
        seg = seg_rows(ends, first)
        together = seg.T[:, 3:4] == seg[3:4, :]
        open_mask[2] = jnp.where(together & (row_at >= col_at), 0.0, FAR)
        open_mask[3] = jnp.where(together & (row_at <= col_at), 0.0, FAR)

    def mix(masked):
        window = load_window((h0, h1, h2, h3), chunk, g)
        masks = None
        if masked:
            seg = seg_rows(ends, first)
            masks = (seg == seg[3:4, :]).astype(f32).T
        proj_f = jnp.dot(window[: EDGE + BLOCK], w_f[...], preferred_element_type=f32)
        proj_r = jnp.dot(window[EDGE:], w_r[...], preferred_element_type=f32)
        keep_rounded(sf, proj_f)
        keep_rounded(sr, proj_r)
        z_f[...] = silu(proj_f[EDGE:, NSTATE:].astype(bf16).astype(f32))
        z_r[...] = silu(proj_r[0:BLOCK, NSTATE:].astype(bf16).astype(f32))
        taps = tap_rows(conv_x, conv_bc)[3]
        cum = cum_i[...]
        cum_t = cum.T
        log_dt = jnp.log(dt_i[...]) - cum
        lane_head = lax.broadcasted_iota(jnp.int32, (BLOCK, INNER), 1) // HEAD_DIM
        skip = per_head(skip_gain, (1, INNER), 1, HEAD_DIM)
        for stream, xb, scratch, c_ref, y_ref in ((0, xb_f, sf, c_f, y_f), (1, xb_r, sr, c_r, y_r)):
            c_rows = conv_tile(scratch, 0, taps, stream == 1, masks)
            c_ref[...] = c_rows
            x = xb[:, 0:INNER]
            b = xb[:, INNER:MIX]
            heads = [jnp.where(lane_head == h, x, jnp.zeros_like(x)) for h in range(HEADS_HERE)]
            for part in range(2):
                rows = slice(part * half, (part + 1) * half)
                if stream == 0:
                    cols = slice(0, half) if part == 0 else slice(0, BLOCK)
                else:
                    cols = slice(0, BLOCK) if part == 0 else slice(half, BLOCK)
                scores = lax.dot_general(
                    c_rows[rows, :], b[cols, :], (((1,), (1,)), ((), ())), preferred_element_type=f32
                )
                mask = open_mask[(2 if masked else 0) + stream, rows, cols]
                total = x[rows, :].astype(f32) * skip
                for h in range(HEADS_HERE):
                    at = stream * HEADS_HERE + h
                    gap = (cum_t[rows, at : at + 1] + log_dt[at : at + 1, cols]) + mask
                    weight = (jnp.exp(gap) * scores).astype(bf16)
                    total = total + jnp.dot(weight, heads[h][cols, :], preferred_element_type=f32)
                y_ref[rows, :] = total

    pl.when(crosses)(lambda: mix(True))
    pl.when(jnp.logical_not(crosses))(lambda: mix(False))


def intra(chunk, part, n_parts, pieces, meta, skip_gain, hs, w_f, w_r, conv_x, conv_bc, xb_f, xb_r, cum, dt, before):
    rows = HERE * BLOCK
    here = HERE // n_parts
    base = part * here
    col = pl.BlockSpec((8, BLOCK), lambda g: (0, g + base))
    mixed = pl.BlockSpec((BLOCK, MIX), lambda g: (g + base, 0))
    c_out = pl.BlockSpec((BLOCK, NSTATE), lambda g: (g + base, 0))
    y_out = pl.BlockSpec((BLOCK, INNER), lambda g: (g + base, 0))
    fixed = [*hs, w_f, w_r, conv_x, conv_bc]
    before = list(before)
    n_in = 3 + len(fixed) + 4
    return pl.pallas_call(
        functools.partial(k2_body, chunk, base, len(before)),
        grid=(here,),
        in_specs=[SMEM] * 3 + [whole(a.shape) for a in fixed] + [mixed, mixed, col, col]
        + [pl.BlockSpec(memory_space=pl.ANY)] * len(before),
        out_specs=[c_out, c_out, y_out, y_out, y_out, y_out],
        out_shape=[jax.ShapeDtypeStruct((rows, NSTATE), bf16)] * 2
        + [jax.ShapeDtypeStruct((rows, INNER), f32)] * 4,
        input_output_aliases={n_in + k: k for k in range(len(before))},
        scratch_shapes=[
            pltpu.VMEM((1, EDGE + BLOCK, 128), f32),
            pltpu.VMEM((1, EDGE + BLOCK, 128), f32),
            pltpu.VMEM((4, BLOCK, BLOCK), f32),
        ],
        compiler_params=params(24),
        cost_estimate=cost(here * BLOCK * 5e6, here * BLOCK * 5000),
        name="intra",
    )(pieces, meta, skip_gain, *fixed, xb_f, xb_r, cum, dt, *before)


def state_rows(ref, stream):
    return ref[stream * QUARTER : (stream + 1) * QUARTER, :].astype(f32)


def put_payload(ref, states, decays):
    for stream in range(2):
        ref[stream * QUARTER : (stream + 1) * QUARTER, :] = states[stream].astype(bf16)
    ref[2 * QUARTER : PAY, :] = split_rows(decays)


def group_body(meta, own, r1, r2, r3, pre_s, pre_a, pay, stage):
    me = meta[1]
    for s, ref in enumerate((own, r1, r2, r3)):
        stage[lax.rem(me - s + 4, 4)] = ref[...]
    states, decays = [], []
    for stream in range(2):
        state = jnp.zeros((QUARTER, INNER), f32)
        decay = jnp.ones((1, INNER), f32)
        for step in range(4):
            k = step if stream == 0 else 3 - step
            pre_s[k, stream] = state
            pre_a[k, stream] = jnp.broadcast_to(decay, (8, INNER))
            one = stage[k]
            d = decays_of(one[2 * QUARTER :])[stream]
            state = d * state + one[stream * QUARTER : (stream + 1) * QUARTER].astype(f32)
            decay = decay * d
        states.append(state)
        decays.append(decay)
    put_payload(pay, states, decays)


def before_digit(place, stream, got):
    low_s, low_a = jnp.zeros((QUARTER, INNER), f32), jnp.ones((1, INNER), f32)
    for s in (1, 2, 3):
        there = s <= place
        state, decay = got[s if stream == 0 else 4 - s]
        low_s = jnp.where(there, low_s + low_a * state, low_s)
        low_a = jnp.where(there, low_a * decay, low_a)
    return low_s, low_a


def middle_body(meta, own, r1, r2, r3, low_o, low_ao, pay):
    digit = meta[2]
    states, decays = [], []
    rows = [decays_of(r[2 * QUARTER : PAY, :]) for r in (own, r1, r2, r3)]
    for stream in range(2):
        got = [(state_rows(r, stream), rows[s][stream]) for s, r in enumerate((own, r1, r2, r3))]
        place = digit if stream == 0 else 3 - digit
        low_s, low_a = before_digit(place, stream, got)
        low_o[stream] = low_s
        low_ao[stream] = jnp.broadcast_to(low_a, (8, INNER))
        total_s, total_a = got[0][1] * low_s + got[0][0], got[0][1] * low_a
        for s in (3, 2, 1):
            there = s > place
            state, decay = got[s if stream == 0 else 4 - s]
            total_s = jnp.where(there, decay * total_s + state, total_s)
            total_a = jnp.where(there, decay * total_a, total_a)
        states.append(total_s)
        decays.append(total_a)
    put_payload(pay, states, decays)


def top_body(meta, r1, r2, r3, low_i, low_ai, pre_s, pre_a, *outs):
    digit = meta[3]
    rows = [None] + [decays_of(r[2 * QUARTER : PAY, :]) for r in (r1, r2, r3)]
    for stream in range(2):
        got = [None] + [
            (state_rows(r, stream), rows[s + 1][stream]) for s, r in enumerate((r1, r2, r3))
        ]
        place = digit if stream == 0 else 3 - digit
        top_s, _ = before_digit(place, stream, got)
        group_s = low_ai[stream, 0:1, :] * top_s + low_i[stream]
        for s, ref in enumerate(outs):
            k = lax.rem(meta[1] + s, 4)
            member = pre_a[k, stream][0:1, :] * group_s + pre_s[k, stream]
            ref[stream * QUARTER : (stream + 1) * QUARTER, :] = member.astype(bf16)


def small_call(body, name, meta, arrays, shapes, scratch=()):
    return pl.pallas_call(
        body,
        grid=(1,),
        in_specs=[SMEM] + [whole(a.shape) for a in arrays],
        out_specs=[whole(s.shape) for s in shapes],
        out_shape=shapes,
        scratch_shapes=list(scratch),
        compiler_params=params(6),
        cost_estimate=cost(2e6, 1e6),
        name=name,
    )(meta, *arrays)


PAYLOAD = jax.ShapeDtypeStruct((PAY, INNER), bf16)


def join_group(meta, arrays):
    shapes = [
        jax.ShapeDtypeStruct((4, 2, QUARTER, INNER), f32),
        jax.ShapeDtypeStruct((4, 2, 8, INNER), f32),
        PAYLOAD,
    ]
    return small_call(group_body, "join_group", meta, arrays, shapes, [pltpu.VMEM((4, PAY, INNER), bf16)])


def join_middle(meta, arrays):
    shapes = [
        jax.ShapeDtypeStruct((2, QUARTER, INNER), f32),
        jax.ShapeDtypeStruct((2, 8, INNER), f32),
        PAYLOAD,
    ]
    return small_call(middle_body, "join_middle", meta, arrays, shapes)


def join_top(meta, arrays):
    shapes = [jax.ShapeDtypeStruct((2 * QUARTER, INNER), bf16)] * 4
    return small_call(top_body, "join_top", meta, arrays, shapes)


def k3_body(meta, c_f, c_r, y_f, y_r, z_f, z_r, fs, starts, decays, q0, q1, q2, q3, gain, spread, *rest):
    g_f, g_r, sums, s_in = rest[-4:]

    @pl.when(pl.program_id(0) == 0)
    def _():
        for s, ref in enumerate((q0, q1, q2, q3)):
            at = pl.multiple_of(lax.rem(meta[1] - s + 4, 4) * QUARTER, QUARTER)
            for stream in range(2):
                s_in[stream, pl.ds(at, QUARTER), :] = state_rows(ref, stream)

    wide = rows_to_cols(fs[...], spread[...])
    out = []
    for stream, c_ref, y_ref, z_ref, g_ref in ((0, c_f, y_f, z_f, g_f), (1, c_r, y_r, z_r, g_r)):
        state = starts[stream, 0] + decays[stream, 0, 0:1, :] * s_in[stream]
        carried = jnp.dot(c_ref[...], state.astype(bf16), preferred_element_type=f32)
        mixed = y_ref[...] + carried * wide[:, stream * INNER : (stream + 1) * INNER]
        gated = mixed * z_ref[...]
        square = gated * gated
        out.append(jnp.sum((square[:, 0:128] + square[:, 128:256]).T, axis=0, keepdims=True))
        g_ref[...] = (gated * gain[...]).astype(bf16)
    sums[...] = jnp.concatenate(out, axis=0)


def gate(chunk, meta, locals_, fs, starts, decays, quarters, gain, spread, before):
    base = chunk * HERE
    m = BLOCKS * BLOCK
    c_in = pl.BlockSpec((BLOCK, NSTATE), lambda g: (g, 0))
    y_in = pl.BlockSpec((BLOCK, INNER), lambda g: (g, 0))
    y_out = pl.BlockSpec((BLOCK, INNER), lambda g: (g + base, 0))
    fixed = [*quarters, gain, spread]
    before = list(before)
    n_in = 1 + 6 + 3 + len(fixed)
    return pl.pallas_call(
        k3_body,
        grid=(HERE,),
        in_specs=[SMEM, c_in, c_in, y_in, y_in, y_in, y_in,
                  pl.BlockSpec((8, BLOCK), lambda g: (0, g)),
                  pl.BlockSpec((2, 1, NSTATE, INNER), lambda g: (0, block_of(chunk, g), 0, 0)),
                  pl.BlockSpec((2, 1, 8, INNER), lambda g: (0, block_of(chunk, g), 0, 0))]
        + [whole(a.shape) for a in fixed] + [pl.BlockSpec(memory_space=pl.ANY)] * len(before),
        out_specs=[y_out, y_out, pl.BlockSpec((2, BLOCK), lambda g: (0, g + base))],
        out_shape=[
            jax.ShapeDtypeStruct((m, INNER), bf16),
            jax.ShapeDtypeStruct((m, INNER), bf16),
            jax.ShapeDtypeStruct((2, m), f32),
        ],
        input_output_aliases={n_in + k: k for k in range(len(before))},
        scratch_shapes=[pltpu.VMEM((2, NSTATE, INNER), f32)],
        compiler_params=params(16),
        cost_estimate=cost(m * 3e5, m * 3000),
        name="gate",
    )(meta, *locals_, fs, starts, decays, *fixed, *before)


def k4_body(g_f, g_r, s0, s1, s2, s3, w_f, w_r, spread, o0, o1, o2, o3):
    total = (s0[...] + s1[...]) + (s2[...] + s3[...])
    scale = lax.rsqrt(total / E + EPSILON)
    scale = jnp.concatenate([scale, jnp.zeros((6, BLOCK), f32)], axis=0)
    wide = rows_to_cols(scale, spread[...])
    out_f = jnp.dot(g_f[...], w_f[...], preferred_element_type=f32)
    out_r = jnp.dot(g_r[...], w_r[...], preferred_element_type=f32)
    for s, ref in enumerate((o0, o1, o2, o3)):
        cols = slice(s * 128, (s + 1) * 128)
        part = out_f[:, cols] * wide[:, 0:128] + out_r[:, cols] * wide[:, 128:256]
        ref[...] = part.astype(ref.dtype)


def project_out(half, kinds, g_f, g_r, sums, w_f, w_r, spread):
    m = HERE * BLOCK

    def at(g):
        return jnp.where(g < 2, g + 4, g - 2) if half == 0 else jnp.where(g < 2, g + 2, g + 4)

    g_in = pl.BlockSpec((BLOCK, INNER), lambda g: (at(g), 0))
    s_in = pl.BlockSpec((2, BLOCK), lambda g: (0, at(g)))
    o = pl.BlockSpec((BLOCK, 128), lambda g: (g, 0))
    return pl.pallas_call(
        k4_body,
        grid=(HERE,),
        in_specs=[g_in, g_in] + [s_in] * 4 + [whole(w_f.shape), whole(w_r.shape), whole(spread.shape)],
        out_specs=[o] * 4,
        out_shape=[jax.ShapeDtypeStruct((m, 128), kind) for kind in kinds],
        compiler_params=params(16),
        cost_estimate=cost(m * 1e6, m * 3000),
        name="project_out",
    )(g_f, g_r, *sums, w_f, w_r, spread)


def join_body(a1, b1, a2, b2, o1, o2):
    o1[...] = (a1[...] + b1[...].astype(f32)).astype(bf16)
    o2[...] = (a2[...] + b2[...].astype(f32)).astype(bf16)


def join_shares(a1, b1, a2, b2):
    arrays = (a1, b1, a2, b2)
    shapes = [jax.ShapeDtypeStruct(a1.shape, bf16)] * 2
    return pl.pallas_call(
        join_body,
        grid=(1,),
        in_specs=[whole(a.shape) for a in arrays],
        out_specs=[whole(a.shape) for a in shapes],
        out_shape=shapes,
        compiler_params=params(8),
        cost_estimate=cost(1e6, 3e6),
        name="join_shares",
    )(*arrays)


def last_body(a0, a1, a2, b0, b1, b2, out):
    for k, (own, one, other) in enumerate(((a0, a1, a2), (b0, b1, b2))):
        @pl.when(pl.program_id(0) == k)
        def _():
            out[...] = (own[...] + one[...].astype(f32) + other[...].astype(f32)).astype(bf16)


def last_sum(*arrays):
    m = HERE * BLOCK
    return pl.pallas_call(
        last_body,
        grid=(2,),
        in_specs=[whole(a.shape) for a in arrays],
        out_specs=pl.BlockSpec((m, 128), lambda g: (g, 0)),
        out_shape=jax.ShapeDtypeStruct((2 * m, 128), bf16),
        compiler_params=params(8),
        cost_estimate=cost(1e6, 3e6),
        name="last_sum",
    )(*arrays)


def orders(mp, n_mp, width):
    here = width // n_mp
    shape = (width, width)
    row = lax.broadcasted_iota(jnp.int32, shape, 0)
    col = lax.broadcasted_iota(jnp.int32, shape, 1)
    place = lax.rem(mp - row // here + n_mp, n_mp) * here + lax.rem(row, here)
    goal = lax.rem(mp + col // here, n_mp) * here + lax.rem(col, here)
    return [
        keep.astype(f32).astype(bf16)
        for keep in (place == col, width - 1 - place == col, goal == row, width - 1 - goal == row)
    ]


def prepare_1_body(n_mp, mp, w_x, w_bc, w_dt, o_f, o_r, o_dt):
    pick_f, pick_r, _, _ = orders(mp[0], n_mp, w_x.shape[0])
    w = jnp.concatenate([w_x[...], w_bc[:, 0:NSTATE]], axis=1)
    o_f[...] = jnp.dot(pick_f, w, preferred_element_type=f32).astype(bf16)
    o_r[...] = jnp.dot(pick_r, w, preferred_element_type=f32).astype(bf16)
    rows = [
        lax.dot_general(w_dt[...], pick, (((1,), (1,)), ((), ())), preferred_element_type=f32)
        for pick in (pick_f, pick_r)
    ]
    o_dt[...] = jnp.concatenate(rows, axis=0).astype(bf16)


def prepare_2_body(n_mp, mp, w_bc, w_z, w_out, o_f, o_r, p_f, p_r):
    pick_f, pick_r, out_f, out_r = orders(mp[0], n_mp, w_z.shape[0])
    w = jnp.concatenate([w_bc[:, NSTATE:], w_z[...]], axis=1)
    o_f[...] = jnp.dot(pick_f, w, preferred_element_type=f32).astype(bf16)
    o_r[...] = jnp.dot(pick_r, w, preferred_element_type=f32).astype(bf16)
    p_f[...] = jnp.dot(w_out[...], out_f, preferred_element_type=f32).astype(bf16)
    p_r[...] = jnp.dot(w_out[...], out_r, preferred_element_type=f32).astype(bf16)


def prepare(body, name, n_mp, mp, arrays, shapes):
    return pl.pallas_call(
        functools.partial(body, n_mp),
        grid=(1,),
        in_specs=[SMEM] + [whole(a.shape) for a in arrays],
        out_specs=[whole(a) for a in shapes],
        out_shape=[jax.ShapeDtypeStruct(a, bf16) for a in shapes],
        compiler_params=params(20),
        cost_estimate=cost(1e9, 3e6),
        name=name,
    )(mp, *arrays)


def row_spread():
    out = np.zeros((16, 256), np.float32)
    for part in range(2):
        out[part * 8, 0:128] = 1.0
        out[part * 8 + 1, 128:256] = 1.0
    return out


def around(array, axis, count, shift):
    return lax.ppermute(array, axis, [(i, (i + shift) % count) for i in range(count)])


def digit_perm(count, stride, shift):
    pairs = []
    for i in range(count):
        d = (i // stride) % 4
        pairs.append((i, i + (((d + shift) % 4) - d) * stride))
    return pairs


INTRA_PARTS = 2


def shards(
    hidden, w_x, w_z, w_bc, w_dt, conv_x, conv_bc, dt_bias, decay_rate, skip_gain, norm_gain, w_out,
    piece_lengths,
):
    rows = hidden.shape[0]
    ctx, mp = lax.axis_index("ctx"), lax.axis_index("mp")
    n_ctx, n_mp = lax.axis_size("ctx"), lax.axis_size("mp")

    run = rows // 4
    middle = hidden[run - EDGE : 3 * run + EDGE]
    hs_0 = [middle] + [around(middle, "mp", n_mp, s) for s in range(1, n_mp)]
    low = lax.ppermute(hidden[rows - EDGE :], "ctx", [(i, i + 1) for i in range(n_ctx - 1)])
    high = lax.ppermute(hidden[:EDGE], "ctx", [(i + 1, i) for i in range(n_ctx - 1)])
    outer = jnp.concatenate([low, hidden[: run + EDGE], hidden[3 * run - EDGE :], high], axis=0)

    width = w_x.shape[0]
    place, outer = lax.optimization_barrier((mp[None].astype(jnp.int32), outer))
    hs_1 = [outer] + [around(outer, "mp", n_mp, s) for s in range(1, n_mp)]
    w_1f, w_1r, wdt = prepare(
        prepare_1_body, "prepare_1", n_mp, place, (w_x, w_bc, w_dt.T),
        [(width, MIX), (width, MIX), (8, width)],
    )
    w_2f, w_2r, w_of, w_or = prepare(
        prepare_2_body, "prepare_2", n_mp, place, (w_bc, w_z, w_out),
        [(width, MIX), (width, MIX), w_out.shape, w_out.shape],
    )

    gain = norm_gain[None, :]
    spread = jnp.asarray(head_spread(), bf16)
    spread_rows = jnp.asarray(row_spread(), bf16)
    meta = jnp.stack([ctx * rows, ctx % 4, (ctx // 4) % 4, (ctx // 16) % 4]).astype(jnp.int32)

    first = (piece_lengths, meta, dt_bias, decay_rate)
    weights_1 = (w_1f, w_1r, wdt, conv_x, conv_bc, spread)
    weights_2 = (w_2f, w_2r, conv_x, conv_bc)

    xb_f, xb_r, cum, dt, fs_0, *middle_states = local_states(0, *first, hs_0, *weights_1)
    arguments = [(piece_lengths, meta, skip_gain, hs_0, *weights_2, xb_f, xb_r, cum, dt)]
    done = [(), ()]

    def beside(chunk, part, received):
        new = intra(chunk, part, INTRA_PARTS, *arguments[chunk], done[chunk])
        received, new = lax.optimization_barrier((received, tuple(new)))
        done[chunk] = new
        return received

    hs_1 = beside(0, 0, tuple(hs_1))
    xb_f, xb_r, cum, dt, fs_1, starts, decays, *pays = local_states(
        1, *first, hs_1, *weights_1, middle_states
    )
    arguments.append((piece_lengths, meta, skip_gain, hs_1, *weights_2, xb_f, xb_r, cum, dt))

    def moved(arrays, stride):
        return [lax.ppermute(a, "ctx", digit_perm(n_ctx, stride, s)) for s, a in zip((1, 2, 3), arrays)]

    pre_s, pre_a, pay = join_group(meta, [pays[0]] + beside(0, 1, moved(pays[1:], 1)))
    low_s, low_a, top = join_middle(meta, [pay] + beside(1, 0, moved([pay] * 3, 4)))
    back = join_top(meta, beside(1, 1, moved([top] * 3, 16)) + [low_s, low_a, pre_s, pre_a])
    quarters = [back[0]] + moved(back[1:], 1)

    gated = gate(0, meta, done[0], fs_0, starts, decays, quarters, gain, spread, ())
    g_f, g_r, sums = gate(1, meta, done[1], fs_1, starts, decays, quarters, gain, spread, gated)
    all_sums = [sums] + [around(sums, "mp", n_mp, s) for s in range(1, n_mp)]
    tail = (g_f, g_r, all_sums, w_of, w_or, spread_rows)
    own_a, up_a, far_a, down_a = project_out(0, (f32, f32, bf16, bf16), *tail)
    far_a = around(far_a, "mp", n_mp, 1)
    own_b, up_b, far_b, down_b = project_out(1, (f32, bf16, bf16, f32), *tail)
    far_b = around(far_b, "mp", n_mp, n_mp - 1)
    down_a, up_b = around(down_a, "mp", n_mp, n_mp - 1), around(up_b, "mp", n_mp, 1)
    up_a, down_b = join_shares(up_a, far_a, down_b, far_b)
    up_a, down_b = around(up_a, "mp", n_mp, 1), around(down_b, "mp", n_mp, n_mp - 1)
    return last_sum(own_a, down_a, up_a, own_b, up_b, down_b)


def solution(mesh):
    return jax.shard_map(
        shards,
        mesh=mesh,
        in_specs=(
            P("ctx", "mp"),
            P(None, "mp"),
            P(None, "mp"),
            P(),
            P(None, "mp"),
            P(None, "mp"),
            P(),
            P("mp"),
            P("mp"),
            P("mp"),
            P("mp"),
            P("mp", None),
            P(),
        ),
        out_specs=P("ctx", "mp"),
        check_vma=False,
    )
```

```python
import functools

import jax
import jax.numpy as jnp
import numpy as np
from jax import lax
from jax.experimental import pallas as pl
from jax.experimental.pallas import tpu as pltpu
from jax.sharding import PartitionSpec as P

E = 1024
HEAD_DIM = 64
NSTATE = 128
BLOCK = 256
HEADS_HERE = 4
INNER = HEADS_HERE * HEAD_DIM
PIECES = 16
EPSILON = 1e-05
FAR = -1e30
EDGE = 16
MIX = INNER + NSTATE
QUARTER = NSTATE // 4
RUN = (4, 2)
HERE = 4
BLOCKS = 2 * HERE
PAY = 2 * QUARTER + 16

bf16 = jnp.bfloat16
f32 = jnp.float32


def head_spread():
    out = np.zeros((16, 2 * INNER), np.float32)
    for part in range(2):
        for stream in range(2):
            for h in range(HEADS_HERE):
                first = stream * INNER + h * HEAD_DIM
                out[part * 8 + stream * 4 + h, first : first + HEAD_DIM] = 1.0
    return out


def whole(shape):
    return pl.BlockSpec(shape, lambda *_: (0,) * len(shape))


SMEM = pl.BlockSpec(memory_space=pltpu.SMEM)
VMEM = pl.BlockSpec(memory_space=pltpu.VMEM)


def rows_at(g):
    return pl.ds(pl.multiple_of(g * BLOCK, BLOCK), BLOCK)


def params(mib):
    return pltpu.CompilerParams(vmem_limit_bytes=mib * 1024 * 1024)


def cost(flops, nbytes):
    return pl.CostEstimate(flops=int(flops), bytes_accessed=int(nbytes), transcendentals=0)


def bounds_of(pieces_ref):
    total = pieces_ref[0]
    ends = [total]
    for k in range(1, PIECES):
        total = total + pieces_ref[k]
        ends.append(total)
    return ends


def seg_rows(ends, first):
    shape = (8, BLOCK)
    pos = (
        first - 3 + lax.broadcasted_iota(jnp.int32, shape, 0)
        + lax.broadcasted_iota(jnp.int32, shape, 1)
    )
    seg = jnp.zeros(shape, jnp.int32)
    for end in ends:
        seg = seg + (pos >= end).astype(jnp.int32)
    return seg.astype(f32)


def has_boundary(ends, first):
    found = jnp.int32(0)
    for end in ends:
        found = found + ((end > first - 3) & (end <= first + BLOCK + 2)).astype(jnp.int32)
    return found > 0


def split2(rows):
    high = rows.astype(bf16)
    return jnp.concatenate([high, (rows - high.astype(f32)).astype(bf16)], axis=0)


def rows_to_cols(rows, spread):
    return lax.dot_general(
        split2(rows), spread, (((0,), (0,)), ((), ())), preferred_element_type=f32
    )


def row_of(chunk, g):
    return EDGE + g * BLOCK + (g // RUN[chunk]) * 2 * EDGE


def block_of(chunk, g):
    return g + 2 if chunk == 0 else g + 4 * (g // 2)


def load_window(hs, chunk, g):
    at = pl.multiple_of(row_of(chunk, g) - EDGE, EDGE)
    return jnp.concatenate([h[pl.ds(at, BLOCK + 2 * EDGE), :] for h in hs], axis=1)


def silu(v):
    half = 0.5 * v
    return half + half * jnp.tanh(half)


def tap_rows(conv_x, conv_bc):
    return [conv_x[:, 0:128], conv_x[:, 128:256], conv_bc[:, 0:128], conv_bc[:, 128:256]]


def conv_tile(scratch, tile, taps, reverse, masks):
    total = None
    for back in range(4):
        first = back if reverse else EDGE - back
        term = scratch[tile, pl.ds(first, BLOCK), :] * taps[3 - back : 4 - back, :]
        if masks is not None and back:
            row = 3 + back if reverse else 3 - back
            term = term * masks[:, row : row + 1]
        total = term if total is None else total + term
    return silu(total).astype(bf16)


def keep_rounded(scratch, proj):
    for tile in range(scratch.shape[0]):
        scratch[tile] = proj[:, tile * 128 : (tile + 1) * 128].astype(bf16).astype(f32)


def per_head(scalars, shape, axis, width):
    head = lax.broadcasted_iota(jnp.int32, shape, axis) // width % HEADS_HERE
    out = jnp.full(shape, scalars[0], f32)
    for h in range(1, HEADS_HERE):
        out = jnp.where(head == h, scalars[h], out)
    return out


def split_rows(decays):
    at = lax.broadcasted_iota(jnp.int32, (16, INNER), 0)
    out = jnp.zeros((16, INNER), f32)
    for k, decay in enumerate(decays):
        high = decay.astype(bf16).astype(f32)
        out = jnp.where(at == 2 * k, high, jnp.where(at == 2 * k + 1, decay - high, out))
    return out.astype(bf16)


def decays_of(rows):
    wide = rows.astype(f32)
    return [wide[2 * k : 2 * k + 1, :] + wide[2 * k + 1 : 2 * k + 2, :] for k in range(2)]


def row_quantities(
    chunk, ends, origin, hs, wdt, dt_bias, rate, spread, cum_o, dt_o, fs_o, same_s, te_s, blockdec
):
    raw = []
    for b in range(HERE):
        at = row_of(chunk, b)
        block = jnp.concatenate([h[at : at + BLOCK, :] for h in hs], axis=1)
        raw.append(
            lax.dot_general(wdt[...], block, (((1,), (1,)), ((), ())), preferred_element_type=f32)
        )
    shape = (8 * HERE, BLOCK)
    v = jnp.concatenate(raw, axis=0).astype(bf16).astype(f32) + per_head(dt_bias, shape, 0, 1)
    dt = jnp.maximum(v, 0.0) + jnp.log1p(jnp.exp(-jnp.abs(v)))
    logd = -dt * per_head(rate, shape, 0, 1)
    high = logd.astype(bf16)
    rest = logd - high.astype(f32)
    middle = rest.astype(bf16)
    low = (rest - middle.astype(f32)).astype(bf16)
    row_at = lax.broadcasted_iota(jnp.int32, (BLOCK, BLOCK), 0)
    col_at = lax.broadcasted_iota(jnp.int32, (BLOCK, BLOCK), 1)
    summed = []
    for keep in (row_at <= col_at, row_at >= col_at):
        ones = keep.astype(f32).astype(bf16)
        summed.append(sum(jnp.dot(p, ones, preferred_element_type=f32) for p in (low, middle, high)))
    forward = lax.broadcasted_iota(jnp.int32, (8, BLOCK), 0) < HEADS_HERE
    spread_f = spread[0:8, :].astype(f32)
    for b in range(HERE):
        rows = slice(b * 8, (b + 1) * 8)
        cols = slice(b * BLOCK, (b + 1) * BLOCK)
        cum = jnp.where(forward, summed[0][rows], summed[1][rows])
        dt_b = dt[rows]
        seg = seg_rows(ends, origin + block_of(chunk, b) * BLOCK)
        same_s[b] = (seg == seg[3:4, :]).astype(f32)
        own = jnp.broadcast_to(seg[3:4, :], (8, BLOCK))
        seg_end = jnp.where(forward, seg[3:4, BLOCK - 1 : BLOCK], seg[3:4, 0:1])
        seg_in = jnp.where(forward, seg[2:3, 0:1], seg[4:5, BLOCK - 1 : BLOCK])
        total = jnp.where(forward, cum[:, BLOCK - 1 : BLOCK], cum[:, 0:1])
        to_end = jnp.exp(total - cum) * (own == seg_end).astype(f32) * dt_b
        block_decay = jnp.exp(total) * (seg_end == seg_in).astype(f32)
        cum_o[:, cols] = cum
        dt_o[:, cols] = dt_b
        fs_o[:, cols] = jnp.exp(cum) * (own == seg_in).astype(f32)
        te_s[b] = split2(to_end)
        decay_row = jnp.sum(
            jnp.concatenate([block_decay, block_decay], axis=1) * spread_f, axis=0, keepdims=True
        )
        blockdec[b] = jnp.broadcast_to(decay_row, (8, 2 * INNER))


def k1_body(chunk, pieces, meta, dt_bias, rate, h0, h1, h2, h3, w_f, w_r, wdt, conv_x, conv_bc, spread, *rest):
    if chunk == 0:
        xb_f, xb_r, cum_o, dt_o, fs_o, added, blockdec, sf, sr, same_s, te_s = rest
    else:
        added_0, blockdec_0, *rest = rest
        xb_f, xb_r, cum_o, dt_o, fs_o, start_o, decay_o, p0, p1, p2, p3 = rest[:11]
        sf, sr, same_s, te_s, added, blockdec, total_s = rest[11:]
    ends = bounds_of(pieces)
    hs = (h0, h1, h2, h3)
    row_quantities(
        chunk, ends, meta[0], hs, wdt, dt_bias, rate, spread, cum_o, dt_o, fs_o, same_s, te_s, blockdec
    )

    def states(g, masked):
        window = load_window(hs, chunk, g)
        masks = same_s[g].T if masked else None
        taps = tap_rows(conv_x, conv_bc)
        wide = lax.dot_general(
            te_s[g], spread[...], (((0,), (0,)), ((), ())), preferred_element_type=f32
        )
        keep_rounded(sf, jnp.dot(window[: EDGE + BLOCK], w_f[...], preferred_element_type=f32))
        keep_rounded(sr, jnp.dot(window[EDGE:], w_r[...], preferred_element_type=f32))
        rows = rows_at(g)
        for stream, scratch, ref in ((0, sf, xb_f), (1, sr, xb_r)):
            scaled = []
            for tile in (0, 1):
                x = conv_tile(scratch, tile, taps[tile], stream == 1, masks)
                ref[rows, tile * 128 : (tile + 1) * 128] = x
                at = stream * INNER + tile * 128
                scaled.append((x.astype(f32) * wide[:, at : at + 128]).astype(bf16))
            b = conv_tile(scratch, 2, taps[2], stream == 1, masks)
            ref[rows, INNER:MIX] = b
            added[stream, g] = lax.dot_general(
                b, jnp.concatenate(scaled, axis=1), (((0,), (0,)), ((), ())), preferred_element_type=f32
            )

    @pl.loop(0, HERE)
    def _(g):
        crosses = has_boundary(ends, meta[0] + block_of(chunk, g) * BLOCK)
        pl.when(crosses)(lambda: states(g, True))
        pl.when(jnp.logical_not(crosses))(lambda: states(g, False))

    if chunk == 0:
        return
    sources = {block_of(0, k): (added_0, blockdec_0, k) for k in range(HERE)}
    sources.update({block_of(1, k): (added, blockdec, k) for k in range(HERE)})
    decays = []
    for stream in range(2):
        state = jnp.zeros((NSTATE, INNER), f32)
        decay = jnp.ones((1, INNER), f32)
        for step in range(BLOCKS):
            b = step if stream == 0 else BLOCKS - 1 - step
            start_o[stream, b] = state
            decay_o[stream, b] = jnp.broadcast_to(decay, (8, INNER))
            states_ref, decays_ref, k = sources[b]
            d = decays_ref[k, 0:1, stream * INNER : (stream + 1) * INNER]
            state = d * state + states_ref[stream, k]
            decay = decay * d
        total_s[stream] = state
        decays.append(decay)
    rows = split_rows(decays)
    for s, ref in enumerate((p0, p1, p2, p3)):
        at = pl.multiple_of(lax.rem(meta[1] + s, 4) * QUARTER, QUARTER)
        ref[0:QUARTER, :] = total_s[0, pl.ds(at, QUARTER), :].astype(bf16)
        ref[QUARTER : 2 * QUARTER, :] = total_s[1, pl.ds(at, QUARTER), :].astype(bf16)
        ref[2 * QUARTER : PAY, :] = rows


def local_states(chunk, pieces, meta, dt_bias, rate, hs, w_f, w_r, wdt, conv_x, conv_bc, spread, others=()):
    rows = HERE * BLOCK
    fixed = [*hs, w_f, w_r, wdt, conv_x, conv_bc, spread, *others]
    added = jax.ShapeDtypeStruct((2, HERE, NSTATE, INNER), f32)
    blockdec = jax.ShapeDtypeStruct((HERE, 8, 2 * INNER), f32)
    shapes = [
        jax.ShapeDtypeStruct((rows, MIX), bf16),
        jax.ShapeDtypeStruct((rows, MIX), bf16),
        jax.ShapeDtypeStruct((8, rows), f32),
        jax.ShapeDtypeStruct((8, rows), f32),
        jax.ShapeDtypeStruct((8, rows), f32),
    ]
    scratch = [
        pltpu.VMEM((MIX // 128, EDGE + BLOCK, 128), f32),
        pltpu.VMEM((MIX // 128, EDGE + BLOCK, 128), f32),
        pltpu.VMEM((HERE, 8, BLOCK), f32),
        pltpu.VMEM((HERE, 16, BLOCK), bf16),
    ]
    if chunk == 0:
        shapes += [added, blockdec]
    else:
        shapes += [
            jax.ShapeDtypeStruct((2, BLOCKS, NSTATE, INNER), f32),
            jax.ShapeDtypeStruct((2, BLOCKS, 8, INNER), f32),
        ] + [jax.ShapeDtypeStruct((PAY, INNER), bf16)] * 4
        scratch += [pltpu.VMEM(a.shape, f32) for a in (added, blockdec)]
        scratch += [pltpu.VMEM((2, NSTATE, INNER), f32)]
    return pl.pallas_call(
        functools.partial(k1_body, chunk),
        in_specs=[SMEM] * 4 + [VMEM] * len(fixed),
        out_specs=[VMEM] * len(shapes),
        out_shape=shapes,
        scratch_shapes=scratch,
        compiler_params=params(24),
        cost_estimate=cost(rows * 6e6, rows * 4000),
        name="local_states",
    )(pieces, meta, dt_bias, rate, *fixed)


def k2_body(
    chunk, base, count, pieces, meta, skip_gain, h0, h1, h2, h3, w_f, w_r, conv_x, conv_bc,
    xb_f, xb_r, cum_i, dt_i, c_f, c_r, y_f, y_r, z_f, z_r, sf, sr, open_mask,
):
    ends = bounds_of(pieces)
    row_at = lax.broadcasted_iota(jnp.int32, (BLOCK, BLOCK), 0)
    col_at = lax.broadcasted_iota(jnp.int32, (BLOCK, BLOCK), 1)
    half = BLOCK // 2

    open_mask[0] = jnp.where(row_at >= col_at, 0.0, FAR)
    open_mask[1] = jnp.where(row_at <= col_at, 0.0, FAR)

    def mix(step, masked):
        g = step + base
        first = meta[0] + block_of(chunk, g) * BLOCK
        here, there = rows_at(step), rows_at(g)
        window = load_window((h0, h1, h2, h3), chunk, g)
        masks = None
        if masked:
            seg = seg_rows(ends, first)
            masks = (seg == seg[3:4, :]).astype(f32).T
            together = seg.T[:, 3:4] == seg[3:4, :]
            open_mask[2] = jnp.where(together & (row_at >= col_at), 0.0, FAR)
            open_mask[3] = jnp.where(together & (row_at <= col_at), 0.0, FAR)
        proj_f = jnp.dot(window[: EDGE + BLOCK], w_f[...], preferred_element_type=f32)
        proj_r = jnp.dot(window[EDGE:], w_r[...], preferred_element_type=f32)
        keep_rounded(sf, proj_f)
        keep_rounded(sr, proj_r)
        z_f[here, :] = silu(proj_f[EDGE:, NSTATE:].astype(bf16).astype(f32))
        z_r[here, :] = silu(proj_r[0:BLOCK, NSTATE:].astype(bf16).astype(f32))
        taps = tap_rows(conv_x, conv_bc)[3]
        cum = cum_i[:, there]
        cum_t = cum.T
        log_dt = jnp.log(dt_i[:, there]) - cum
        lane_head = lax.broadcasted_iota(jnp.int32, (BLOCK, INNER), 1) // HEAD_DIM
        skip = per_head(skip_gain, (1, INNER), 1, HEAD_DIM)
        for stream, xb, scratch, c_ref, y_ref in ((0, xb_f, sf, c_f, y_f), (1, xb_r, sr, c_r, y_r)):
            c_rows = conv_tile(scratch, 0, taps, stream == 1, masks)
            c_ref[here, :] = c_rows
            x = xb[there, 0:INNER]
            b = xb[there, INNER:MIX]
            heads = [jnp.where(lane_head == h, x, jnp.zeros_like(x)) for h in range(HEADS_HERE)]
            for part in range(2):
                rows = slice(part * half, (part + 1) * half)
                if stream == 0:
                    cols = slice(0, half) if part == 0 else slice(0, BLOCK)
                else:
                    cols = slice(0, BLOCK) if part == 0 else slice(half, BLOCK)
                scores = lax.dot_general(
                    c_rows[rows, :], b[cols, :], (((1,), (1,)), ((), ())), preferred_element_type=f32
                )
                mask = open_mask[(2 if masked else 0) + stream, rows, cols]
                total = x[rows, :].astype(f32) * skip
                for h in range(HEADS_HERE):
                    at = stream * HEADS_HERE + h
                    gap = (cum_t[rows, at : at + 1] + log_dt[at : at + 1, cols]) + mask
                    weight = (jnp.exp(gap) * scores).astype(bf16)
                    total = total + jnp.dot(weight, heads[h][cols, :], preferred_element_type=f32)
                at = pl.multiple_of(step * BLOCK + part * half, half)
                y_ref[pl.ds(at, half), :] = total

    @pl.loop(0, count)
    def _(step):
        crosses = has_boundary(ends, meta[0] + block_of(chunk, step + base) * BLOCK)
        pl.when(crosses)(lambda: mix(step, True))
        pl.when(jnp.logical_not(crosses))(lambda: mix(step, False))


def intra(chunk, part, n_parts, pieces, meta, skip_gain, hs, w_f, w_r, conv_x, conv_bc, xb_f, xb_r, cum, dt):
    count = HERE // n_parts
    rows = count * BLOCK
    arrays = [*hs, w_f, w_r, conv_x, conv_bc, xb_f, xb_r, cum, dt]
    return pl.pallas_call(
        functools.partial(k2_body, chunk, part * count, count),
        in_specs=[SMEM] * 3 + [VMEM] * len(arrays),
        out_specs=[VMEM] * 6,
        out_shape=[jax.ShapeDtypeStruct((rows, NSTATE), bf16)] * 2
        + [jax.ShapeDtypeStruct((rows, INNER), f32)] * 4,
        scratch_shapes=[
            pltpu.VMEM((1, EDGE + BLOCK, 128), f32),
            pltpu.VMEM((1, EDGE + BLOCK, 128), f32),
            pltpu.VMEM((4, BLOCK, BLOCK), f32),
        ],
        compiler_params=params(16),
        cost_estimate=cost(rows * 5e6, rows * 5000),
        name="intra",
    )(pieces, meta, skip_gain, *arrays)


def state_rows(ref, stream):
    return ref[stream * QUARTER : (stream + 1) * QUARTER, :].astype(f32)


def put_payload(ref, states, decays):
    for stream in range(2):
        ref[stream * QUARTER : (stream + 1) * QUARTER, :] = states[stream].astype(bf16)
    ref[2 * QUARTER : PAY, :] = split_rows(decays)


def group_body(meta, own, r1, r2, r3, pre_s, pre_a, pay, stage):
    me = meta[1]
    for s, ref in enumerate((own, r1, r2, r3)):
        stage[lax.rem(me - s + 4, 4)] = ref[...]
    states, decays = [], []
    for stream in range(2):
        state = jnp.zeros((QUARTER, INNER), f32)
        decay = jnp.ones((1, INNER), f32)
        for step in range(4):
            k = step if stream == 0 else 3 - step
            pre_s[k, stream] = state
            pre_a[k, stream] = jnp.broadcast_to(decay, (8, INNER))
            one = stage[k]
            d = decays_of(one[2 * QUARTER :])[stream]
            state = d * state + one[stream * QUARTER : (stream + 1) * QUARTER].astype(f32)
            decay = decay * d
        states.append(state)
        decays.append(decay)
    put_payload(pay, states, decays)


def before_digit(place, stream, got):
    low_s, low_a = jnp.zeros((QUARTER, INNER), f32), jnp.ones((1, INNER), f32)
    for s in (1, 2, 3):
        there = s <= place
        state, decay = got[s if stream == 0 else 4 - s]
        low_s = jnp.where(there, low_s + low_a * state, low_s)
        low_a = jnp.where(there, low_a * decay, low_a)
    return low_s, low_a


def middle_body(meta, own, r1, r2, r3, low_o, low_ao, pay):
    digit = meta[2]
    states, decays = [], []
    rows = [decays_of(r[2 * QUARTER : PAY, :]) for r in (own, r1, r2, r3)]
    for stream in range(2):
        got = [(state_rows(r, stream), rows[s][stream]) for s, r in enumerate((own, r1, r2, r3))]
        place = digit if stream == 0 else 3 - digit
        low_s, low_a = before_digit(place, stream, got)
        low_o[stream] = low_s
        low_ao[stream] = jnp.broadcast_to(low_a, (8, INNER))
        total_s, total_a = got[0][1] * low_s + got[0][0], got[0][1] * low_a
        for s in (3, 2, 1):
            there = s > place
            state, decay = got[s if stream == 0 else 4 - s]
            total_s = jnp.where(there, decay * total_s + state, total_s)
            total_a = jnp.where(there, decay * total_a, total_a)
        states.append(total_s)
        decays.append(total_a)
    put_payload(pay, states, decays)


def top_body(meta, r1, r2, r3, low_i, low_ai, pre_s, pre_a, *outs):
    digit = meta[3]
    rows = [None] + [decays_of(r[2 * QUARTER : PAY, :]) for r in (r1, r2, r3)]
    for stream in range(2):
        got = [None] + [
            (state_rows(r, stream), rows[s + 1][stream]) for s, r in enumerate((r1, r2, r3))
        ]
        place = digit if stream == 0 else 3 - digit
        top_s, _ = before_digit(place, stream, got)
        group_s = low_ai[stream, 0:1, :] * top_s + low_i[stream]
        for s, ref in enumerate(outs):
            k = lax.rem(meta[1] + s, 4)
            member = pre_a[k, stream][0:1, :] * group_s + pre_s[k, stream]
            ref[stream * QUARTER : (stream + 1) * QUARTER, :] = member.astype(bf16)


def small_call(body, name, meta, arrays, shapes, scratch=()):
    return pl.pallas_call(
        body,
        in_specs=[SMEM] + [VMEM] * len(arrays),
        out_specs=[VMEM] * len(shapes),
        out_shape=shapes,
        scratch_shapes=list(scratch),
        compiler_params=params(6),
        cost_estimate=cost(2e6, 1e6),
        name=name,
    )(meta, *arrays)


PAYLOAD = jax.ShapeDtypeStruct((PAY, INNER), bf16)


def join_group(meta, arrays):
    shapes = [
        jax.ShapeDtypeStruct((4, 2, QUARTER, INNER), f32),
        jax.ShapeDtypeStruct((4, 2, 8, INNER), f32),
        PAYLOAD,
    ]
    return small_call(group_body, "join_group", meta, arrays, shapes, [pltpu.VMEM((4, PAY, INNER), bf16)])


def join_middle(meta, arrays):
    shapes = [
        jax.ShapeDtypeStruct((2, QUARTER, INNER), f32),
        jax.ShapeDtypeStruct((2, 8, INNER), f32),
        PAYLOAD,
    ]
    return small_call(middle_body, "join_middle", meta, arrays, shapes)


def join_top(meta, arrays):
    shapes = [jax.ShapeDtypeStruct((2 * QUARTER, INNER), bf16)] * 4
    return small_call(top_body, "join_top", meta, arrays, shapes)


def k3_body(meta, *refs):
    parts, refs = refs[:24], refs[24:]
    fs, (starts, decays, q0, q1, q2, q3, gain, spread, g_f, g_r, sums, s_in) = refs[:2], refs[2:]
    for s, ref in enumerate((q0, q1, q2, q3)):
        at = pl.multiple_of(lax.rem(meta[1] - s + 4, 4) * QUARTER, QUARTER)
        for stream in range(2):
            s_in[stream, pl.ds(at, QUARTER), :] = state_rows(ref, stream)
    for chunk in range(2):
        for k in range(HERE):
            b = block_of(chunk, k)
            to = slice(b * BLOCK, (b + 1) * BLOCK)
            part, at = divmod(k, HERE // INTRA_PARTS)
            rows = slice(at * BLOCK, (at + 1) * BLOCK)
            first = 6 * (chunk * INTRA_PARTS + part)
            c, y, z = (parts[first + n : first + n + 2] for n in (0, 2, 4))
            wide = rows_to_cols(fs[chunk][:, k * BLOCK : (k + 1) * BLOCK], spread[...])
            for stream, g_ref in ((0, g_f), (1, g_r)):
                state = starts[stream, b] + decays[stream, b, 0:1, :] * s_in[stream]
                carried = jnp.dot(c[stream][rows, :], state.astype(bf16), preferred_element_type=f32)
                mixed = y[stream][rows, :] + carried * wide[:, stream * INNER : (stream + 1) * INNER]
                gated = mixed * z[stream][rows, :]
                square = gated * gated
                sums[stream : stream + 1, to] = jnp.sum(
                    (square[:, 0:128] + square[:, 128:256]).T, axis=0, keepdims=True
                )
                g_ref[to, :] = (gated * gain[...]).astype(bf16)


def gate(meta, locals_, fs, starts, decays, quarters, gain, spread):
    m = BLOCKS * BLOCK
    arrays = [*locals_, *fs, starts, decays, *quarters, gain, spread]
    return pl.pallas_call(
        k3_body,
        in_specs=[SMEM] + [VMEM] * len(arrays),
        out_specs=[VMEM] * 3,
        out_shape=[
            jax.ShapeDtypeStruct((m, INNER), bf16),
            jax.ShapeDtypeStruct((m, INNER), bf16),
            jax.ShapeDtypeStruct((2, m), f32),
        ],
        scratch_shapes=[pltpu.VMEM((2, NSTATE, INNER), f32)],
        compiler_params=params(12),
        cost_estimate=cost(m * 5e5, m * 6000),
        name="gate",
    )(meta, *arrays)


def k4_body(half, g_f, g_r, s0, s1, s2, s3, w_f, w_r, spread, o0, o1, o2, o3):
    for k in range(HERE):
        rows = slice((half * HERE + k) * BLOCK, (half * HERE + k + 1) * BLOCK)
        total = (s0[:, rows] + s1[:, rows]) + (s2[:, rows] + s3[:, rows])
        scale = lax.rsqrt(total / E + EPSILON)
        scale = jnp.concatenate([scale, jnp.zeros((6, BLOCK), f32)], axis=0)
        wide = rows_to_cols(scale, spread[...])
        out_f = jnp.dot(g_f[rows, :], w_f[...], preferred_element_type=f32)
        out_r = jnp.dot(g_r[rows, :], w_r[...], preferred_element_type=f32)
        for s, ref in enumerate((o0, o1, o2, o3)):
            cols = slice(s * 128, (s + 1) * 128)
            part = out_f[:, cols] * wide[:, 0:128] + out_r[:, cols] * wide[:, 128:256]
            ref[k * BLOCK : (k + 1) * BLOCK, :] = part.astype(ref.dtype)


def project_out(half, kinds, g_f, g_r, sums, w_f, w_r, spread):
    m = HERE * BLOCK
    arrays = [g_f, g_r, *sums, w_f, w_r, spread]
    return pl.pallas_call(
        functools.partial(k4_body, half),
        in_specs=[VMEM] * len(arrays),
        out_specs=[VMEM] * 4,
        out_shape=[jax.ShapeDtypeStruct((m, 128), kind) for kind in kinds],
        compiler_params=params(12),
        cost_estimate=cost(m * 1e6, m * 3000),
        name="project_out",
    )(*arrays)


def join_body(a1, b1, a2, b2, o1, o2):
    o1[...] = (a1[...] + b1[...].astype(f32)).astype(bf16)
    o2[...] = (a2[...] + b2[...].astype(f32)).astype(bf16)


def join_shares(a1, b1, a2, b2):
    arrays = (a1, b1, a2, b2)
    shapes = [jax.ShapeDtypeStruct(a1.shape, bf16)] * 2
    return pl.pallas_call(
        join_body,
        in_specs=[VMEM] * len(arrays),
        out_specs=[VMEM] * len(shapes),
        out_shape=shapes,
        compiler_params=params(8),
        cost_estimate=cost(1e6, 3e6),
        name="join_shares",
    )(*arrays)


def last_body(a0, a1, a2, b0, b1, b2, out):
    for k, (own, one, other) in enumerate(((a0, a1, a2), (b0, b1, b2))):
        @pl.when(pl.program_id(0) == k)
        def _():
            out[...] = (own[...] + one[...].astype(f32) + other[...].astype(f32)).astype(bf16)


def last_sum(*arrays):
    m = HERE * BLOCK
    return pl.pallas_call(
        last_body,
        grid=(2,),
        in_specs=[whole(a.shape) for a in arrays],
        out_specs=pl.BlockSpec((m, 128), lambda g: (g, 0)),
        out_shape=jax.ShapeDtypeStruct((2 * m, 128), bf16),
        compiler_params=params(8),
        cost_estimate=cost(1e6, 3e6),
        name="last_sum",
    )(*arrays)


def orders(mp, n_mp, width):
    here = width // n_mp
    shape = (width, width)
    row = lax.broadcasted_iota(jnp.int32, shape, 0)
    col = lax.broadcasted_iota(jnp.int32, shape, 1)
    place = lax.rem(mp - row // here + n_mp, n_mp) * here + lax.rem(row, here)
    goal = lax.rem(mp + col // here, n_mp) * here + lax.rem(col, here)
    return [
        keep.astype(f32).astype(bf16)
        for keep in (place == col, width - 1 - place == col, goal == row, width - 1 - goal == row)
    ]


def prepare_1_body(n_mp, mp, w_x, w_bc, w_dt, o_f, o_r, o_dt):
    pick_f, pick_r, _, _ = orders(mp[0], n_mp, w_x.shape[0])
    w = jnp.concatenate([w_x[...], w_bc[:, 0:NSTATE]], axis=1)
    o_f[...] = jnp.dot(pick_f, w, preferred_element_type=f32).astype(bf16)
    o_r[...] = jnp.dot(pick_r, w, preferred_element_type=f32).astype(bf16)
    rows = [
        lax.dot_general(w_dt[...], pick, (((1,), (1,)), ((), ())), preferred_element_type=f32)
        for pick in (pick_f, pick_r)
    ]
    o_dt[...] = jnp.concatenate(rows, axis=0).astype(bf16)


def prepare_2_body(n_mp, mp, w_bc, w_z, w_out, o_f, o_r, p_f, p_r):
    pick_f, pick_r, out_f, out_r = orders(mp[0], n_mp, w_z.shape[0])
    w = jnp.concatenate([w_bc[:, NSTATE:], w_z[...]], axis=1)
    o_f[...] = jnp.dot(pick_f, w, preferred_element_type=f32).astype(bf16)
    o_r[...] = jnp.dot(pick_r, w, preferred_element_type=f32).astype(bf16)
    p_f[...] = jnp.dot(w_out[...], out_f, preferred_element_type=f32).astype(bf16)
    p_r[...] = jnp.dot(w_out[...], out_r, preferred_element_type=f32).astype(bf16)


def prepare(body, name, n_mp, mp, arrays, shapes):
    return pl.pallas_call(
        functools.partial(body, n_mp),
        grid=(1,),
        in_specs=[SMEM] + [whole(a.shape) for a in arrays],
        out_specs=[whole(a) for a in shapes],
        out_shape=[jax.ShapeDtypeStruct(a, bf16) for a in shapes],
        compiler_params=params(20),
        cost_estimate=cost(1e9, 3e6),
        name=name,
    )(mp, *arrays)


def row_spread():
    out = np.zeros((16, 256), np.float32)
    for part in range(2):
        out[part * 8, 0:128] = 1.0
        out[part * 8 + 1, 128:256] = 1.0
    return out


def around(array, axis, count, shift):
    return lax.ppermute(array, axis, [(i, (i + shift) % count) for i in range(count)])


def digit_perm(count, stride, shift):
    pairs = []
    for i in range(count):
        d = (i // stride) % 4
        pairs.append((i, i + (((d + shift) % 4) - d) * stride))
    return pairs


INTRA_PARTS = 2


def shards(
    hidden, w_x, w_z, w_bc, w_dt, conv_x, conv_bc, dt_bias, decay_rate, skip_gain, norm_gain, w_out,
    piece_lengths,
):
    rows = hidden.shape[0]
    ctx, mp = lax.axis_index("ctx"), lax.axis_index("mp")
    n_ctx, n_mp = lax.axis_size("ctx"), lax.axis_size("mp")

    run = rows // 4
    middle = hidden[run - EDGE : 3 * run + EDGE]
    hs_0 = [middle] + [around(middle, "mp", n_mp, s) for s in range(1, n_mp)]
    low = lax.ppermute(hidden[rows - EDGE :], "ctx", [(i, i + 1) for i in range(n_ctx - 1)])
    high = lax.ppermute(hidden[:EDGE], "ctx", [(i + 1, i) for i in range(n_ctx - 1)])
    outer = jnp.concatenate([low, hidden[: run + EDGE], hidden[3 * run - EDGE :], high], axis=0)

    width = w_x.shape[0]
    place = mp[None].astype(jnp.int32)
    hs_1 = [outer] + [around(outer, "mp", n_mp, s) for s in range(1, n_mp)]
    w_1f, w_1r, wdt = prepare(
        prepare_1_body, "prepare_1", n_mp, place, (w_x, w_bc, w_dt.T),
        [(width, MIX), (width, MIX), (8, width)],
    )
    w_2f, w_2r, w_of, w_or = prepare(
        prepare_2_body, "prepare_2", n_mp, place, (w_bc, w_z, w_out),
        [(width, MIX), (width, MIX), w_out.shape, w_out.shape],
    )

    gain = norm_gain[None, :]
    spread = jnp.asarray(head_spread(), bf16)
    spread_rows = jnp.asarray(row_spread(), bf16)
    meta = jnp.stack([ctx * rows, ctx % 4, (ctx // 4) % 4, (ctx // 16) % 4]).astype(jnp.int32)

    first = (piece_lengths, meta, dt_bias, decay_rate)
    weights_1 = (w_1f, w_1r, wdt, conv_x, conv_bc, spread)
    weights_2 = (w_2f, w_2r, conv_x, conv_bc)

    xb_f, xb_r, cum, dt, fs_0, *middle_states = local_states(0, *first, hs_0, *weights_1)
    arguments = [(piece_lengths, meta, skip_gain, hs_0, *weights_2, xb_f, xb_r, cum, dt)]
    done = [[], []]

    def beside(chunk, part, received):
        new = intra(chunk, part, INTRA_PARTS, *arguments[chunk])
        received, new = lax.optimization_barrier((received, tuple(new)))
        done[chunk] += new
        return received

    hs_1 = beside(0, 0, tuple(hs_1))
    xb_f, xb_r, cum, dt, fs_1, starts, decays, *pays = local_states(
        1, *first, hs_1, *weights_1, middle_states
    )
    arguments.append((piece_lengths, meta, skip_gain, hs_1, *weights_2, xb_f, xb_r, cum, dt))

    def moved(arrays, stride):
        return [lax.ppermute(a, "ctx", digit_perm(n_ctx, stride, s)) for s, a in zip((1, 2, 3), arrays)]

    pre_s, pre_a, pay = join_group(meta, [pays[0]] + beside(0, 1, moved(pays[1:], 1)))
    low_s, low_a, top = join_middle(meta, [pay] + beside(1, 0, moved([pay] * 3, 4)))
    back = join_top(meta, beside(1, 1, moved([top] * 3, 16)) + [low_s, low_a, pre_s, pre_a])
    quarters = [back[0]] + moved(back[1:], 1)

    g_f, g_r, sums = gate(
        meta, done[0] + done[1], (fs_0, fs_1), starts, decays, quarters, gain, spread
    )
    all_sums = [sums] + [around(sums, "mp", n_mp, s) for s in range(1, n_mp)]
    tail = (g_f, g_r, all_sums, w_of, w_or, spread_rows)
    own_a, up_a, far_a, down_a = project_out(0, (f32, f32, bf16, bf16), *tail)
    far_a = around(far_a, "mp", n_mp, 1)
    own_b, up_b, far_b, down_b = project_out(1, (f32, bf16, bf16, f32), *tail)
    far_b = around(far_b, "mp", n_mp, n_mp - 1)
    down_a, up_b = around(down_a, "mp", n_mp, n_mp - 1), around(up_b, "mp", n_mp, 1)
    up_a, down_b = join_shares(up_a, far_a, down_b, far_b)
    up_a, down_b = around(up_a, "mp", n_mp, 1), around(down_b, "mp", n_mp, n_mp - 1)
    return last_sum(own_a, down_a, up_a, own_b, up_b, down_b)


def solution(mesh):
    return jax.shard_map(
        shards,
        mesh=mesh,
        in_specs=(
            P("ctx", "mp"),
            P(None, "mp"),
            P(None, "mp"),
            P(),
            P(None, "mp"),
            P(None, "mp"),
            P(),
            P("mp"),
            P("mp"),
            P("mp"),
            P("mp"),
            P("mp", None),
            P(),
        ),
        out_specs=P("ctx", "mp"),
        check_vma=False,
    )
```

```python
import functools

import jax
import jax.numpy as jnp
import numpy as np
from jax import lax
from jax.experimental import pallas as pl
from jax.experimental.pallas import tpu as pltpu
from jax.sharding import PartitionSpec as P

E = 1024
HEAD_DIM = 64
NSTATE = 128
BLOCK = 256
HEADS_HERE = 4
INNER = HEADS_HERE * HEAD_DIM
PIECES = 16
EPSILON = 1e-05
FAR = -1e30
EDGE = 16
MIX = INNER + NSTATE
QUARTER = NSTATE // 4
COUNT = (6, 2)
RUN = (6, 1)
BLOCKS = 8
HERE = BLOCKS // 2
PART = 2
PAY = 2 * QUARTER + 16

bf16 = jnp.bfloat16
f32 = jnp.float32


def head_spread():
    out = np.zeros((16, 2 * INNER), np.float32)
    for part in range(2):
        for stream in range(2):
            for h in range(HEADS_HERE):
                first = stream * INNER + h * HEAD_DIM
                out[part * 8 + stream * 4 + h, first : first + HEAD_DIM] = 1.0
    return out


def whole(shape):
    return pl.BlockSpec(shape, lambda *_: (0,) * len(shape))


SMEM = pl.BlockSpec(memory_space=pltpu.SMEM)
VMEM = pl.BlockSpec(memory_space=pltpu.VMEM)


def rows_at(g):
    return pl.ds(pl.multiple_of(g * BLOCK, BLOCK), BLOCK)


def params(mib):
    return pltpu.CompilerParams(vmem_limit_bytes=mib * 1024 * 1024)


def cost(flops, nbytes):
    return pl.CostEstimate(flops=int(flops), bytes_accessed=int(nbytes), transcendentals=0)


def bounds_of(pieces_ref):
    total = pieces_ref[0]
    ends = [total]
    for k in range(1, PIECES):
        total = total + pieces_ref[k]
        ends.append(total)
    return ends


def seg_rows(ends, first):
    shape = (8, BLOCK)
    pos = (
        first - 3 + lax.broadcasted_iota(jnp.int32, shape, 0)
        + lax.broadcasted_iota(jnp.int32, shape, 1)
    )
    seg = jnp.zeros(shape, jnp.int32)
    for end in ends:
        seg = seg + (pos >= end).astype(jnp.int32)
    return seg.astype(f32)


def has_boundary(ends, first):
    found = jnp.int32(0)
    for end in ends:
        found = found + ((end > first - 3) & (end <= first + BLOCK + 2)).astype(jnp.int32)
    return found > 0


def split2(rows):
    high = rows.astype(bf16)
    return jnp.concatenate([high, (rows - high.astype(f32)).astype(bf16)], axis=0)


def rows_to_cols(rows, spread):
    return lax.dot_general(
        split2(rows), spread, (((0,), (0,)), ((), ())), preferred_element_type=f32
    )


def row_of(chunk, g):
    return EDGE + g * BLOCK + (g // RUN[chunk]) * 2 * EDGE


def block_of(chunk, g):
    return g + 1 if chunk == 0 else g * (BLOCKS - 1)


def load_window(hs, chunk, g):
    at = pl.multiple_of(row_of(chunk, g) - EDGE, EDGE)
    return jnp.concatenate([h[pl.ds(at, BLOCK + 2 * EDGE), :] for h in hs], axis=1)


def silu(v):
    half = 0.5 * v
    return half + half * jnp.tanh(half)


def tap_rows(conv_x, conv_bc):
    return [conv_x[:, 0:128], conv_x[:, 128:256], conv_bc[:, 0:128], conv_bc[:, 128:256]]


def conv_tile(scratch, tile, taps, reverse, masks):
    total = None
    for back in range(4):
        first = back if reverse else EDGE - back
        term = scratch[tile, pl.ds(first, BLOCK), :] * taps[3 - back : 4 - back, :]
        if masks is not None and back:
            row = 3 + back if reverse else 3 - back
            term = term * masks[:, row : row + 1]
        total = term if total is None else total + term
    return silu(total).astype(bf16)


def keep_rounded(scratch, proj):
    for tile in range(scratch.shape[0]):
        scratch[tile] = proj[:, tile * 128 : (tile + 1) * 128].astype(bf16).astype(f32)


def per_head(scalars, shape, axis, width):
    head = lax.broadcasted_iota(jnp.int32, shape, axis) // width % HEADS_HERE
    out = jnp.full(shape, scalars[0], f32)
    for h in range(1, HEADS_HERE):
        out = jnp.where(head == h, scalars[h], out)
    return out


def split_rows(decays):
    at = lax.broadcasted_iota(jnp.int32, (16, INNER), 0)
    out = jnp.zeros((16, INNER), f32)
    for k, decay in enumerate(decays):
        high = decay.astype(bf16).astype(f32)
        out = jnp.where(at == 2 * k, high, jnp.where(at == 2 * k + 1, decay - high, out))
    return out.astype(bf16)


def decays_of(rows):
    wide = rows.astype(f32)
    return [wide[2 * k : 2 * k + 1, :] + wide[2 * k + 1 : 2 * k + 2, :] for k in range(2)]


def row_quantities(
    chunk, ends, origin, hs, wdt, dt_bias, rate, spread, cum_o, dt_o, fs_o, same_s, te_s, blockdec
):
    raw = []
    for b in range(COUNT[chunk]):
        at = row_of(chunk, b)
        block = jnp.concatenate([h[at : at + BLOCK, :] for h in hs], axis=1)
        raw.append(
            lax.dot_general(wdt[...], block, (((1,), (1,)), ((), ())), preferred_element_type=f32)
        )
    shape = (8 * COUNT[chunk], BLOCK)
    v = jnp.concatenate(raw, axis=0).astype(bf16).astype(f32) + per_head(dt_bias, shape, 0, 1)
    dt = jnp.maximum(v, 0.0) + jnp.log1p(jnp.exp(-jnp.abs(v)))
    logd = -dt * per_head(rate, shape, 0, 1)
    high = logd.astype(bf16)
    rest = logd - high.astype(f32)
    middle = rest.astype(bf16)
    low = (rest - middle.astype(f32)).astype(bf16)
    row_at = lax.broadcasted_iota(jnp.int32, (BLOCK, BLOCK), 0)
    col_at = lax.broadcasted_iota(jnp.int32, (BLOCK, BLOCK), 1)
    summed = []
    for keep in (row_at <= col_at, row_at >= col_at):
        ones = keep.astype(f32).astype(bf16)
        summed.append(sum(jnp.dot(p, ones, preferred_element_type=f32) for p in (low, middle, high)))
    forward = lax.broadcasted_iota(jnp.int32, (8, BLOCK), 0) < HEADS_HERE
    spread_f = spread[0:8, :].astype(f32)
    for b in range(COUNT[chunk]):
        rows = slice(b * 8, (b + 1) * 8)
        cols = slice(b * BLOCK, (b + 1) * BLOCK)
        cum = jnp.where(forward, summed[0][rows], summed[1][rows])
        dt_b = dt[rows]
        seg = seg_rows(ends, origin + block_of(chunk, b) * BLOCK)
        same_s[b] = (seg == seg[3:4, :]).astype(f32)
        own = jnp.broadcast_to(seg[3:4, :], (8, BLOCK))
        seg_end = jnp.where(forward, seg[3:4, BLOCK - 1 : BLOCK], seg[3:4, 0:1])
        seg_in = jnp.where(forward, seg[2:3, 0:1], seg[4:5, BLOCK - 1 : BLOCK])
        total = jnp.where(forward, cum[:, BLOCK - 1 : BLOCK], cum[:, 0:1])
        to_end = jnp.exp(total - cum) * (own == seg_end).astype(f32) * dt_b
        block_decay = jnp.exp(total) * (seg_end == seg_in).astype(f32)
        cum_o[:, cols] = cum
        dt_o[:, cols] = dt_b
        fs_o[:, cols] = jnp.exp(cum) * (own == seg_in).astype(f32)
        te_s[b] = split2(to_end)
        decay_row = jnp.sum(
            jnp.concatenate([block_decay, block_decay], axis=1) * spread_f, axis=0, keepdims=True
        )
        blockdec[b] = jnp.broadcast_to(decay_row, (8, 2 * INNER))


def k1_body(chunk, pieces, meta, dt_bias, rate, h0, h1, h2, h3, w_f, w_r, wdt, conv_x, conv_bc, spread, *rest):
    if chunk == 0:
        xb_f, xb_r, cum_o, dt_o, fs_o, added, blockdec, sf, sr, same_s, te_s = rest
    else:
        added_0, blockdec_0, *rest = rest
        xb_f, xb_r, cum_o, dt_o, fs_o, start_o, decay_o, p0, p1, p2, p3 = rest[:11]
        sf, sr, same_s, te_s, added, blockdec, total_s = rest[11:]
    ends = bounds_of(pieces)
    hs = (h0, h1, h2, h3)
    row_quantities(
        chunk, ends, meta[0], hs, wdt, dt_bias, rate, spread, cum_o, dt_o, fs_o, same_s, te_s, blockdec
    )

    def states(g, masked):
        window = load_window(hs, chunk, g)
        masks = same_s[g].T if masked else None
        taps = tap_rows(conv_x, conv_bc)
        wide = lax.dot_general(
            te_s[g], spread[...], (((0,), (0,)), ((), ())), preferred_element_type=f32
        )
        keep_rounded(sf, jnp.dot(window[: EDGE + BLOCK], w_f[...], preferred_element_type=f32))
        keep_rounded(sr, jnp.dot(window[EDGE:], w_r[...], preferred_element_type=f32))
        rows = rows_at(g)
        for stream, scratch, ref in ((0, sf, xb_f), (1, sr, xb_r)):
            scaled = []
            for tile in (0, 1):
                x = conv_tile(scratch, tile, taps[tile], stream == 1, masks)
                ref[rows, tile * 128 : (tile + 1) * 128] = x
                at = stream * INNER + tile * 128
                scaled.append((x.astype(f32) * wide[:, at : at + 128]).astype(bf16))
            b = conv_tile(scratch, 2, taps[2], stream == 1, masks)
            ref[rows, INNER:MIX] = b
            added[stream, g] = lax.dot_general(
                b, jnp.concatenate(scaled, axis=1), (((0,), (0,)), ((), ())), preferred_element_type=f32
            )

    @pl.loop(0, COUNT[chunk])
    def _(g):
        crosses = has_boundary(ends, meta[0] + block_of(chunk, g) * BLOCK)
        pl.when(crosses)(lambda: states(g, True))
        pl.when(jnp.logical_not(crosses))(lambda: states(g, False))

    if chunk == 0:
        return
    sources = {block_of(0, k): (added_0, blockdec_0, k) for k in range(COUNT[0])}
    sources.update({block_of(1, k): (added, blockdec, k) for k in range(COUNT[1])})
    decays = []
    for stream in range(2):
        state = jnp.zeros((NSTATE, INNER), f32)
        decay = jnp.ones((1, INNER), f32)
        for step in range(BLOCKS):
            b = step if stream == 0 else BLOCKS - 1 - step
            start_o[stream, b] = state
            decay_o[stream, b] = jnp.broadcast_to(decay, (8, INNER))
            states_ref, decays_ref, k = sources[b]
            d = decays_ref[k, 0:1, stream * INNER : (stream + 1) * INNER]
            state = d * state + states_ref[stream, k]
            decay = decay * d
        total_s[stream] = state
        decays.append(decay)
    rows = split_rows(decays)
    for s, ref in enumerate((p0, p1, p2, p3)):
        at = pl.multiple_of(lax.rem(meta[1] + s, 4) * QUARTER, QUARTER)
        ref[0:QUARTER, :] = total_s[0, pl.ds(at, QUARTER), :].astype(bf16)
        ref[QUARTER : 2 * QUARTER, :] = total_s[1, pl.ds(at, QUARTER), :].astype(bf16)
        ref[2 * QUARTER : PAY, :] = rows


def local_states(chunk, pieces, meta, dt_bias, rate, hs, w_f, w_r, wdt, conv_x, conv_bc, spread, others=()):
    count = COUNT[chunk]
    rows = count * BLOCK
    fixed = [*hs, w_f, w_r, wdt, conv_x, conv_bc, spread, *others]
    added = jax.ShapeDtypeStruct((2, count, NSTATE, INNER), f32)
    blockdec = jax.ShapeDtypeStruct((count, 8, 2 * INNER), f32)
    shapes = [
        jax.ShapeDtypeStruct((rows, MIX), bf16),
        jax.ShapeDtypeStruct((rows, MIX), bf16),
        jax.ShapeDtypeStruct((8, rows), f32),
        jax.ShapeDtypeStruct((8, rows), f32),
        jax.ShapeDtypeStruct((8, rows), f32),
    ]
    scratch = [
        pltpu.VMEM((MIX // 128, EDGE + BLOCK, 128), f32),
        pltpu.VMEM((MIX // 128, EDGE + BLOCK, 128), f32),
        pltpu.VMEM((count, 8, BLOCK), f32),
        pltpu.VMEM((count, 16, BLOCK), bf16),
    ]
    if chunk == 0:
        shapes += [added, blockdec]
    else:
        shapes += [
            jax.ShapeDtypeStruct((2, BLOCKS, NSTATE, INNER), f32),
            jax.ShapeDtypeStruct((2, BLOCKS, 8, INNER), f32),
        ] + [jax.ShapeDtypeStruct((PAY, INNER), bf16)] * 4
        scratch += [pltpu.VMEM(a.shape, f32) for a in (added, blockdec)]
        scratch += [pltpu.VMEM((2, NSTATE, INNER), f32)]
    return pl.pallas_call(
        functools.partial(k1_body, chunk),
        in_specs=[SMEM] * 4 + [VMEM] * len(fixed),
        out_specs=[VMEM] * len(shapes),
        out_shape=shapes,
        scratch_shapes=scratch,
        compiler_params=params(24),
        cost_estimate=cost(rows * 6e6, rows * 4000),
        name="local_states",
    )(pieces, meta, dt_bias, rate, *fixed)


def k2_body(
    chunk, base, count, pieces, meta, skip_gain, h0, h1, h2, h3, w_f, w_r, conv_x, conv_bc,
    xb_f, xb_r, cum_i, dt_i, c_f, c_r, y_f, y_r, z_f, z_r, sf, sr, open_mask,
):
    ends = bounds_of(pieces)
    row_at = lax.broadcasted_iota(jnp.int32, (BLOCK, BLOCK), 0)
    col_at = lax.broadcasted_iota(jnp.int32, (BLOCK, BLOCK), 1)
    half = BLOCK // 2

    open_mask[0] = jnp.where(row_at >= col_at, 0.0, FAR)
    open_mask[1] = jnp.where(row_at <= col_at, 0.0, FAR)

    def mix(step, masked):
        g = step + base
        first = meta[0] + block_of(chunk, g) * BLOCK
        here, there = rows_at(step), rows_at(g)
        window = load_window((h0, h1, h2, h3), chunk, g)
        masks = None
        if masked:
            seg = seg_rows(ends, first)
            masks = (seg == seg[3:4, :]).astype(f32).T
            together = seg.T[:, 3:4] == seg[3:4, :]
            open_mask[2] = jnp.where(together & (row_at >= col_at), 0.0, FAR)
            open_mask[3] = jnp.where(together & (row_at <= col_at), 0.0, FAR)
        proj_f = jnp.dot(window[: EDGE + BLOCK], w_f[...], preferred_element_type=f32)
        proj_r = jnp.dot(window[EDGE:], w_r[...], preferred_element_type=f32)
        keep_rounded(sf, proj_f)
        keep_rounded(sr, proj_r)
        z_f[here, :] = silu(proj_f[EDGE:, NSTATE:].astype(bf16).astype(f32))
        z_r[here, :] = silu(proj_r[0:BLOCK, NSTATE:].astype(bf16).astype(f32))
        taps = tap_rows(conv_x, conv_bc)[3]
        cum = cum_i[:, there]
        cum_t = cum.T
        log_dt = jnp.log(dt_i[:, there]) - cum
        lane_head = lax.broadcasted_iota(jnp.int32, (BLOCK, INNER), 1) // HEAD_DIM
        skip = per_head(skip_gain, (1, INNER), 1, HEAD_DIM)
        for stream, xb, scratch, c_ref, y_ref in ((0, xb_f, sf, c_f, y_f), (1, xb_r, sr, c_r, y_r)):
            c_rows = conv_tile(scratch, 0, taps, stream == 1, masks)
            c_ref[here, :] = c_rows
            x = xb[there, 0:INNER]
            b = xb[there, INNER:MIX]
            heads = [jnp.where(lane_head == h, x, jnp.zeros_like(x)) for h in range(HEADS_HERE)]
            for part in range(2):
                rows = slice(part * half, (part + 1) * half)
                if stream == 0:
                    cols = slice(0, half) if part == 0 else slice(0, BLOCK)
                else:
                    cols = slice(0, BLOCK) if part == 0 else slice(half, BLOCK)
                scores = lax.dot_general(
                    c_rows[rows, :], b[cols, :], (((1,), (1,)), ((), ())), preferred_element_type=f32
                )
                mask = open_mask[(2 if masked else 0) + stream, rows, cols]
                total = x[rows, :].astype(f32) * skip
                for h in range(HEADS_HERE):
                    at = stream * HEADS_HERE + h
                    gap = (cum_t[rows, at : at + 1] + log_dt[at : at + 1, cols]) + mask
                    weight = (jnp.exp(gap) * scores).astype(bf16)
                    total = total + jnp.dot(weight, heads[h][cols, :], preferred_element_type=f32)
                at = pl.multiple_of(step * BLOCK + part * half, half)
                y_ref[pl.ds(at, half), :] = total

    @pl.loop(0, count)
    def _(step):
        crosses = has_boundary(ends, meta[0] + block_of(chunk, step + base) * BLOCK)
        pl.when(crosses)(lambda: mix(step, True))
        pl.when(jnp.logical_not(crosses))(lambda: mix(step, False))


def intra(chunk, part, pieces, meta, skip_gain, hs, w_f, w_r, conv_x, conv_bc, xb_f, xb_r, cum, dt):
    count = PART
    rows = count * BLOCK
    arrays = [*hs, w_f, w_r, conv_x, conv_bc, xb_f, xb_r, cum, dt]
    return pl.pallas_call(
        functools.partial(k2_body, chunk, part * count, count),
        in_specs=[SMEM] * 3 + [VMEM] * len(arrays),
        out_specs=[VMEM] * 6,
        out_shape=[jax.ShapeDtypeStruct((rows, NSTATE), bf16)] * 2
        + [jax.ShapeDtypeStruct((rows, INNER), f32)] * 4,
        scratch_shapes=[
            pltpu.VMEM((1, EDGE + BLOCK, 128), f32),
            pltpu.VMEM((1, EDGE + BLOCK, 128), f32),
            pltpu.VMEM((4, BLOCK, BLOCK), f32),
        ],
        compiler_params=params(16),
        cost_estimate=cost(rows * 5e6, rows * 5000),
        name="intra",
    )(pieces, meta, skip_gain, *arrays)


def state_rows(ref, stream):
    return ref[stream * QUARTER : (stream + 1) * QUARTER, :].astype(f32)


def put_payload(ref, states, decays):
    for stream in range(2):
        ref[stream * QUARTER : (stream + 1) * QUARTER, :] = states[stream].astype(bf16)
    ref[2 * QUARTER : PAY, :] = split_rows(decays)


def group_body(meta, own, r1, r2, r3, pre_s, pre_a, pay, stage):
    me = meta[1]
    for s, ref in enumerate((own, r1, r2, r3)):
        stage[lax.rem(me - s + 4, 4)] = ref[...]
    states, decays = [], []
    for stream in range(2):
        state = jnp.zeros((QUARTER, INNER), f32)
        decay = jnp.ones((1, INNER), f32)
        for step in range(4):
            k = step if stream == 0 else 3 - step
            pre_s[k, stream] = state
            pre_a[k, stream] = jnp.broadcast_to(decay, (8, INNER))
            one = stage[k]
            d = decays_of(one[2 * QUARTER :])[stream]
            state = d * state + one[stream * QUARTER : (stream + 1) * QUARTER].astype(f32)
            decay = decay * d
        states.append(state)
        decays.append(decay)
    put_payload(pay, states, decays)


def before_digit(place, stream, got):
    low_s, low_a = jnp.zeros((QUARTER, INNER), f32), jnp.ones((1, INNER), f32)
    for s in (1, 2, 3):
        there = s <= place
        state, decay = got[s if stream == 0 else 4 - s]
        low_s = jnp.where(there, low_s + low_a * state, low_s)
        low_a = jnp.where(there, low_a * decay, low_a)
    return low_s, low_a


def middle_body(meta, own, r1, r2, r3, low_o, low_ao, pay):
    digit = meta[2]
    states, decays = [], []
    rows = [decays_of(r[2 * QUARTER : PAY, :]) for r in (own, r1, r2, r3)]
    for stream in range(2):
        got = [(state_rows(r, stream), rows[s][stream]) for s, r in enumerate((own, r1, r2, r3))]
        place = digit if stream == 0 else 3 - digit
        low_s, low_a = before_digit(place, stream, got)
        low_o[stream] = low_s
        low_ao[stream] = jnp.broadcast_to(low_a, (8, INNER))
        total_s, total_a = got[0][1] * low_s + got[0][0], got[0][1] * low_a
        for s in (3, 2, 1):
            there = s > place
            state, decay = got[s if stream == 0 else 4 - s]
            total_s = jnp.where(there, decay * total_s + state, total_s)
            total_a = jnp.where(there, decay * total_a, total_a)
        states.append(total_s)
        decays.append(total_a)
    put_payload(pay, states, decays)


def top_body(meta, r1, r2, r3, low_i, low_ai, pre_s, pre_a, *outs):
    digit = meta[3]
    rows = [None] + [decays_of(r[2 * QUARTER : PAY, :]) for r in (r1, r2, r3)]
    for stream in range(2):
        got = [None] + [
            (state_rows(r, stream), rows[s + 1][stream]) for s, r in enumerate((r1, r2, r3))
        ]
        place = digit if stream == 0 else 3 - digit
        top_s, _ = before_digit(place, stream, got)
        group_s = low_ai[stream, 0:1, :] * top_s + low_i[stream]
        for s, ref in enumerate(outs):
            k = lax.rem(meta[1] + s, 4)
            member = pre_a[k, stream][0:1, :] * group_s + pre_s[k, stream]
            ref[stream * QUARTER : (stream + 1) * QUARTER, :] = member.astype(bf16)


def small_call(body, name, meta, arrays, shapes, scratch=()):
    return pl.pallas_call(
        body,
        in_specs=[SMEM] + [VMEM] * len(arrays),
        out_specs=[VMEM] * len(shapes),
        out_shape=shapes,
        scratch_shapes=list(scratch),
        compiler_params=params(6),
        cost_estimate=cost(2e6, 1e6),
        name=name,
    )(meta, *arrays)


PAYLOAD = jax.ShapeDtypeStruct((PAY, INNER), bf16)


def join_group(meta, arrays):
    shapes = [
        jax.ShapeDtypeStruct((4, 2, QUARTER, INNER), f32),
        jax.ShapeDtypeStruct((4, 2, 8, INNER), f32),
        PAYLOAD,
    ]
    return small_call(group_body, "join_group", meta, arrays, shapes, [pltpu.VMEM((4, PAY, INNER), bf16)])


def join_middle(meta, arrays):
    shapes = [
        jax.ShapeDtypeStruct((2, QUARTER, INNER), f32),
        jax.ShapeDtypeStruct((2, 8, INNER), f32),
        PAYLOAD,
    ]
    return small_call(middle_body, "join_middle", meta, arrays, shapes)


def join_top(meta, arrays):
    shapes = [jax.ShapeDtypeStruct((2 * QUARTER, INNER), bf16)] * 4
    return small_call(top_body, "join_top", meta, arrays, shapes)


def k3_body(meta, *refs):
    parts, refs = refs[:24], refs[24:]
    fs, (starts, decays, q0, q1, q2, q3, gain, spread, g_f, g_r, sums, s_in) = refs[:2], refs[2:]
    for s, ref in enumerate((q0, q1, q2, q3)):
        at = pl.multiple_of(lax.rem(meta[1] - s + 4, 4) * QUARTER, QUARTER)
        for stream in range(2):
            s_in[stream, pl.ds(at, QUARTER), :] = state_rows(ref, stream)
    for chunk in range(2):
        for k in range(COUNT[chunk]):
            b = block_of(chunk, k)
            to = slice(b * BLOCK, (b + 1) * BLOCK)
            part, at = divmod(k, PART)
            rows = slice(at * BLOCK, (at + 1) * BLOCK)
            first = 6 * (chunk * COUNT[0] // PART + part)
            c, y, z = (parts[first + n : first + n + 2] for n in (0, 2, 4))
            wide = rows_to_cols(fs[chunk][:, k * BLOCK : (k + 1) * BLOCK], spread[...])
            for stream, g_ref in ((0, g_f), (1, g_r)):
                state = starts[stream, b] + decays[stream, b, 0:1, :] * s_in[stream]
                carried = jnp.dot(c[stream][rows, :], state.astype(bf16), preferred_element_type=f32)
                mixed = y[stream][rows, :] + carried * wide[:, stream * INNER : (stream + 1) * INNER]
                gated = mixed * z[stream][rows, :]
                square = gated * gated
                sums[stream : stream + 1, to] = jnp.sum(
                    (square[:, 0:128] + square[:, 128:256]).T, axis=0, keepdims=True
                )
                g_ref[to, :] = (gated * gain[...]).astype(bf16)


def gate(meta, locals_, fs, starts, decays, quarters, gain, spread):
    m = BLOCKS * BLOCK
    arrays = [*locals_, *fs, starts, decays, *quarters, gain, spread]
    return pl.pallas_call(
        k3_body,
        in_specs=[SMEM] + [VMEM] * len(arrays),
        out_specs=[VMEM] * 3,
        out_shape=[
            jax.ShapeDtypeStruct((m, INNER), bf16),
            jax.ShapeDtypeStruct((m, INNER), bf16),
            jax.ShapeDtypeStruct((2, m), f32),
        ],
        scratch_shapes=[pltpu.VMEM((2, NSTATE, INNER), f32)],
        compiler_params=params(12),
        cost_estimate=cost(m * 5e5, m * 6000),
        name="gate",
    )(meta, *arrays)


def k4_body(half, g_f, g_r, s0, s1, s2, s3, w_f, w_r, spread, o0, o1, o2, o3):
    for k in range(HERE):
        rows = slice((half * HERE + k) * BLOCK, (half * HERE + k + 1) * BLOCK)
        total = (s0[:, rows] + s1[:, rows]) + (s2[:, rows] + s3[:, rows])
        scale = lax.rsqrt(total / E + EPSILON)
        scale = jnp.concatenate([scale, jnp.zeros((6, BLOCK), f32)], axis=0)
        wide = rows_to_cols(scale, spread[...])
        out_f = jnp.dot(g_f[rows, :], w_f[...], preferred_element_type=f32)
        out_r = jnp.dot(g_r[rows, :], w_r[...], preferred_element_type=f32)
        for s, ref in enumerate((o0, o1, o2, o3)):
            cols = slice(s * 128, (s + 1) * 128)
            part = out_f[:, cols] * wide[:, 0:128] + out_r[:, cols] * wide[:, 128:256]
            ref[k * BLOCK : (k + 1) * BLOCK, :] = part.astype(ref.dtype)


def project_out(half, kinds, g_f, g_r, sums, w_f, w_r, spread):
    m = HERE * BLOCK
    arrays = [g_f, g_r, *sums, w_f, w_r, spread]
    return pl.pallas_call(
        functools.partial(k4_body, half),
        in_specs=[VMEM] * len(arrays),
        out_specs=[VMEM] * 4,
        out_shape=[jax.ShapeDtypeStruct((m, 128), kind) for kind in kinds],
        compiler_params=params(12),
        cost_estimate=cost(m * 1e6, m * 3000),
        name="project_out",
    )(*arrays)


def join_body(a1, b1, a2, b2, o1, o2):
    o1[...] = (a1[...] + b1[...].astype(f32)).astype(bf16)
    o2[...] = (a2[...] + b2[...].astype(f32)).astype(bf16)


def join_shares(a1, b1, a2, b2):
    arrays = (a1, b1, a2, b2)
    shapes = [jax.ShapeDtypeStruct(a1.shape, bf16)] * 2
    return pl.pallas_call(
        join_body,
        in_specs=[VMEM] * len(arrays),
        out_specs=[VMEM] * len(shapes),
        out_shape=shapes,
        compiler_params=params(8),
        cost_estimate=cost(1e6, 3e6),
        name="join_shares",
    )(*arrays)


def last_body(a0, a1, a2, b0, b1, b2, out):
    for k, (own, one, other) in enumerate(((a0, a1, a2), (b0, b1, b2))):
        @pl.when(pl.program_id(0) == k)
        def _():
            out[...] = (own[...] + one[...].astype(f32) + other[...].astype(f32)).astype(bf16)


def last_sum(*arrays):
    m = HERE * BLOCK
    return pl.pallas_call(
        last_body,
        grid=(2,),
        in_specs=[whole(a.shape) for a in arrays],
        out_specs=pl.BlockSpec((m, 128), lambda g: (g, 0)),
        out_shape=jax.ShapeDtypeStruct((2 * m, 128), bf16),
        compiler_params=params(8),
        cost_estimate=cost(1e6, 3e6),
        name="last_sum",
    )(*arrays)


def orders(mp, n_mp, width):
    here = width // n_mp
    shape = (width, width)
    row = lax.broadcasted_iota(jnp.int32, shape, 0)
    col = lax.broadcasted_iota(jnp.int32, shape, 1)
    place = lax.rem(mp - row // here + n_mp, n_mp) * here + lax.rem(row, here)
    goal = lax.rem(mp + col // here, n_mp) * here + lax.rem(col, here)
    return [
        keep.astype(f32).astype(bf16)
        for keep in (place == col, width - 1 - place == col, goal == row, width - 1 - goal == row)
    ]


def prepare_body(n_mp, mp, w, o_f, o_r, o_dt, q_f, q_r):
    pick_f, pick_r, _, _ = orders(mp[0], n_mp, w.shape[0])
    moved = [jnp.dot(pick, w[...], preferred_element_type=f32) for pick in (pick_f, pick_r)]
    for rows, first, second in ((moved[0], o_f, q_f), (moved[1], o_r, q_r)):
        first[...] = rows[:, 0:MIX].astype(bf16)
        second[...] = rows[:, MIX : 2 * MIX].astype(bf16)
    lane = lax.broadcasted_iota(jnp.int32, (w.shape[0], 128), 1)
    steps = jnp.where(lane < HEADS_HERE, moved[0][:, 2 * MIX :], moved[1][:, 2 * MIX :])
    o_dt[...] = steps.T[0:8, :].astype(bf16)


def prepare_out_body(n_mp, mp, w_out, p_f, p_r):
    _, _, out_f, out_r = orders(mp[0], n_mp, w_out.shape[1])
    p_f[...] = jnp.dot(w_out[...], out_f, preferred_element_type=f32).astype(bf16)
    p_r[...] = jnp.dot(w_out[...], out_r, preferred_element_type=f32).astype(bf16)


def prepare(body, name, n_mp, mp, w, shapes):
    return pl.pallas_call(
        functools.partial(body, n_mp),
        in_specs=[SMEM, VMEM],
        out_specs=[VMEM] * len(shapes),
        out_shape=[jax.ShapeDtypeStruct(a, bf16) for a in shapes],
        compiler_params=params(16),
        cost_estimate=cost(1e9, 3e6),
        name=name,
    )(mp, w)


def row_spread():
    out = np.zeros((16, 256), np.float32)
    for part in range(2):
        out[part * 8, 0:128] = 1.0
        out[part * 8 + 1, 128:256] = 1.0
    return out


def around(array, axis, count, shift):
    return lax.ppermute(array, axis, [(i, (i + shift) % count) for i in range(count)])


def digit_perm(count, stride, shift):
    pairs = []
    for i in range(count):
        d = (i // stride) % 4
        pairs.append((i, i + (((d + shift) % 4) - d) * stride))
    return pairs


def shards(
    hidden, w_x, w_z, w_bc, w_dt, conv_x, conv_bc, dt_bias, decay_rate, skip_gain, norm_gain, w_out,
    piece_lengths,
):
    rows = hidden.shape[0]
    ctx, mp = lax.axis_index("ctx"), lax.axis_index("mp")
    n_ctx, n_mp = lax.axis_size("ctx"), lax.axis_size("mp")

    run = RUN[1] * BLOCK
    middle = hidden[run - EDGE : rows - run + EDGE]
    hs_0 = [middle] + [around(middle, "mp", n_mp, s) for s in range(1, n_mp)]
    low = lax.ppermute(hidden[rows - EDGE :], "ctx", [(i, i + 1) for i in range(n_ctx - 1)])
    high = lax.ppermute(hidden[:EDGE], "ctx", [(i + 1, i) for i in range(n_ctx - 1)])
    outer = jnp.concatenate([low, hidden[: run + EDGE], hidden[rows - run - EDGE :], high], axis=0)

    hs_1 = [outer] + [around(outer, "mp", n_mp, s) for s in range(1, n_mp)]
    width = w_x.shape[0]
    place = mp[None].astype(jnp.int32)
    spare = jnp.zeros((width, 128 - 2 * HEADS_HERE), bf16)
    w_1f, w_1r, wdt, w_2f, w_2r = prepare(
        prepare_body, "prepare", n_mp, place, jnp.concatenate([w_x, w_bc, w_z, w_dt, w_dt, spare], axis=1),
        [(width, MIX), (width, MIX), (8, width), (width, MIX), (width, MIX)],
    )

    gain = norm_gain[None, :]
    spread = jnp.asarray(head_spread(), bf16)
    spread_rows = jnp.asarray(row_spread(), bf16)
    meta = jnp.stack([ctx * rows, ctx % 4, (ctx // 4) % 4, (ctx // 16) % 4]).astype(jnp.int32)

    first = (piece_lengths, meta, dt_bias, decay_rate)
    weights_1 = (w_1f, w_1r, wdt, conv_x, conv_bc, spread)
    weights_2 = (w_2f, w_2r, conv_x, conv_bc)

    xb_f, xb_r, cum, dt, fs_0, *middle_states = local_states(0, *first, hs_0, *weights_1)
    arguments = [(piece_lengths, meta, skip_gain, hs_0, *weights_2, xb_f, xb_r, cum, dt)]
    done = [[], []]

    def beside(chunk, part, received):
        new = intra(chunk, part, *arguments[chunk])
        received, new = lax.optimization_barrier((received, tuple(new)))
        done[chunk] += new
        return received

    xb_f, xb_r, cum, dt, fs_1, starts, decays, *pays = local_states(
        1, *first, hs_1, *weights_1, middle_states
    )
    pays, late, late_place = lax.optimization_barrier((pays, w_out, place))
    w_of, w_or = prepare(prepare_out_body, "prepare_out", n_mp, late_place, late, [w_out.shape] * 2)
    arguments.append((piece_lengths, meta, skip_gain, hs_1, *weights_2, xb_f, xb_r, cum, dt))

    def moved(arrays, stride):
        return [lax.ppermute(a, "ctx", digit_perm(n_ctx, stride, s)) for s, a in zip((1, 2, 3), arrays)]

    pre_s, pre_a, pay = join_group(meta, [pays[0]] + beside(0, 0, moved(pays[1:], 1)))
    low_s, low_a, top = join_middle(meta, [pay] + beside(0, 1, moved([pay] * 3, 4)))
    back = join_top(meta, beside(0, 2, moved([top] * 3, 16)) + [low_s, low_a, pre_s, pre_a])
    quarters = [back[0]] + beside(1, 0, moved(back[1:], 1))

    g_f, g_r, sums = gate(
        meta, done[0] + done[1], (fs_0, fs_1), starts, decays, quarters, gain, spread
    )
    all_sums = [sums] + [around(sums, "mp", n_mp, s) for s in range(1, n_mp)]
    tail = (g_f, g_r, all_sums, w_of, w_or, spread_rows)
    own_a, up_a, far_a, down_a = project_out(0, (f32, f32, bf16, bf16), *tail)
    far_a = around(far_a, "mp", n_mp, 1)
    own_b, up_b, far_b, down_b = project_out(1, (f32, bf16, bf16, f32), *tail)
    far_b = around(far_b, "mp", n_mp, n_mp - 1)
    down_a, up_b = around(down_a, "mp", n_mp, n_mp - 1), around(up_b, "mp", n_mp, 1)
    up_a, down_b = join_shares(up_a, far_a, down_b, far_b)
    up_a, down_b = around(up_a, "mp", n_mp, 1), around(down_b, "mp", n_mp, n_mp - 1)
    return last_sum(own_a, down_a, up_a, own_b, up_b, down_b)


def solution(mesh):
    return jax.shard_map(
        shards,
        mesh=mesh,
        in_specs=(
            P("ctx", "mp"),
            P(None, "mp"),
            P(None, "mp"),
            P(),
            P(None, "mp"),
            P(None, "mp"),
            P(),
            P("mp"),
            P("mp"),
            P("mp"),
            P("mp"),
            P("mp", None),
            P(),
        ),
        out_specs=P("ctx", "mp"),
        check_vma=False,
    )
```

```python
import functools

import jax
import jax.numpy as jnp
import numpy as np
from jax import lax
from jax.experimental import pallas as pl
from jax.experimental.pallas import tpu as pltpu
from jax.sharding import PartitionSpec as P

E = 1024
HEAD_DIM = 64
NSTATE = 128
BLOCK = 256
HEADS_HERE = 4
INNER = HEADS_HERE * HEAD_DIM
PIECES = 16
EPSILON = 1e-05
FAR = -1e30
EDGE = 16
MIX = INNER + NSTATE
QUARTER = NSTATE // 4
COUNT = (6, 2)
RUN = (6, 1)
BLOCKS = 8
HERE = BLOCKS // 2
PART = 2
PAY = 2 * QUARTER + 16

bf16 = jnp.bfloat16
f32 = jnp.float32


def head_spread():
    out = np.zeros((16, 2 * INNER), np.float32)
    for part in range(2):
        for stream in range(2):
            for h in range(HEADS_HERE):
                first = stream * INNER + h * HEAD_DIM
                out[part * 8 + stream * 4 + h, first : first + HEAD_DIM] = 1.0
    return out


def whole(shape):
    return pl.BlockSpec(shape, lambda *_: (0,) * len(shape))


SMEM = pl.BlockSpec(memory_space=pltpu.SMEM)
VMEM = pl.BlockSpec(memory_space=pltpu.VMEM)


def rows_at(g):
    return pl.ds(pl.multiple_of(g * BLOCK, BLOCK), BLOCK)


def params(mib):
    return pltpu.CompilerParams(vmem_limit_bytes=mib * 1024 * 1024)


def cost(flops, nbytes):
    return pl.CostEstimate(flops=int(flops), bytes_accessed=int(nbytes), transcendentals=0)


def scalars_of(ctx, rows, piece_lengths):
    order = jnp.arange(PIECES, dtype=jnp.int32)
    ends = jnp.sum(jnp.where(order[:, None] <= order[None, :], piece_lengths[:, None], 0), axis=0)
    first = ctx * rows + BLOCK * jnp.arange(BLOCKS, dtype=jnp.int32)
    near = (ends[None, :] > first[:, None] - 3) & (ends[None, :] <= first[:, None] + BLOCK + 2)
    flags = jnp.sum(near.astype(jnp.int32), axis=1)
    digits = jnp.stack([ctx * rows, ctx % 4, (ctx // 4) % 4, (ctx // 16) % 4])
    return jnp.concatenate([digits, flags, ends]).astype(jnp.int32)


def ends_of(meta):
    return [meta[4 + BLOCKS + k] for k in range(PIECES)]


def seg_rows(ends, first):
    shape = (8, BLOCK)
    pos = (
        first - 3 + lax.broadcasted_iota(jnp.int32, shape, 0)
        + lax.broadcasted_iota(jnp.int32, shape, 1)
    )
    seg = jnp.zeros(shape, jnp.int32)
    for end in ends:
        seg = seg + (pos >= end).astype(jnp.int32)
    return seg.astype(f32)


def split2(rows):
    high = rows.astype(bf16)
    return jnp.concatenate([high, (rows - high.astype(f32)).astype(bf16)], axis=0)


def rows_to_cols(rows, spread):
    return lax.dot_general(
        split2(rows), spread, (((0,), (0,)), ((), ())), preferred_element_type=f32
    )


def row_of(chunk, g):
    return EDGE + g * BLOCK + (g // RUN[chunk]) * 2 * EDGE


def block_of(chunk, g):
    return g + 1 if chunk == 0 else g * (BLOCKS - 1)


def load_window(hs, chunk, g):
    at = pl.multiple_of(row_of(chunk, g) - EDGE, EDGE)
    return jnp.concatenate([h[pl.ds(at, BLOCK + 2 * EDGE), :] for h in hs], axis=1)


def silu(v):
    half = 0.5 * v
    return half + half * jnp.tanh(half)


def tap_rows(conv_x, conv_bc):
    return [conv_x[:, 0:128], conv_x[:, 128:256], conv_bc[:, 0:128], conv_bc[:, 128:256]]


def conv_tile(scratch, tile, taps, reverse, masks):
    total = None
    for back in range(4):
        first = back if reverse else EDGE - back
        term = scratch[tile, pl.ds(first, BLOCK), :] * taps[3 - back : 4 - back, :]
        if masks is not None and back:
            row = 3 + back if reverse else 3 - back
            term = term * masks[:, row : row + 1]
        total = term if total is None else total + term
    return silu(total).astype(bf16)


def keep_rounded(scratch, proj):
    for tile in range(scratch.shape[0]):
        scratch[tile] = proj[:, tile * 128 : (tile + 1) * 128].astype(bf16).astype(f32)


def per_head(scalars, shape, axis, width):
    head = lax.broadcasted_iota(jnp.int32, shape, axis) // width % HEADS_HERE
    out = jnp.full(shape, scalars[0], f32)
    for h in range(1, HEADS_HERE):
        out = jnp.where(head == h, scalars[h], out)
    return out


def split_rows(decays):
    at = lax.broadcasted_iota(jnp.int32, (16, INNER), 0)
    out = jnp.zeros((16, INNER), f32)
    for k, decay in enumerate(decays):
        high = decay.astype(bf16).astype(f32)
        out = jnp.where(at == 2 * k, high, jnp.where(at == 2 * k + 1, decay - high, out))
    return out.astype(bf16)


def decays_of(rows):
    wide = rows.astype(f32)
    return [wide[2 * k : 2 * k + 1, :] + wide[2 * k + 1 : 2 * k + 2, :] for k in range(2)]


def row_quantities(
    chunk, ends, origin, hs, wdt, dt_bias, rate, spread, cum_o, dt_o, fs_o, same_s, te_s, blockdec
):
    raw = []
    for b in range(COUNT[chunk]):
        at = row_of(chunk, b)
        block = jnp.concatenate([h[at : at + BLOCK, :] for h in hs], axis=1)
        raw.append(
            lax.dot_general(wdt[...], block, (((1,), (1,)), ((), ())), preferred_element_type=f32)
        )
    shape = (8 * COUNT[chunk], BLOCK)
    v = jnp.concatenate(raw, axis=0).astype(bf16).astype(f32) + per_head(dt_bias, shape, 0, 1)
    dt = jnp.maximum(v, 0.0) + jnp.log1p(jnp.exp(-jnp.abs(v)))
    logd = -dt * per_head(rate, shape, 0, 1)
    high = logd.astype(bf16)
    rest = logd - high.astype(f32)
    middle = rest.astype(bf16)
    low = (rest - middle.astype(f32)).astype(bf16)
    row_at = lax.broadcasted_iota(jnp.int32, (BLOCK, BLOCK), 0)
    col_at = lax.broadcasted_iota(jnp.int32, (BLOCK, BLOCK), 1)
    summed = []
    for keep in (row_at <= col_at, row_at >= col_at):
        ones = keep.astype(f32).astype(bf16)
        summed.append(sum(jnp.dot(p, ones, preferred_element_type=f32) for p in (low, middle, high)))
    forward = lax.broadcasted_iota(jnp.int32, (8, BLOCK), 0) < HEADS_HERE
    spread_f = spread[0:8, :].astype(f32)
    for b in range(COUNT[chunk]):
        rows = slice(b * 8, (b + 1) * 8)
        cols = slice(b * BLOCK, (b + 1) * BLOCK)
        cum = jnp.where(forward, summed[0][rows], summed[1][rows])
        dt_b = dt[rows]
        seg = seg_rows(ends, origin + block_of(chunk, b) * BLOCK)
        same_s[b] = (seg == seg[3:4, :]).astype(f32)
        own = jnp.broadcast_to(seg[3:4, :], (8, BLOCK))
        seg_end = jnp.where(forward, seg[3:4, BLOCK - 1 : BLOCK], seg[3:4, 0:1])
        seg_in = jnp.where(forward, seg[2:3, 0:1], seg[4:5, BLOCK - 1 : BLOCK])
        total = jnp.where(forward, cum[:, BLOCK - 1 : BLOCK], cum[:, 0:1])
        to_end = jnp.exp(total - cum) * (own == seg_end).astype(f32) * dt_b
        block_decay = jnp.exp(total) * (seg_end == seg_in).astype(f32)
        cum_o[:, cols] = cum
        dt_o[:, cols] = dt_b
        fs_o[:, cols] = jnp.exp(cum) * (own == seg_in).astype(f32)
        te_s[b] = split2(to_end)
        decay_row = jnp.sum(
            jnp.concatenate([block_decay, block_decay], axis=1) * spread_f, axis=0, keepdims=True
        )
        blockdec[b] = jnp.broadcast_to(decay_row, (8, 2 * INNER))


def k1_body(chunk, meta, dt_bias, rate, h0, h1, h2, h3, w_f, w_r, wdt, conv_x, conv_bc, spread, *rest):
    if chunk == 0:
        xb_f, xb_r, cum_o, dt_o, fs_o, added, blockdec, sf, sr, same_s, te_s = rest
    else:
        added_0, blockdec_0, *rest = rest
        xb_f, xb_r, cum_o, dt_o, fs_o, start_o, decay_o, p0, p1, p2, p3 = rest[:11]
        sf, sr, same_s, te_s, added, blockdec, total_s = rest[11:]
    ends = ends_of(meta)
    hs = (h0, h1, h2, h3)
    row_quantities(
        chunk, ends, meta[0], hs, wdt, dt_bias, rate, spread, cum_o, dt_o, fs_o, same_s, te_s, blockdec
    )

    def states(g, masked):
        window = load_window(hs, chunk, g)
        masks = same_s[g].T if masked else None
        taps = tap_rows(conv_x, conv_bc)
        wide = lax.dot_general(
            te_s[g], spread[...], (((0,), (0,)), ((), ())), preferred_element_type=f32
        )
        keep_rounded(sf, jnp.dot(window[: EDGE + BLOCK], w_f[...], preferred_element_type=f32))
        keep_rounded(sr, jnp.dot(window[EDGE:], w_r[...], preferred_element_type=f32))
        rows = rows_at(g)
        for stream, scratch, ref in ((0, sf, xb_f), (1, sr, xb_r)):
            scaled = []
            for tile in (0, 1):
                x = conv_tile(scratch, tile, taps[tile], stream == 1, masks)
                ref[rows, tile * 128 : (tile + 1) * 128] = x
                at = stream * INNER + tile * 128
                scaled.append((x.astype(f32) * wide[:, at : at + 128]).astype(bf16))
            b = conv_tile(scratch, 2, taps[2], stream == 1, masks)
            ref[rows, INNER:MIX] = b
            added[stream, g] = lax.dot_general(
                b, jnp.concatenate(scaled, axis=1), (((0,), (0,)), ((), ())), preferred_element_type=f32
            )

    @pl.loop(0, COUNT[chunk])
    def _(g):
        crosses = meta[4 + block_of(chunk, g)] > 0
        pl.when(crosses)(lambda: states(g, True))
        pl.when(jnp.logical_not(crosses))(lambda: states(g, False))

    if chunk == 0:
        return
    sources = {block_of(0, k): (added_0, blockdec_0, k) for k in range(COUNT[0])}
    sources.update({block_of(1, k): (added, blockdec, k) for k in range(COUNT[1])})
    decays = []
    for stream in range(2):
        state = jnp.zeros((NSTATE, INNER), f32)
        decay = jnp.ones((1, INNER), f32)
        for step in range(BLOCKS):
            b = step if stream == 0 else BLOCKS - 1 - step
            start_o[stream, b] = state
            decay_o[stream, b] = jnp.broadcast_to(decay, (8, INNER))
            states_ref, decays_ref, k = sources[b]
            d = decays_ref[k, 0:1, stream * INNER : (stream + 1) * INNER]
            state = d * state + states_ref[stream, k]
            decay = decay * d
        total_s[stream] = state
        decays.append(decay)
    rows = split_rows(decays)
    for s, ref in enumerate((p0, p1, p2, p3)):
        at = pl.multiple_of(lax.rem(meta[1] + s, 4) * QUARTER, QUARTER)
        ref[0:QUARTER, :] = total_s[0, pl.ds(at, QUARTER), :].astype(bf16)
        ref[QUARTER : 2 * QUARTER, :] = total_s[1, pl.ds(at, QUARTER), :].astype(bf16)
        ref[2 * QUARTER : PAY, :] = rows


def local_states(chunk, meta, dt_bias, rate, hs, w_f, w_r, wdt, conv_x, conv_bc, spread, others=()):
    count = COUNT[chunk]
    rows = count * BLOCK
    fixed = [*hs, w_f, w_r, wdt, conv_x, conv_bc, spread, *others]
    added = jax.ShapeDtypeStruct((2, count, NSTATE, INNER), f32)
    blockdec = jax.ShapeDtypeStruct((count, 8, 2 * INNER), f32)
    shapes = [
        jax.ShapeDtypeStruct((rows, MIX), bf16),
        jax.ShapeDtypeStruct((rows, MIX), bf16),
        jax.ShapeDtypeStruct((8, rows), f32),
        jax.ShapeDtypeStruct((8, rows), f32),
        jax.ShapeDtypeStruct((8, rows), f32),
    ]
    scratch = [
        pltpu.VMEM((MIX // 128, EDGE + BLOCK, 128), f32),
        pltpu.VMEM((MIX // 128, EDGE + BLOCK, 128), f32),
        pltpu.VMEM((count, 8, BLOCK), f32),
        pltpu.VMEM((count, 16, BLOCK), bf16),
    ]
    if chunk == 0:
        shapes += [added, blockdec]
    else:
        shapes += [
            jax.ShapeDtypeStruct((2, BLOCKS, NSTATE, INNER), f32),
            jax.ShapeDtypeStruct((2, BLOCKS, 8, INNER), f32),
        ] + [jax.ShapeDtypeStruct((PAY, INNER), bf16)] * 4
        scratch += [pltpu.VMEM(a.shape, f32) for a in (added, blockdec)]
        scratch += [pltpu.VMEM((2, NSTATE, INNER), f32)]
    return pl.pallas_call(
        functools.partial(k1_body, chunk),
        in_specs=[SMEM] * 3 + [VMEM] * len(fixed),
        out_specs=[VMEM] * len(shapes),
        out_shape=shapes,
        scratch_shapes=scratch,
        compiler_params=params(12),
        cost_estimate=cost(rows * 6e6, rows * 4000),
        name="local_states",
    )(meta, dt_bias, rate, *fixed)


def k2_body(
    chunk, base, count, meta, skip_gain, h0, h1, h2, h3, w_f, w_r, conv_x, conv_bc,
    xb_f, xb_r, cum_i, dt_i, c_f, c_r, y_f, y_r, z_f, z_r, sf, sr, open_mask,
):
    row_at = lax.broadcasted_iota(jnp.int32, (BLOCK, BLOCK), 0)
    col_at = lax.broadcasted_iota(jnp.int32, (BLOCK, BLOCK), 1)
    half = BLOCK // 2

    open_mask[0] = jnp.where(row_at >= col_at, 0.0, FAR)
    open_mask[1] = jnp.where(row_at <= col_at, 0.0, FAR)

    def mix(step, masked):
        g = step + base
        first = meta[0] + block_of(chunk, g) * BLOCK
        here, there = rows_at(step), rows_at(g)
        window = load_window((h0, h1, h2, h3), chunk, g)
        masks = None
        if masked:
            seg = seg_rows(ends_of(meta), first)
            masks = (seg == seg[3:4, :]).astype(f32).T
            together = seg.T[:, 3:4] == seg[3:4, :]
            open_mask[2] = jnp.where(together & (row_at >= col_at), 0.0, FAR)
            open_mask[3] = jnp.where(together & (row_at <= col_at), 0.0, FAR)
        proj_f = jnp.dot(window[: EDGE + BLOCK], w_f[...], preferred_element_type=f32)
        proj_r = jnp.dot(window[EDGE:], w_r[...], preferred_element_type=f32)
        keep_rounded(sf, proj_f)
        keep_rounded(sr, proj_r)
        z_f[here, :] = silu(proj_f[EDGE:, NSTATE:].astype(bf16).astype(f32))
        z_r[here, :] = silu(proj_r[0:BLOCK, NSTATE:].astype(bf16).astype(f32))
        taps = tap_rows(conv_x, conv_bc)[3]
        cum = cum_i[:, there]
        cum_t = cum.T
        log_dt = jnp.log(dt_i[:, there]) - cum
        lane_head = lax.broadcasted_iota(jnp.int32, (BLOCK, INNER), 1) // HEAD_DIM
        skip = per_head(skip_gain, (1, INNER), 1, HEAD_DIM)
        for stream, xb, scratch, c_ref, y_ref in ((0, xb_f, sf, c_f, y_f), (1, xb_r, sr, c_r, y_r)):
            c_rows = conv_tile(scratch, 0, taps, stream == 1, masks)
            c_ref[here, :] = c_rows
            x = xb[there, 0:INNER]
            b = xb[there, INNER:MIX]
            heads = [jnp.where(lane_head == h, x, jnp.zeros_like(x)) for h in range(HEADS_HERE)]
            for part in range(2):
                rows = slice(part * half, (part + 1) * half)
                if stream == 0:
                    cols = slice(0, half) if part == 0 else slice(0, BLOCK)
                else:
                    cols = slice(0, BLOCK) if part == 0 else slice(half, BLOCK)
                scores = lax.dot_general(
                    c_rows[rows, :], b[cols, :], (((1,), (1,)), ((), ())), preferred_element_type=f32
                )
                mask = open_mask[(2 if masked else 0) + stream, rows, cols]
                total = x[rows, :].astype(f32) * skip
                for h in range(HEADS_HERE):
                    at = stream * HEADS_HERE + h
                    gap = (cum_t[rows, at : at + 1] + log_dt[at : at + 1, cols]) + mask
                    weight = (jnp.exp(gap) * scores).astype(bf16)
                    total = total + jnp.dot(weight, heads[h][cols, :], preferred_element_type=f32)
                at = pl.multiple_of(step * BLOCK + part * half, half)
                y_ref[pl.ds(at, half), :] = total

    @pl.loop(0, count)
    def _(step):
        crosses = meta[4 + block_of(chunk, step + base)] > 0
        pl.when(crosses)(lambda: mix(step, True))
        pl.when(jnp.logical_not(crosses))(lambda: mix(step, False))


def intra(chunk, part, meta, skip_gain, hs, w_f, w_r, conv_x, conv_bc, xb_f, xb_r, cum, dt):
    count = PART
    rows = count * BLOCK
    arrays = [*hs, w_f, w_r, conv_x, conv_bc, xb_f, xb_r, cum, dt]
    return pl.pallas_call(
        functools.partial(k2_body, chunk, part * count, count),
        in_specs=[SMEM] * 2 + [VMEM] * len(arrays),
        out_specs=[VMEM] * 6,
        out_shape=[jax.ShapeDtypeStruct((rows, NSTATE), bf16)] * 2
        + [jax.ShapeDtypeStruct((rows, INNER), f32)] * 4,
        scratch_shapes=[
            pltpu.VMEM((1, EDGE + BLOCK, 128), f32),
            pltpu.VMEM((1, EDGE + BLOCK, 128), f32),
            pltpu.VMEM((4, BLOCK, BLOCK), f32),
        ],
        compiler_params=params(10),
        cost_estimate=cost(rows * 5e6, rows * 5000),
        name="intra",
    )(meta, skip_gain, *arrays)


def state_rows(ref, stream):
    return ref[stream * QUARTER : (stream + 1) * QUARTER, :].astype(f32)


def put_payload(ref, states, decays):
    for stream in range(2):
        ref[stream * QUARTER : (stream + 1) * QUARTER, :] = states[stream].astype(bf16)
    ref[2 * QUARTER : PAY, :] = split_rows(decays)


def group_body(meta, own, r1, r2, r3, pre_s, pre_a, pay, stage):
    me = meta[1]
    for s, ref in enumerate((own, r1, r2, r3)):
        stage[lax.rem(me - s + 4, 4)] = ref[...]
    states, decays = [], []
    for stream in range(2):
        state = jnp.zeros((QUARTER, INNER), f32)
        decay = jnp.ones((1, INNER), f32)
        for step in range(4):
            k = step if stream == 0 else 3 - step
            pre_s[k, stream] = state
            pre_a[k, stream] = jnp.broadcast_to(decay, (8, INNER))
            one = stage[k]
            d = decays_of(one[2 * QUARTER :])[stream]
            state = d * state + one[stream * QUARTER : (stream + 1) * QUARTER].astype(f32)
            decay = decay * d
        states.append(state)
        decays.append(decay)
    put_payload(pay, states, decays)


def before_digit(place, stream, got):
    low_s, low_a = jnp.zeros((QUARTER, INNER), f32), jnp.ones((1, INNER), f32)
    for s in (1, 2, 3):
        there = s <= place
        state, decay = got[s if stream == 0 else 4 - s]
        low_s = jnp.where(there, low_s + low_a * state, low_s)
        low_a = jnp.where(there, low_a * decay, low_a)
    return low_s, low_a


def middle_body(meta, own, r1, r2, r3, low_o, low_ao, pay):
    digit = meta[2]
    states, decays = [], []
    rows = [decays_of(r[2 * QUARTER : PAY, :]) for r in (own, r1, r2, r3)]
    for stream in range(2):
        got = [(state_rows(r, stream), rows[s][stream]) for s, r in enumerate((own, r1, r2, r3))]
        place = digit if stream == 0 else 3 - digit
        low_s, low_a = before_digit(place, stream, got)
        low_o[stream] = low_s
        low_ao[stream] = jnp.broadcast_to(low_a, (8, INNER))
        total_s, total_a = got[0][1] * low_s + got[0][0], got[0][1] * low_a
        for s in (3, 2, 1):
            there = s > place
            state, decay = got[s if stream == 0 else 4 - s]
            total_s = jnp.where(there, decay * total_s + state, total_s)
            total_a = jnp.where(there, decay * total_a, total_a)
        states.append(total_s)
        decays.append(total_a)
    put_payload(pay, states, decays)


def top_body(meta, r1, r2, r3, low_i, low_ai, pre_s, pre_a, *outs):
    digit = meta[3]
    rows = [None] + [decays_of(r[2 * QUARTER : PAY, :]) for r in (r1, r2, r3)]
    for stream in range(2):
        got = [None] + [
            (state_rows(r, stream), rows[s + 1][stream]) for s, r in enumerate((r1, r2, r3))
        ]
        place = digit if stream == 0 else 3 - digit
        top_s, _ = before_digit(place, stream, got)
        group_s = low_ai[stream, 0:1, :] * top_s + low_i[stream]
        for s, ref in enumerate(outs):
            k = lax.rem(meta[1] + s, 4)
            member = pre_a[k, stream][0:1, :] * group_s + pre_s[k, stream]
            ref[stream * QUARTER : (stream + 1) * QUARTER, :] = member.astype(bf16)


def small_call(body, name, meta, arrays, shapes, scratch=()):
    return pl.pallas_call(
        body,
        in_specs=[SMEM] + [VMEM] * len(arrays),
        out_specs=[VMEM] * len(shapes),
        out_shape=shapes,
        scratch_shapes=list(scratch),
        compiler_params=params(6),
        cost_estimate=cost(2e6, 1e6),
        name=name,
    )(meta, *arrays)


PAYLOAD = jax.ShapeDtypeStruct((PAY, INNER), bf16)


def join_group(meta, arrays):
    shapes = [
        jax.ShapeDtypeStruct((4, 2, QUARTER, INNER), f32),
        jax.ShapeDtypeStruct((4, 2, 8, INNER), f32),
        PAYLOAD,
    ]
    return small_call(group_body, "join_group", meta, arrays, shapes, [pltpu.VMEM((4, PAY, INNER), bf16)])


def join_middle(meta, arrays):
    shapes = [
        jax.ShapeDtypeStruct((2, QUARTER, INNER), f32),
        jax.ShapeDtypeStruct((2, 8, INNER), f32),
        PAYLOAD,
    ]
    return small_call(middle_body, "join_middle", meta, arrays, shapes)


def join_top(meta, arrays):
    shapes = [jax.ShapeDtypeStruct((2 * QUARTER, INNER), bf16)] * 4
    return small_call(top_body, "join_top", meta, arrays, shapes)


def k3_body(meta, *refs):
    parts, refs = refs[:24], refs[24:]
    fs, (starts, decays, q0, q1, q2, q3, gain, spread, g_f, g_r, sums, s_in) = refs[:2], refs[2:]
    for s, ref in enumerate((q0, q1, q2, q3)):
        at = pl.multiple_of(lax.rem(meta[1] - s + 4, 4) * QUARTER, QUARTER)
        for stream in range(2):
            s_in[stream, pl.ds(at, QUARTER), :] = state_rows(ref, stream)
    for chunk in range(2):
        for k in range(COUNT[chunk]):
            b = block_of(chunk, k)
            to = slice(b * BLOCK, (b + 1) * BLOCK)
            part, at = divmod(k, PART)
            rows = slice(at * BLOCK, (at + 1) * BLOCK)
            first = 6 * (chunk * COUNT[0] // PART + part)
            c, y, z = (parts[first + n : first + n + 2] for n in (0, 2, 4))
            wide = rows_to_cols(fs[chunk][:, k * BLOCK : (k + 1) * BLOCK], spread[...])
            for stream, g_ref in ((0, g_f), (1, g_r)):
                state = starts[stream, b] + decays[stream, b, 0:1, :] * s_in[stream]
                carried = jnp.dot(c[stream][rows, :], state.astype(bf16), preferred_element_type=f32)
                mixed = y[stream][rows, :] + carried * wide[:, stream * INNER : (stream + 1) * INNER]
                gated = mixed * z[stream][rows, :]
                square = gated * gated
                sums[stream : stream + 1, to] = jnp.sum(
                    (square[:, 0:128] + square[:, 128:256]).T, axis=0, keepdims=True
                )
                g_ref[to, :] = (gated * gain[...]).astype(bf16)


def gate(meta, locals_, fs, starts, decays, quarters, gain, spread):
    m = BLOCKS * BLOCK
    arrays = [*locals_, *fs, starts, decays, *quarters, gain, spread]
    return pl.pallas_call(
        k3_body,
        in_specs=[SMEM] + [VMEM] * len(arrays),
        out_specs=[VMEM] * 3,
        out_shape=[
            jax.ShapeDtypeStruct((m, INNER), bf16),
            jax.ShapeDtypeStruct((m, INNER), bf16),
            jax.ShapeDtypeStruct((2, m), f32),
        ],
        scratch_shapes=[pltpu.VMEM((2, NSTATE, INNER), f32)],
        compiler_params=params(12),
        cost_estimate=cost(m * 5e5, m * 6000),
        name="gate",
    )(meta, *arrays)


def k4_body(half, g_f, g_r, s0, s1, s2, s3, w_f, w_r, spread, o0, o1, o2, o3):
    for k in range(HERE):
        rows = slice((half * HERE + k) * BLOCK, (half * HERE + k + 1) * BLOCK)
        total = (s0[:, rows] + s1[:, rows]) + (s2[:, rows] + s3[:, rows])
        scale = lax.rsqrt(total / E + EPSILON)
        scale = jnp.concatenate([scale, jnp.zeros((6, BLOCK), f32)], axis=0)
        wide = rows_to_cols(scale, spread[...])
        out_f = jnp.dot(g_f[rows, :], w_f[...], preferred_element_type=f32)
        out_r = jnp.dot(g_r[rows, :], w_r[...], preferred_element_type=f32)
        for s, ref in enumerate((o0, o1, o2, o3)):
            cols = slice(s * 128, (s + 1) * 128)
            part = out_f[:, cols] * wide[:, 0:128] + out_r[:, cols] * wide[:, 128:256]
            ref[k * BLOCK : (k + 1) * BLOCK, :] = part.astype(ref.dtype)


def project_out(half, kinds, g_f, g_r, sums, w_f, w_r, spread):
    m = HERE * BLOCK
    arrays = [g_f, g_r, *sums, w_f, w_r, spread]
    return pl.pallas_call(
        functools.partial(k4_body, half),
        in_specs=[VMEM] * len(arrays),
        out_specs=[VMEM] * 4,
        out_shape=[jax.ShapeDtypeStruct((m, 128), kind) for kind in kinds],
        compiler_params=params(12),
        cost_estimate=cost(m * 1e6, m * 3000),
        name="project_out",
    )(*arrays)


def join_body(a1, b1, a2, b2, o1, o2):
    o1[...] = (a1[...] + b1[...].astype(f32)).astype(bf16)
    o2[...] = (a2[...] + b2[...].astype(f32)).astype(bf16)


def join_shares(a1, b1, a2, b2):
    arrays = (a1, b1, a2, b2)
    shapes = [jax.ShapeDtypeStruct(a1.shape, bf16)] * 2
    return pl.pallas_call(
        join_body,
        in_specs=[VMEM] * len(arrays),
        out_specs=[VMEM] * len(shapes),
        out_shape=shapes,
        compiler_params=params(8),
        cost_estimate=cost(1e6, 3e6),
        name="join_shares",
    )(*arrays)


def last_body(a0, a1, a2, b0, b1, b2, out):
    for k, (own, one, other) in enumerate(((a0, a1, a2), (b0, b1, b2))):
        @pl.when(pl.program_id(0) == k)
        def _():
            out[...] = (own[...] + one[...].astype(f32) + other[...].astype(f32)).astype(bf16)


def last_sum(*arrays):
    m = HERE * BLOCK
    return pl.pallas_call(
        last_body,
        grid=(2,),
        in_specs=[whole(a.shape) for a in arrays],
        out_specs=pl.BlockSpec((m, 128), lambda g: (g, 0)),
        out_shape=jax.ShapeDtypeStruct((2 * m, 128), bf16),
        compiler_params=params(8),
        cost_estimate=cost(1e6, 3e6),
        name="last_sum",
    )(*arrays)


def orders(mp, n_mp, width):
    here = width // n_mp
    shape = (width, width)
    row = lax.broadcasted_iota(jnp.int32, shape, 0)
    col = lax.broadcasted_iota(jnp.int32, shape, 1)
    place = lax.rem(mp - row // here + n_mp, n_mp) * here + lax.rem(row, here)
    goal = lax.rem(mp + col // here, n_mp) * here + lax.rem(col, here)
    return [
        keep.astype(f32).astype(bf16)
        for keep in (place == col, width - 1 - place == col, goal == row, width - 1 - goal == row)
    ]


def prepare_1_body(n_mp, mp, w, o_f, o_r, o_dt):
    pick_f, pick_r, _, _ = orders(mp[0], n_mp, w.shape[0])
    moved = [jnp.dot(pick, w[...], preferred_element_type=f32) for pick in (pick_f, pick_r)]
    o_f[...] = moved[0][:, 0:MIX].astype(bf16)
    o_r[...] = moved[1][:, 0:MIX].astype(bf16)
    lane = lax.broadcasted_iota(jnp.int32, (w.shape[0], 128), 1)
    steps = jnp.where(lane < HEADS_HERE, moved[0][:, MIX:], moved[1][:, MIX:])
    o_dt[...] = steps.T[0:8, :].astype(bf16)


def prepare_2_body(n_mp, mp, w_bc, w_z, w_out, o_f, o_r, p_f, p_r):
    pick_f, pick_r, out_f, out_r = orders(mp[0], n_mp, w_z.shape[0])
    w = jnp.concatenate([w_bc[:, NSTATE:], w_z[...]], axis=1)
    o_f[...] = jnp.dot(pick_f, w, preferred_element_type=f32).astype(bf16)
    o_r[...] = jnp.dot(pick_r, w, preferred_element_type=f32).astype(bf16)
    p_f[...] = jnp.dot(w_out[...], out_f, preferred_element_type=f32).astype(bf16)
    p_r[...] = jnp.dot(w_out[...], out_r, preferred_element_type=f32).astype(bf16)


def prepare(body, name, n_mp, mp, weights, shapes):
    return pl.pallas_call(
        functools.partial(body, n_mp),
        in_specs=[SMEM] + [VMEM] * len(weights),
        out_specs=[VMEM] * len(shapes),
        out_shape=[jax.ShapeDtypeStruct(a, bf16) for a in shapes],
        compiler_params=params(10),
        cost_estimate=cost(1e9, 3e6),
        name=name,
    )(mp, *weights)


def row_spread():
    out = np.zeros((16, 256), np.float32)
    for part in range(2):
        out[part * 8, 0:128] = 1.0
        out[part * 8 + 1, 128:256] = 1.0
    return out


def around(array, axis, count, shift):
    return lax.ppermute(array, axis, [(i, (i + shift) % count) for i in range(count)])


def digit_perm(count, stride, shift):
    pairs = []
    for i in range(count):
        d = (i // stride) % 4
        pairs.append((i, i + (((d + shift) % 4) - d) * stride))
    return pairs


def shards(
    hidden, w_x, w_z, w_bc, w_dt, conv_x, conv_bc, dt_bias, decay_rate, skip_gain, norm_gain, w_out,
    piece_lengths,
):
    rows = hidden.shape[0]
    ctx, mp = lax.axis_index("ctx"), lax.axis_index("mp")
    n_ctx, n_mp = lax.axis_size("ctx"), lax.axis_size("mp")

    run = RUN[1] * BLOCK
    middle = hidden[run - EDGE : rows - run + EDGE]
    hs_0 = [middle] + [around(middle, "mp", n_mp, s) for s in range(1, n_mp)]
    low = lax.ppermute(hidden[rows - EDGE :], "ctx", [(i, i + 1) for i in range(n_ctx - 1)])
    high = lax.ppermute(hidden[:EDGE], "ctx", [(i + 1, i) for i in range(n_ctx - 1)])
    outer = jnp.concatenate([low, hidden[: run + EDGE], hidden[rows - run - EDGE :], high], axis=0)

    hs_1 = [outer] + [around(outer, "mp", n_mp, s) for s in range(1, n_mp)]
    width = w_x.shape[0]
    place = mp[None].astype(jnp.int32)
    spare = jnp.zeros((width, 128 - 2 * HEADS_HERE), bf16)
    together = jnp.concatenate([w_x, w_bc[:, :NSTATE], w_dt, w_dt, spare], axis=1)
    w_1f, w_1r, wdt = prepare(
        prepare_1_body, "prepare_1", n_mp, place, (together,), [(width, MIX), (width, MIX), (8, width)]
    )

    gain = norm_gain[None, :]
    spread = jnp.asarray(head_spread(), bf16)
    spread_rows = jnp.asarray(row_spread(), bf16)
    meta = scalars_of(ctx, rows, piece_lengths)

    first = (meta, dt_bias, decay_rate)
    weights_1 = (w_1f, w_1r, wdt, conv_x, conv_bc, spread)

    xb_f, xb_r, cum, dt, fs_0, *middle_states = local_states(0, *first, hs_0, *weights_1)
    rows_0 = (xb_f, xb_r, cum, dt)
    done = [[], []]

    def beside(chunk, part, received):
        new = intra(chunk, part, *arguments[chunk])
        received, new = lax.optimization_barrier((received, tuple(new)))
        done[chunk] += new
        return received

    xb_f, xb_r, cum, dt, fs_1, starts, decays, *pays = local_states(
        1, *first, hs_1, *weights_1, middle_states
    )
    pays, place = lax.optimization_barrier((pays, place))
    w_2f, w_2r, w_of, w_or = prepare(
        prepare_2_body, "prepare_2", n_mp, place, (w_bc, w_z, w_out),
        [(width, MIX), (width, MIX), w_out.shape, w_out.shape],
    )
    weights_2 = (w_2f, w_2r, conv_x, conv_bc)
    arguments = [(meta, skip_gain, hs_0, *weights_2, *rows_0)]
    arguments.append((meta, skip_gain, hs_1, *weights_2, xb_f, xb_r, cum, dt))

    def moved(arrays, stride):
        return [lax.ppermute(a, "ctx", digit_perm(n_ctx, stride, s)) for s, a in zip((1, 2, 3), arrays)]

    pre_s, pre_a, pay = join_group(meta, [pays[0]] + beside(0, 0, moved(pays[1:], 1)))
    low_s, low_a, top = join_middle(meta, [pay] + beside(0, 1, moved([pay] * 3, 4)))
    back = join_top(meta, beside(0, 2, moved([top] * 3, 16)) + [low_s, low_a, pre_s, pre_a])
    quarters = [back[0]] + beside(1, 0, moved(back[1:], 1))

    g_f, g_r, sums = gate(
        meta, done[0] + done[1], (fs_0, fs_1), starts, decays, quarters, gain, spread
    )
    all_sums = [sums] + [around(sums, "mp", n_mp, s) for s in range(1, n_mp)]
    tail = (g_f, g_r, all_sums, w_of, w_or, spread_rows)
    own_a, up_a, far_a, down_a = project_out(0, (f32, f32, bf16, bf16), *tail)
    far_a = around(far_a, "mp", n_mp, 1)
    own_b, up_b, far_b, down_b = project_out(1, (f32, bf16, bf16, f32), *tail)
    far_b = around(far_b, "mp", n_mp, n_mp - 1)
    down_a, up_b = around(down_a, "mp", n_mp, n_mp - 1), around(up_b, "mp", n_mp, 1)
    up_a, down_b = join_shares(up_a, far_a, down_b, far_b)
    up_a, down_b = around(up_a, "mp", n_mp, 1), around(down_b, "mp", n_mp, n_mp - 1)
    return last_sum(own_a, down_a, up_a, own_b, up_b, down_b)


def solution(mesh):
    return jax.shard_map(
        shards,
        mesh=mesh,
        in_specs=(
            P("ctx", "mp"),
            P(None, "mp"),
            P(None, "mp"),
            P(),
            P(None, "mp"),
            P(None, "mp"),
            P(),
            P("mp"),
            P("mp"),
            P("mp"),
            P("mp"),
            P("mp", None),
            P(),
        ),
        out_specs=P("ctx", "mp"),
        check_vma=False,
    )
```

```python
import functools

import jax
import jax.numpy as jnp
import numpy as np
from jax import lax
from jax.experimental import pallas as pl
from jax.experimental.pallas import tpu as pltpu
from jax.sharding import PartitionSpec as P

E = 1024
HEAD_DIM = 64
NSTATE = 128
BLOCK = 256
HEADS_HERE = 4
INNER = HEADS_HERE * HEAD_DIM
PIECES = 16
EPSILON = 1e-05
FAR = -1e30
EDGE = 16
MIX = INNER + NSTATE
QUARTER = NSTATE // 4
COUNT = (6, 2)
RUN = (6, 1)
BLOCKS = 8
HERE = BLOCKS // 2
PART = 2
PAY = 2 * QUARTER + 16

bf16 = jnp.bfloat16
f32 = jnp.float32


def head_spread():
    out = np.zeros((16, 2 * INNER), np.float32)
    for part in range(2):
        for stream in range(2):
            for h in range(HEADS_HERE):
                first = stream * INNER + h * HEAD_DIM
                out[part * 8 + stream * 4 + h, first : first + HEAD_DIM] = 1.0
    return out


def whole(shape):
    return pl.BlockSpec(shape, lambda *_: (0,) * len(shape))


SMEM = pl.BlockSpec(memory_space=pltpu.SMEM)
VMEM = pl.BlockSpec(memory_space=pltpu.VMEM)


def rows_at(g):
    return pl.ds(pl.multiple_of(g * BLOCK, BLOCK), BLOCK)


def params(mib):
    return pltpu.CompilerParams(vmem_limit_bytes=mib * 1024 * 1024)


def cost(flops, nbytes):
    return pl.CostEstimate(flops=int(flops), bytes_accessed=int(nbytes), transcendentals=0)


def bounds_of(pieces_ref):
    total = pieces_ref[0]
    ends = [total]
    for k in range(1, PIECES):
        total = total + pieces_ref[k]
        ends.append(total)
    return ends


def seg_rows(ends, first):
    shape = (8, BLOCK)
    pos = (
        first - 3 + lax.broadcasted_iota(jnp.int32, shape, 0)
        + lax.broadcasted_iota(jnp.int32, shape, 1)
    )
    seg = jnp.zeros(shape, jnp.int32)
    for end in ends:
        seg = seg + (pos >= end).astype(jnp.int32)
    return seg.astype(f32)


def has_boundary(ends, first):
    found = jnp.int32(0)
    for end in ends:
        found = found + ((end > first - 3) & (end <= first + BLOCK + 2)).astype(jnp.int32)
    return found > 0


def split2(rows):
    high = rows.astype(bf16)
    return jnp.concatenate([high, (rows - high.astype(f32)).astype(bf16)], axis=0)


def rows_to_cols(rows, spread):
    return lax.dot_general(
        split2(rows), spread, (((0,), (0,)), ((), ())), preferred_element_type=f32
    )


def row_of(chunk, g):
    return EDGE + g * BLOCK + (g // RUN[chunk]) * 2 * EDGE


def block_of(chunk, g):
    return g + 1 if chunk == 0 else g * (BLOCKS - 1)


def load_window(hs, chunk, g):
    at = pl.multiple_of(row_of(chunk, g) - EDGE, EDGE)
    return jnp.concatenate([h[pl.ds(at, BLOCK + 2 * EDGE), :] for h in hs], axis=1)


def silu(v):
    half = 0.5 * v
    return half + half * jnp.tanh(half)


def tap_rows(conv_x, conv_bc):
    return [conv_x[:, 0:128], conv_x[:, 128:256], conv_bc[:, 0:128], conv_bc[:, 128:256]]


def conv_tile(scratch, tile, taps, reverse, masks):
    total = None
    for back in range(4):
        first = back if reverse else EDGE - back
        term = scratch[tile, pl.ds(first, BLOCK), :] * taps[3 - back : 4 - back, :]
        if masks is not None and back:
            row = 3 + back if reverse else 3 - back
            term = term * masks[:, row : row + 1]
        total = term if total is None else total + term
    return silu(total).astype(bf16)


def keep_rounded(scratch, proj):
    for tile in range(scratch.shape[0]):
        scratch[tile] = proj[:, tile * 128 : (tile + 1) * 128].astype(bf16).astype(f32)


def per_head(scalars, shape, axis, width):
    head = lax.broadcasted_iota(jnp.int32, shape, axis) // width % HEADS_HERE
    out = jnp.full(shape, scalars[0], f32)
    for h in range(1, HEADS_HERE):
        out = jnp.where(head == h, scalars[h], out)
    return out


def split_rows(decays):
    at = lax.broadcasted_iota(jnp.int32, (16, INNER), 0)
    out = jnp.zeros((16, INNER), f32)
    for k, decay in enumerate(decays):
        high = decay.astype(bf16).astype(f32)
        out = jnp.where(at == 2 * k, high, jnp.where(at == 2 * k + 1, decay - high, out))
    return out.astype(bf16)


def decays_of(rows):
    wide = rows.astype(f32)
    return [wide[2 * k : 2 * k + 1, :] + wide[2 * k + 1 : 2 * k + 2, :] for k in range(2)]


def row_quantities(
    chunk, ends, origin, hs, wdt, dt_bias, rate, spread, cum_o, dt_o, fs_o, same_s, te_s, blockdec
):
    raw = []
    for b in range(COUNT[chunk]):
        at = row_of(chunk, b)
        block = jnp.concatenate([h[at : at + BLOCK, :] for h in hs], axis=1)
        raw.append(
            lax.dot_general(wdt[...], block, (((1,), (1,)), ((), ())), preferred_element_type=f32)
        )
    shape = (8 * COUNT[chunk], BLOCK)
    v = jnp.concatenate(raw, axis=0).astype(bf16).astype(f32) + per_head(dt_bias, shape, 0, 1)
    dt = jnp.maximum(v, 0.0) + jnp.log1p(jnp.exp(-jnp.abs(v)))
    logd = -dt * per_head(rate, shape, 0, 1)
    high = logd.astype(bf16)
    rest = logd - high.astype(f32)
    middle = rest.astype(bf16)
    low = (rest - middle.astype(f32)).astype(bf16)
    row_at = lax.broadcasted_iota(jnp.int32, (BLOCK, BLOCK), 0)
    col_at = lax.broadcasted_iota(jnp.int32, (BLOCK, BLOCK), 1)
    summed = []
    for keep in (row_at <= col_at, row_at >= col_at):
        ones = keep.astype(f32).astype(bf16)
        summed.append(sum(jnp.dot(p, ones, preferred_element_type=f32) for p in (low, middle, high)))
    forward = lax.broadcasted_iota(jnp.int32, (8, BLOCK), 0) < HEADS_HERE
    spread_f = spread[0:8, :].astype(f32)
    for b in range(COUNT[chunk]):
        rows = slice(b * 8, (b + 1) * 8)
        cols = slice(b * BLOCK, (b + 1) * BLOCK)
        cum = jnp.where(forward, summed[0][rows], summed[1][rows])
        dt_b = dt[rows]
        seg = seg_rows(ends, origin + block_of(chunk, b) * BLOCK)
        same_s[b] = (seg == seg[3:4, :]).astype(f32)
        own = jnp.broadcast_to(seg[3:4, :], (8, BLOCK))
        seg_end = jnp.where(forward, seg[3:4, BLOCK - 1 : BLOCK], seg[3:4, 0:1])
        seg_in = jnp.where(forward, seg[2:3, 0:1], seg[4:5, BLOCK - 1 : BLOCK])
        total = jnp.where(forward, cum[:, BLOCK - 1 : BLOCK], cum[:, 0:1])
        to_end = jnp.exp(total - cum) * (own == seg_end).astype(f32) * dt_b
        block_decay = jnp.exp(total) * (seg_end == seg_in).astype(f32)
        cum_o[:, cols] = cum
        dt_o[:, cols] = dt_b
        fs_o[:, cols] = jnp.exp(cum) * (own == seg_in).astype(f32)
        te_s[b] = split2(to_end)
        decay_row = jnp.sum(
            jnp.concatenate([block_decay, block_decay], axis=1) * spread_f, axis=0, keepdims=True
        )
        blockdec[b] = jnp.broadcast_to(decay_row, (8, 2 * INNER))


def k1_body(chunk, pieces, meta, dt_bias, rate, h0, h1, h2, h3, w_f, w_r, wdt, conv_x, conv_bc, spread, *rest):
    if chunk == 0:
        xb_f, xb_r, cum_o, dt_o, fs_o, added, blockdec, sf, sr, same_s, te_s = rest
    else:
        added_0, blockdec_0, *rest = rest
        xb_f, xb_r, cum_o, dt_o, fs_o, start_o, decay_o, p0, p1, p2, p3 = rest[:11]
        sf, sr, same_s, te_s, added, blockdec, total_s = rest[11:]
    ends = bounds_of(pieces)
    hs = (h0, h1, h2, h3)
    row_quantities(
        chunk, ends, meta[0], hs, wdt, dt_bias, rate, spread, cum_o, dt_o, fs_o, same_s, te_s, blockdec
    )

    def states(g, masked):
        window = load_window(hs, chunk, g)
        masks = same_s[g].T if masked else None
        taps = tap_rows(conv_x, conv_bc)
        wide = lax.dot_general(
            te_s[g], spread[...], (((0,), (0,)), ((), ())), preferred_element_type=f32
        )
        keep_rounded(sf, jnp.dot(window[: EDGE + BLOCK], w_f[...], preferred_element_type=f32))
        keep_rounded(sr, jnp.dot(window[EDGE:], w_r[...], preferred_element_type=f32))
        rows = rows_at(g)
        for stream, scratch, ref in ((0, sf, xb_f), (1, sr, xb_r)):
            scaled = []
            for tile in (0, 1):
                x = conv_tile(scratch, tile, taps[tile], stream == 1, masks)
                ref[rows, tile * 128 : (tile + 1) * 128] = x
                at = stream * INNER + tile * 128
                scaled.append((x.astype(f32) * wide[:, at : at + 128]).astype(bf16))
            b = conv_tile(scratch, 2, taps[2], stream == 1, masks)
            ref[rows, INNER:MIX] = b
            added[stream, g] = lax.dot_general(
                b, jnp.concatenate(scaled, axis=1), (((0,), (0,)), ((), ())), preferred_element_type=f32
            )

    @pl.loop(0, COUNT[chunk])
    def _(g):
        crosses = has_boundary(ends, meta[0] + block_of(chunk, g) * BLOCK)
        pl.when(crosses)(lambda: states(g, True))
        pl.when(jnp.logical_not(crosses))(lambda: states(g, False))

    if chunk == 0:
        return
    sources = {block_of(0, k): (added_0, blockdec_0, k) for k in range(COUNT[0])}
    sources.update({block_of(1, k): (added, blockdec, k) for k in range(COUNT[1])})
    decays = []
    for stream in range(2):
        state = jnp.zeros((NSTATE, INNER), f32)
        decay = jnp.ones((1, INNER), f32)
        for step in range(BLOCKS):
            b = step if stream == 0 else BLOCKS - 1 - step
            start_o[stream, b] = state
            decay_o[stream, b] = jnp.broadcast_to(decay, (8, INNER))
            states_ref, decays_ref, k = sources[b]
            d = decays_ref[k, 0:1, stream * INNER : (stream + 1) * INNER]
            state = d * state + states_ref[stream, k]
            decay = decay * d
        total_s[stream] = state
        decays.append(decay)
    rows = split_rows(decays)
    for s, ref in enumerate((p0, p1, p2, p3)):
        at = pl.multiple_of(lax.rem(meta[1] + s, 4) * QUARTER, QUARTER)
        ref[0:QUARTER, :] = total_s[0, pl.ds(at, QUARTER), :].astype(bf16)
        ref[QUARTER : 2 * QUARTER, :] = total_s[1, pl.ds(at, QUARTER), :].astype(bf16)
        ref[2 * QUARTER : PAY, :] = rows


def local_states(chunk, pieces, meta, dt_bias, rate, hs, w_f, w_r, wdt, conv_x, conv_bc, spread, others=()):
    count = COUNT[chunk]
    rows = count * BLOCK
    fixed = [*hs, w_f, w_r, wdt, conv_x, conv_bc, spread, *others]
    added = jax.ShapeDtypeStruct((2, count, NSTATE, INNER), f32)
    blockdec = jax.ShapeDtypeStruct((count, 8, 2 * INNER), f32)
    shapes = [
        jax.ShapeDtypeStruct((rows, MIX), bf16),
        jax.ShapeDtypeStruct((rows, MIX), bf16),
        jax.ShapeDtypeStruct((8, rows), f32),
        jax.ShapeDtypeStruct((8, rows), f32),
        jax.ShapeDtypeStruct((8, rows), f32),
    ]
    scratch = [
        pltpu.VMEM((MIX // 128, EDGE + BLOCK, 128), f32),
        pltpu.VMEM((MIX // 128, EDGE + BLOCK, 128), f32),
        pltpu.VMEM((count, 8, BLOCK), f32),
        pltpu.VMEM((count, 16, BLOCK), bf16),
    ]
    if chunk == 0:
        shapes += [added, blockdec]
    else:
        shapes += [
            jax.ShapeDtypeStruct((2, BLOCKS, NSTATE, INNER), f32),
            jax.ShapeDtypeStruct((2, BLOCKS, 8, INNER), f32),
        ] + [jax.ShapeDtypeStruct((PAY, INNER), bf16)] * 4
        scratch += [pltpu.VMEM(a.shape, f32) for a in (added, blockdec)]
        scratch += [pltpu.VMEM((2, NSTATE, INNER), f32)]
    return pl.pallas_call(
        functools.partial(k1_body, chunk),
        in_specs=[SMEM] * 4 + [VMEM] * len(fixed),
        out_specs=[VMEM] * len(shapes),
        out_shape=shapes,
        scratch_shapes=scratch,
        compiler_params=params(24),
        cost_estimate=cost(rows * 6e6, rows * 4000),
        name="local_states",
    )(pieces, meta, dt_bias, rate, *fixed)


def k2_body(
    chunk, base, count, pieces, meta, skip_gain, h0, h1, h2, h3, w_f, w_r, conv_x, conv_bc,
    xb_f, xb_r, cum_i, dt_i, c_f, c_r, y_f, y_r, z_f, z_r, sf, sr, open_mask,
):
    ends = bounds_of(pieces)
    row_at = lax.broadcasted_iota(jnp.int32, (BLOCK, BLOCK), 0)
    col_at = lax.broadcasted_iota(jnp.int32, (BLOCK, BLOCK), 1)
    half = BLOCK // 2

    open_mask[0] = jnp.where(row_at >= col_at, 0.0, FAR)
    open_mask[1] = jnp.where(row_at <= col_at, 0.0, FAR)

    def mix(step, masked):
        g = step + base
        first = meta[0] + block_of(chunk, g) * BLOCK
        here, there = rows_at(step), rows_at(g)
        window = load_window((h0, h1, h2, h3), chunk, g)
        masks = None
        if masked:
            seg = seg_rows(ends, first)
            masks = (seg == seg[3:4, :]).astype(f32).T
            together = seg.T[:, 3:4] == seg[3:4, :]
            open_mask[2] = jnp.where(together & (row_at >= col_at), 0.0, FAR)
            open_mask[3] = jnp.where(together & (row_at <= col_at), 0.0, FAR)
        proj_f = jnp.dot(window[: EDGE + BLOCK], w_f[...], preferred_element_type=f32)
        proj_r = jnp.dot(window[EDGE:], w_r[...], preferred_element_type=f32)
        keep_rounded(sf, proj_f)
        keep_rounded(sr, proj_r)
        z_f[here, :] = silu(proj_f[EDGE:, NSTATE:].astype(bf16).astype(f32))
        z_r[here, :] = silu(proj_r[0:BLOCK, NSTATE:].astype(bf16).astype(f32))
        taps = tap_rows(conv_x, conv_bc)[3]
        cum = cum_i[:, there]
        cum_t = cum.T
        log_dt = jnp.log(dt_i[:, there]) - cum
        lane_head = lax.broadcasted_iota(jnp.int32, (BLOCK, INNER), 1) // HEAD_DIM
        skip = per_head(skip_gain, (1, INNER), 1, HEAD_DIM)
        for stream, xb, scratch, c_ref, y_ref in ((0, xb_f, sf, c_f, y_f), (1, xb_r, sr, c_r, y_r)):
            c_rows = conv_tile(scratch, 0, taps, stream == 1, masks)
            c_ref[here, :] = c_rows
            x = xb[there, 0:INNER]
            b = xb[there, INNER:MIX]
            heads = [jnp.where(lane_head == h, x, jnp.zeros_like(x)) for h in range(HEADS_HERE)]
            for part in range(2):
                rows = slice(part * half, (part + 1) * half)
                if stream == 0:
                    cols = slice(0, half) if part == 0 else slice(0, BLOCK)
                else:
                    cols = slice(0, BLOCK) if part == 0 else slice(half, BLOCK)
                scores = lax.dot_general(
                    c_rows[rows, :], b[cols, :], (((1,), (1,)), ((), ())), preferred_element_type=f32
                )
                mask = open_mask[(2 if masked else 0) + stream, rows, cols]
                total = x[rows, :].astype(f32) * skip
                for h in range(HEADS_HERE):
                    at = stream * HEADS_HERE + h
                    gap = (cum_t[rows, at : at + 1] + log_dt[at : at + 1, cols]) + mask
                    weight = (jnp.exp(gap) * scores).astype(bf16)
                    total = total + jnp.dot(weight, heads[h][cols, :], preferred_element_type=f32)
                at = pl.multiple_of(step * BLOCK + part * half, half)
                y_ref[pl.ds(at, half), :] = total

    @pl.loop(0, count)
    def _(step):
        crosses = has_boundary(ends, meta[0] + block_of(chunk, step + base) * BLOCK)
        pl.when(crosses)(lambda: mix(step, True))
        pl.when(jnp.logical_not(crosses))(lambda: mix(step, False))


def intra(chunk, part, pieces, meta, skip_gain, hs, w_f, w_r, conv_x, conv_bc, xb_f, xb_r, cum, dt):
    count = PART
    rows = count * BLOCK
    arrays = [*hs, w_f, w_r, conv_x, conv_bc, xb_f, xb_r, cum, dt]
    return pl.pallas_call(
        functools.partial(k2_body, chunk, part * count, count),
        in_specs=[SMEM] * 3 + [VMEM] * len(arrays),
        out_specs=[VMEM] * 6,
        out_shape=[jax.ShapeDtypeStruct((rows, NSTATE), bf16)] * 2
        + [jax.ShapeDtypeStruct((rows, INNER), f32)] * 4,
        scratch_shapes=[
            pltpu.VMEM((1, EDGE + BLOCK, 128), f32),
            pltpu.VMEM((1, EDGE + BLOCK, 128), f32),
            pltpu.VMEM((4, BLOCK, BLOCK), f32),
        ],
        compiler_params=params(16),
        cost_estimate=cost(rows * 5e6, rows * 5000),
        name="intra",
    )(pieces, meta, skip_gain, *arrays)


def state_rows(ref, stream):
    return ref[stream * QUARTER : (stream + 1) * QUARTER, :].astype(f32)


def put_payload(ref, states, decays):
    for stream in range(2):
        ref[stream * QUARTER : (stream + 1) * QUARTER, :] = states[stream].astype(bf16)
    ref[2 * QUARTER : PAY, :] = split_rows(decays)


def group_body(meta, own, r1, r2, r3, pre_s, pre_a, pay, stage):
    me = meta[1]
    for s, ref in enumerate((own, r1, r2, r3)):
        stage[lax.rem(me - s + 4, 4)] = ref[...]
    states, decays = [], []
    for stream in range(2):
        state = jnp.zeros((QUARTER, INNER), f32)
        decay = jnp.ones((1, INNER), f32)
        for step in range(4):
            k = step if stream == 0 else 3 - step
            pre_s[k, stream] = state
            pre_a[k, stream] = jnp.broadcast_to(decay, (8, INNER))
            one = stage[k]
            d = decays_of(one[2 * QUARTER :])[stream]
            state = d * state + one[stream * QUARTER : (stream + 1) * QUARTER].astype(f32)
            decay = decay * d
        states.append(state)
        decays.append(decay)
    put_payload(pay, states, decays)


def before_digit(place, stream, got):
    low_s, low_a = jnp.zeros((QUARTER, INNER), f32), jnp.ones((1, INNER), f32)
    for s in (1, 2, 3):
        there = s <= place
        state, decay = got[s if stream == 0 else 4 - s]
        low_s = jnp.where(there, low_s + low_a * state, low_s)
        low_a = jnp.where(there, low_a * decay, low_a)
    return low_s, low_a


def pair_body(high, meta, own, other, *rest):
    low_o, low_ao, pay = rest[-3:]
    bit = lax.div(meta[2], 2) if high else lax.rem(meta[2], 2)
    own_a, other_a = (decays_of(r[2 * QUARTER : PAY, :]) for r in (own, other))
    states, decays = [], []
    for stream in range(2):
        later = bit == (1 if stream == 0 else 0)
        mine, theirs = state_rows(own, stream), state_rows(other, stream)
        group_s = jnp.where(later, theirs, 0.0)
        group_a = jnp.where(later, other_a[stream], 1.0)
        if high:
            low_a = rest[1][stream, 0:1, :]
            group_s, group_a = low_a * group_s + rest[0][stream], low_a * group_a
        low_o[stream] = group_s
        low_ao[stream] = jnp.broadcast_to(group_a, (8, INNER))
        states.append(
            jnp.where(later, own_a[stream] * theirs + mine, other_a[stream] * mine + theirs)
        )
        decays.append(own_a[stream] * other_a[stream])
    put_payload(pay, states, decays)


def top_body(meta, r1, r2, r3, low_i, low_ai, pre_s, pre_a, *outs):
    digit = meta[3]
    rows = [None] + [decays_of(r[2 * QUARTER : PAY, :]) for r in (r1, r2, r3)]
    for stream in range(2):
        got = [None] + [
            (state_rows(r, stream), rows[s + 1][stream]) for s, r in enumerate((r1, r2, r3))
        ]
        place = digit if stream == 0 else 3 - digit
        top_s, _ = before_digit(place, stream, got)
        group_s = low_ai[stream, 0:1, :] * top_s + low_i[stream]
        for s, ref in enumerate(outs):
            k = lax.rem(meta[1] + s, 4)
            member = pre_a[k, stream][0:1, :] * group_s + pre_s[k, stream]
            ref[stream * QUARTER : (stream + 1) * QUARTER, :] = member.astype(bf16)


def small_call(body, name, meta, arrays, shapes, scratch=()):
    return pl.pallas_call(
        body,
        in_specs=[SMEM] + [VMEM] * len(arrays),
        out_specs=[VMEM] * len(shapes),
        out_shape=shapes,
        scratch_shapes=list(scratch),
        compiler_params=params(6),
        cost_estimate=cost(2e6, 1e6),
        name=name,
    )(meta, *arrays)


PAYLOAD = jax.ShapeDtypeStruct((PAY, INNER), bf16)


def join_group(meta, arrays):
    shapes = [
        jax.ShapeDtypeStruct((4, 2, QUARTER, INNER), f32),
        jax.ShapeDtypeStruct((4, 2, 8, INNER), f32),
        PAYLOAD,
    ]
    return small_call(group_body, "join_group", meta, arrays, shapes, [pltpu.VMEM((4, PAY, INNER), bf16)])


def join_pair(high, meta, arrays):
    shapes = [
        jax.ShapeDtypeStruct((2, QUARTER, INNER), f32),
        jax.ShapeDtypeStruct((2, 8, INNER), f32),
        PAYLOAD,
    ]
    return small_call(functools.partial(pair_body, high), "join_pair", meta, arrays, shapes)


def join_top(meta, arrays):
    shapes = [jax.ShapeDtypeStruct((2 * QUARTER, INNER), bf16)] * 4
    return small_call(top_body, "join_top", meta, arrays, shapes)


def k3_body(meta, *refs):
    parts, refs = refs[:24], refs[24:]
    fs, (starts, decays, q0, q1, q2, q3, gain, spread, g_f, g_r, sums, s_in) = refs[:2], refs[2:]
    for s, ref in enumerate((q0, q1, q2, q3)):
        at = pl.multiple_of(lax.rem(meta[1] - s + 4, 4) * QUARTER, QUARTER)
        for stream in range(2):
            s_in[stream, pl.ds(at, QUARTER), :] = state_rows(ref, stream)
    for chunk in range(2):
        for k in range(COUNT[chunk]):
            b = block_of(chunk, k)
            to = slice(b * BLOCK, (b + 1) * BLOCK)
            part, at = divmod(k, PART)
            rows = slice(at * BLOCK, (at + 1) * BLOCK)
            first = 6 * (chunk * COUNT[0] // PART + part)
            c, y, z = (parts[first + n : first + n + 2] for n in (0, 2, 4))
            wide = rows_to_cols(fs[chunk][:, k * BLOCK : (k + 1) * BLOCK], spread[...])
            for stream, g_ref in ((0, g_f), (1, g_r)):
                state = starts[stream, b] + decays[stream, b, 0:1, :] * s_in[stream]
                carried = jnp.dot(c[stream][rows, :], state.astype(bf16), preferred_element_type=f32)
                mixed = y[stream][rows, :] + carried * wide[:, stream * INNER : (stream + 1) * INNER]
                gated = mixed * z[stream][rows, :]
                square = gated * gated
                sums[stream : stream + 1, to] = jnp.sum(
                    (square[:, 0:128] + square[:, 128:256]).T, axis=0, keepdims=True
                )
                g_ref[to, :] = (gated * gain[...]).astype(bf16)


def gate(meta, locals_, fs, starts, decays, quarters, gain, spread):
    m = BLOCKS * BLOCK
    arrays = [*locals_, *fs, starts, decays, *quarters, gain, spread]
    return pl.pallas_call(
        k3_body,
        in_specs=[SMEM] + [VMEM] * len(arrays),
        out_specs=[VMEM] * 3,
        out_shape=[
            jax.ShapeDtypeStruct((m, INNER), bf16),
            jax.ShapeDtypeStruct((m, INNER), bf16),
            jax.ShapeDtypeStruct((2, m), f32),
        ],
        scratch_shapes=[pltpu.VMEM((2, NSTATE, INNER), f32)],
        compiler_params=params(12),
        cost_estimate=cost(m * 5e5, m * 6000),
        name="gate",
    )(meta, *arrays)


def k4_body(half, g_f, g_r, s0, s1, s2, s3, w_f, w_r, spread, o0, o1, o2, o3):
    for k in range(HERE):
        rows = slice((half * HERE + k) * BLOCK, (half * HERE + k + 1) * BLOCK)
        total = (s0[:, rows] + s1[:, rows]) + (s2[:, rows] + s3[:, rows])
        scale = lax.rsqrt(total / E + EPSILON)
        scale = jnp.concatenate([scale, jnp.zeros((6, BLOCK), f32)], axis=0)
        wide = rows_to_cols(scale, spread[...])
        out_f = jnp.dot(g_f[rows, :], w_f[...], preferred_element_type=f32)
        out_r = jnp.dot(g_r[rows, :], w_r[...], preferred_element_type=f32)
        for s, ref in enumerate((o0, o1, o2, o3)):
            cols = slice(s * 128, (s + 1) * 128)
            part = out_f[:, cols] * wide[:, 0:128] + out_r[:, cols] * wide[:, 128:256]
            ref[k * BLOCK : (k + 1) * BLOCK, :] = part.astype(ref.dtype)


def project_out(half, kinds, g_f, g_r, sums, w_f, w_r, spread):
    m = HERE * BLOCK
    arrays = [g_f, g_r, *sums, w_f, w_r, spread]
    return pl.pallas_call(
        functools.partial(k4_body, half),
        in_specs=[VMEM] * len(arrays),
        out_specs=[VMEM] * 4,
        out_shape=[jax.ShapeDtypeStruct((m, 128), kind) for kind in kinds],
        compiler_params=params(12),
        cost_estimate=cost(m * 1e6, m * 3000),
        name="project_out",
    )(*arrays)


def join_body(a1, b1, a2, b2, o1, o2):
    o1[...] = (a1[...] + b1[...].astype(f32)).astype(bf16)
    o2[...] = (a2[...] + b2[...].astype(f32)).astype(bf16)


def join_shares(a1, b1, a2, b2):
    arrays = (a1, b1, a2, b2)
    shapes = [jax.ShapeDtypeStruct(a1.shape, bf16)] * 2
    return pl.pallas_call(
        join_body,
        in_specs=[VMEM] * len(arrays),
        out_specs=[VMEM] * len(shapes),
        out_shape=shapes,
        compiler_params=params(8),
        cost_estimate=cost(1e6, 3e6),
        name="join_shares",
    )(*arrays)


def last_body(a0, a1, a2, b0, b1, b2, out):
    for k, (own, one, other) in enumerate(((a0, a1, a2), (b0, b1, b2))):
        @pl.when(pl.program_id(0) == k)
        def _():
            out[...] = (own[...] + one[...].astype(f32) + other[...].astype(f32)).astype(bf16)


def last_sum(*arrays):
    m = HERE * BLOCK
    return pl.pallas_call(
        last_body,
        grid=(2,),
        in_specs=[whole(a.shape) for a in arrays],
        out_specs=pl.BlockSpec((m, 128), lambda g: (g, 0)),
        out_shape=jax.ShapeDtypeStruct((2 * m, 128), bf16),
        compiler_params=params(8),
        cost_estimate=cost(1e6, 3e6),
        name="last_sum",
    )(*arrays)


def orders(mp, n_mp, width):
    here = width // n_mp
    shape = (width, width)
    row = lax.broadcasted_iota(jnp.int32, shape, 0)
    col = lax.broadcasted_iota(jnp.int32, shape, 1)
    place = lax.rem(mp - row // here + n_mp, n_mp) * here + lax.rem(row, here)
    goal = lax.rem(mp + col // here, n_mp) * here + lax.rem(col, here)
    return [
        keep.astype(f32).astype(bf16)
        for keep in (place == col, width - 1 - place == col, goal == row, width - 1 - goal == row)
    ]


def prepare_body(n_mp, mp, w, o_f, o_r, o_dt, q_f, q_r):
    pick_f, pick_r, _, _ = orders(mp[0], n_mp, w.shape[0])
    moved = [jnp.dot(pick, w[...], preferred_element_type=f32) for pick in (pick_f, pick_r)]
    for rows, first, second in ((moved[0], o_f, q_f), (moved[1], o_r, q_r)):
        first[...] = rows[:, 0:MIX].astype(bf16)
        second[...] = rows[:, MIX : 2 * MIX].astype(bf16)
    lane = lax.broadcasted_iota(jnp.int32, (w.shape[0], 128), 1)
    steps = jnp.where(lane < HEADS_HERE, moved[0][:, 2 * MIX :], moved[1][:, 2 * MIX :])
    o_dt[...] = steps.T[0:8, :].astype(bf16)


def prepare_out_body(n_mp, mp, w_out, p_f, p_r):
    _, _, out_f, out_r = orders(mp[0], n_mp, w_out.shape[1])
    p_f[...] = jnp.dot(w_out[...], out_f, preferred_element_type=f32).astype(bf16)
    p_r[...] = jnp.dot(w_out[...], out_r, preferred_element_type=f32).astype(bf16)


def prepare(body, name, n_mp, mp, w, shapes):
    return pl.pallas_call(
        functools.partial(body, n_mp),
        in_specs=[SMEM, VMEM],
        out_specs=[VMEM] * len(shapes),
        out_shape=[jax.ShapeDtypeStruct(a, bf16) for a in shapes],
        compiler_params=params(16),
        cost_estimate=cost(1e9, 3e6),
        name=name,
    )(mp, w)


def row_spread():
    out = np.zeros((16, 256), np.float32)
    for part in range(2):
        out[part * 8, 0:128] = 1.0
        out[part * 8 + 1, 128:256] = 1.0
    return out


def around(array, axis, count, shift):
    return lax.ppermute(array, axis, [(i, (i + shift) % count) for i in range(count)])


def digit_perm(count, stride, shift):
    pairs = []
    for i in range(count):
        d = (i // stride) % 4
        pairs.append((i, i + (((d + shift) % 4) - d) * stride))
    return pairs


def shards(
    hidden, w_x, w_z, w_bc, w_dt, conv_x, conv_bc, dt_bias, decay_rate, skip_gain, norm_gain, w_out,
    piece_lengths,
):
    rows = hidden.shape[0]
    ctx, mp = lax.axis_index("ctx"), lax.axis_index("mp")
    n_ctx, n_mp = lax.axis_size("ctx"), lax.axis_size("mp")

    run = RUN[1] * BLOCK
    middle = hidden[run - EDGE : rows - run + EDGE]
    hs_0 = [middle] + [around(middle, "mp", n_mp, s) for s in range(1, n_mp)]
    low = lax.ppermute(hidden[rows - EDGE :], "ctx", [(i, i + 1) for i in range(n_ctx - 1)])
    high = lax.ppermute(hidden[:EDGE], "ctx", [(i + 1, i) for i in range(n_ctx - 1)])
    outer = jnp.concatenate([low, hidden[: run + EDGE], hidden[rows - run - EDGE :], high], axis=0)

    hs_1 = [outer] + [around(outer, "mp", n_mp, s) for s in range(1, n_mp)]
    width = w_x.shape[0]
    place = mp[None].astype(jnp.int32)
    spare = jnp.zeros((width, 128 - 2 * HEADS_HERE), bf16)
    w_1f, w_1r, wdt, w_2f, w_2r = prepare(
        prepare_body, "prepare", n_mp, place, jnp.concatenate([w_x, w_bc, w_z, w_dt, w_dt, spare], axis=1),
        [(width, MIX), (width, MIX), (8, width), (width, MIX), (width, MIX)],
    )

    gain = norm_gain[None, :]
    spread = jnp.asarray(head_spread(), bf16)
    spread_rows = jnp.asarray(row_spread(), bf16)
    meta = jnp.stack([ctx * rows, ctx % 4, (ctx // 4) % 4, (ctx // 16) % 4]).astype(jnp.int32)

    first = (piece_lengths, meta, dt_bias, decay_rate)
    weights_1 = (w_1f, w_1r, wdt, conv_x, conv_bc, spread)
    weights_2 = (w_2f, w_2r, conv_x, conv_bc)

    xb_f, xb_r, cum, dt, fs_0, *middle_states = local_states(0, *first, hs_0, *weights_1)
    arguments = [(piece_lengths, meta, skip_gain, hs_0, *weights_2, xb_f, xb_r, cum, dt)]
    done = [[], []]

    def beside(chunk, part, received):
        new = intra(chunk, part, *arguments[chunk])
        received, new = lax.optimization_barrier((received, tuple(new)))
        done[chunk] += new
        return received

    xb_f, xb_r, cum, dt, fs_1, starts, decays, *pays = local_states(
        1, *first, hs_1, *weights_1, middle_states
    )
    pays, late, late_place = lax.optimization_barrier((pays, w_out, place))
    w_of, w_or = prepare(prepare_out_body, "prepare_out", n_mp, late_place, late, [w_out.shape] * 2)
    arguments.append((piece_lengths, meta, skip_gain, hs_1, *weights_2, xb_f, xb_r, cum, dt))

    def moved(arrays, stride):
        return [lax.ppermute(a, "ctx", digit_perm(n_ctx, stride, s)) for s, a in zip((1, 2, 3), arrays)]

    pre_s, pre_a, pay = join_group(meta, [pays[0]] + beside(0, 0, moved(pays[1:], 1)))

    def swapped(array, bit):
        return [lax.ppermute(array, "ctx", [(i, i ^ bit) for i in range(n_ctx)])]

    low_s, low_a, half = join_pair(False, meta, [pay] + beside(0, 1, swapped(pay, 4)))
    low_s, low_a, top = join_pair(
        True, meta, [half] + beside(0, 2, swapped(half, 8)) + [low_s, low_a]
    )
    back = join_top(meta, beside(1, 0, moved([top] * 3, 16)) + [low_s, low_a, pre_s, pre_a])
    quarters = [back[0]] + moved(back[1:], 1)

    g_f, g_r, sums = gate(
        meta, done[0] + done[1], (fs_0, fs_1), starts, decays, quarters, gain, spread
    )
    all_sums = [sums] + [around(sums, "mp", n_mp, s) for s in range(1, n_mp)]
    tail = (g_f, g_r, all_sums, w_of, w_or, spread_rows)
    own_a, up_a, far_a, down_a = project_out(0, (f32, f32, bf16, bf16), *tail)
    far_a = around(far_a, "mp", n_mp, 1)
    own_b, up_b, far_b, down_b = project_out(1, (f32, bf16, bf16, f32), *tail)
    far_b = around(far_b, "mp", n_mp, n_mp - 1)
    down_a, up_b = around(down_a, "mp", n_mp, n_mp - 1), around(up_b, "mp", n_mp, 1)
    up_a, down_b = join_shares(up_a, far_a, down_b, far_b)
    up_a, down_b = around(up_a, "mp", n_mp, 1), around(down_b, "mp", n_mp, n_mp - 1)
    return last_sum(own_a, down_a, up_a, own_b, up_b, down_b)


def solution(mesh):
    return jax.shard_map(
        shards,
        mesh=mesh,
        in_specs=(
            P("ctx", "mp"),
            P(None, "mp"),
            P(None, "mp"),
            P(),
            P(None, "mp"),
            P(None, "mp"),
            P(),
            P("mp"),
            P("mp"),
            P("mp"),
            P("mp"),
            P("mp", None),
            P(),
        ),
        out_specs=P("ctx", "mp"),
        check_vma=False,
    )
```

```python
import functools

import jax
import jax.numpy as jnp
import numpy as np
from jax import lax
from jax.experimental import pallas as pl
from jax.experimental.pallas import tpu as pltpu
from jax.sharding import PartitionSpec as P

E = 1024
HEAD_DIM = 64
NSTATE = 128
BLOCK = 256
HEADS_HERE = 4
INNER = HEADS_HERE * HEAD_DIM
PIECES = 16
EPSILON = 1e-05
FAR = -1e30
EDGE = 16
MIX = INNER + NSTATE
QUARTER = NSTATE // 4
COUNT = (5, 3)
BLOCKS = 8
HERE = BLOCKS // 2
PARTS = ((0, 0, 2), (0, 2, 3), (1, 0, 3))
PAY = 2 * QUARTER + 16

bf16 = jnp.bfloat16
f32 = jnp.float32


def head_spread():
    out = np.zeros((16, 2 * INNER), np.float32)
    for part in range(2):
        for stream in range(2):
            for h in range(HEADS_HERE):
                first = stream * INNER + h * HEAD_DIM
                out[part * 8 + stream * 4 + h, first : first + HEAD_DIM] = 1.0
    return out


def whole(shape):
    return pl.BlockSpec(shape, lambda *_: (0,) * len(shape))


SMEM = pl.BlockSpec(memory_space=pltpu.SMEM)
VMEM = pl.BlockSpec(memory_space=pltpu.VMEM)


def rows_at(g):
    return pl.ds(pl.multiple_of(g * BLOCK, BLOCK), BLOCK)


def params(mib):
    return pltpu.CompilerParams(vmem_limit_bytes=mib * 1024 * 1024)


def cost(flops, nbytes):
    return pl.CostEstimate(flops=int(flops), bytes_accessed=int(nbytes), transcendentals=0)


def bounds_of(pieces_ref):
    total = pieces_ref[0]
    ends = [total]
    for k in range(1, PIECES):
        total = total + pieces_ref[k]
        ends.append(total)
    return ends


def seg_rows(ends, first):
    shape = (8, BLOCK)
    pos = (
        first - 3 + lax.broadcasted_iota(jnp.int32, shape, 0)
        + lax.broadcasted_iota(jnp.int32, shape, 1)
    )
    seg = jnp.zeros(shape, jnp.int32)
    for end in ends:
        seg = seg + (pos >= end).astype(jnp.int32)
    return seg.astype(f32)


def has_boundary(ends, first):
    found = jnp.int32(0)
    for end in ends:
        found = found + ((end > first - 3) & (end <= first + BLOCK + 2)).astype(jnp.int32)
    return found > 0


def split2(rows):
    high = rows.astype(bf16)
    return jnp.concatenate([high, (rows - high.astype(f32)).astype(bf16)], axis=0)


def rows_to_cols(rows, spread):
    return lax.dot_general(
        split2(rows), spread, (((0,), (0,)), ((), ())), preferred_element_type=f32
    )


def row_of(chunk, g):
    return EDGE + g * BLOCK + (0 if chunk == 0 else (g + 2) // 3 * 2 * EDGE)


def block_of(chunk, g):
    return g + 1 if chunk == 0 else g + (g + 2) // 3 * COUNT[0]


def load_window(hs, chunk, g):
    at = pl.multiple_of(row_of(chunk, g) - EDGE, EDGE)
    return jnp.concatenate([h[pl.ds(at, BLOCK + 2 * EDGE), :] for h in hs], axis=1)


def silu(v):
    half = 0.5 * v
    return half + half * jnp.tanh(half)


def tap_rows(conv_x, conv_bc):
    return [conv_x[:, 0:128], conv_x[:, 128:256], conv_bc[:, 0:128], conv_bc[:, 128:256]]


def conv_tile(scratch, tile, taps, reverse, masks):
    total = None
    for back in range(4):
        first = back if reverse else EDGE - back
        term = scratch[tile, pl.ds(first, BLOCK), :] * taps[3 - back : 4 - back, :]
        if masks is not None and back:
            row = 3 + back if reverse else 3 - back
            term = term * masks[:, row : row + 1]
        total = term if total is None else total + term
    return silu(total).astype(bf16)


def keep_rounded(scratch, proj):
    for tile in range(scratch.shape[0]):
        scratch[tile] = proj[:, tile * 128 : (tile + 1) * 128].astype(bf16).astype(f32)


def per_head(scalars, shape, axis, width):
    head = lax.broadcasted_iota(jnp.int32, shape, axis) // width % HEADS_HERE
    out = jnp.full(shape, scalars[0], f32)
    for h in range(1, HEADS_HERE):
        out = jnp.where(head == h, scalars[h], out)
    return out


def split_rows(decays):
    at = lax.broadcasted_iota(jnp.int32, (16, INNER), 0)
    out = jnp.zeros((16, INNER), f32)
    for k, decay in enumerate(decays):
        high = decay.astype(bf16).astype(f32)
        out = jnp.where(at == 2 * k, high, jnp.where(at == 2 * k + 1, decay - high, out))
    return out.astype(bf16)


def decays_of(rows):
    wide = rows.astype(f32)
    return [wide[2 * k : 2 * k + 1, :] + wide[2 * k + 1 : 2 * k + 2, :] for k in range(2)]


def row_quantities(
    chunk, ends, origin, hs, wdt, dt_bias, rate, spread, cum_o, dt_o, fs_o, same_s, te_s, blockdec
):
    raw = []
    for b in range(COUNT[chunk]):
        at = row_of(chunk, b)
        block = jnp.concatenate([h[at : at + BLOCK, :] for h in hs], axis=1)
        raw.append(
            lax.dot_general(wdt[...], block, (((1,), (1,)), ((), ())), preferred_element_type=f32)
        )
    shape = (8 * COUNT[chunk], BLOCK)
    v = jnp.concatenate(raw, axis=0).astype(bf16).astype(f32) + per_head(dt_bias, shape, 0, 1)
    dt = jnp.maximum(v, 0.0) + jnp.log1p(jnp.exp(-jnp.abs(v)))
    logd = -dt * per_head(rate, shape, 0, 1)
    high = logd.astype(bf16)
    rest = logd - high.astype(f32)
    middle = rest.astype(bf16)
    low = (rest - middle.astype(f32)).astype(bf16)
    row_at = lax.broadcasted_iota(jnp.int32, (BLOCK, BLOCK), 0)
    col_at = lax.broadcasted_iota(jnp.int32, (BLOCK, BLOCK), 1)
    summed = []
    for keep in (row_at <= col_at, row_at >= col_at):
        ones = keep.astype(f32).astype(bf16)
        summed.append(sum(jnp.dot(p, ones, preferred_element_type=f32) for p in (low, middle, high)))
    forward = lax.broadcasted_iota(jnp.int32, (8, BLOCK), 0) < HEADS_HERE
    spread_f = spread[0:8, :].astype(f32)
    for b in range(COUNT[chunk]):
        rows = slice(b * 8, (b + 1) * 8)
        cols = slice(b * BLOCK, (b + 1) * BLOCK)
        cum = jnp.where(forward, summed[0][rows], summed[1][rows])
        dt_b = dt[rows]
        seg = seg_rows(ends, origin + block_of(chunk, b) * BLOCK)
        same_s[b] = (seg == seg[3:4, :]).astype(f32)
        own = jnp.broadcast_to(seg[3:4, :], (8, BLOCK))
        seg_end = jnp.where(forward, seg[3:4, BLOCK - 1 : BLOCK], seg[3:4, 0:1])
        seg_in = jnp.where(forward, seg[2:3, 0:1], seg[4:5, BLOCK - 1 : BLOCK])
        total = jnp.where(forward, cum[:, BLOCK - 1 : BLOCK], cum[:, 0:1])
        to_end = jnp.exp(total - cum) * (own == seg_end).astype(f32) * dt_b
        block_decay = jnp.exp(total) * (seg_end == seg_in).astype(f32)
        cum_o[:, cols] = cum
        dt_o[:, cols] = dt_b
        fs_o[:, cols] = jnp.exp(cum) * (own == seg_in).astype(f32)
        te_s[b] = split2(to_end)
        decay_row = jnp.sum(
            jnp.concatenate([block_decay, block_decay], axis=1) * spread_f, axis=0, keepdims=True
        )
        blockdec[b] = jnp.broadcast_to(decay_row, (8, 2 * INNER))


def k1_body(chunk, pieces, meta, dt_bias, rate, h0, h1, h2, h3, w_f, w_r, wdt, conv_x, conv_bc, spread, *rest):
    if chunk == 0:
        xb_f, xb_r, cum_o, dt_o, fs_o, added, blockdec, sf, sr, same_s, te_s = rest
    else:
        added_0, blockdec_0, *rest = rest
        xb_f, xb_r, cum_o, dt_o, fs_o, start_o, decay_o, p0, p1, p2, p3 = rest[:11]
        sf, sr, same_s, te_s, added, blockdec, total_s = rest[11:]
    ends = bounds_of(pieces)
    hs = (h0, h1, h2, h3)
    row_quantities(
        chunk, ends, meta[0], hs, wdt, dt_bias, rate, spread, cum_o, dt_o, fs_o, same_s, te_s, blockdec
    )

    def states(g, masked):
        window = load_window(hs, chunk, g)
        masks = same_s[g].T if masked else None
        taps = tap_rows(conv_x, conv_bc)
        wide = lax.dot_general(
            te_s[g], spread[...], (((0,), (0,)), ((), ())), preferred_element_type=f32
        )
        keep_rounded(sf, jnp.dot(window[: EDGE + BLOCK], w_f[...], preferred_element_type=f32))
        keep_rounded(sr, jnp.dot(window[EDGE:], w_r[...], preferred_element_type=f32))
        rows = rows_at(g)
        for stream, scratch, ref in ((0, sf, xb_f), (1, sr, xb_r)):
            scaled = []
            for tile in (0, 1):
                x = conv_tile(scratch, tile, taps[tile], stream == 1, masks)
                ref[rows, tile * 128 : (tile + 1) * 128] = x
                at = stream * INNER + tile * 128
                scaled.append((x.astype(f32) * wide[:, at : at + 128]).astype(bf16))
            b = conv_tile(scratch, 2, taps[2], stream == 1, masks)
            ref[rows, INNER:MIX] = b
            added[stream, g] = lax.dot_general(
                b, jnp.concatenate(scaled, axis=1), (((0,), (0,)), ((), ())), preferred_element_type=f32
            )

    @pl.loop(0, COUNT[chunk])
    def _(g):
        crosses = has_boundary(ends, meta[0] + block_of(chunk, g) * BLOCK)
        pl.when(crosses)(lambda: states(g, True))
        pl.when(jnp.logical_not(crosses))(lambda: states(g, False))

    if chunk == 0:
        return
    sources = {block_of(0, k): (added_0, blockdec_0, k) for k in range(COUNT[0])}
    sources.update({block_of(1, k): (added, blockdec, k) for k in range(COUNT[1])})
    decays = []
    for stream in range(2):
        state = jnp.zeros((NSTATE, INNER), f32)
        decay = jnp.ones((1, INNER), f32)
        for step in range(BLOCKS):
            b = step if stream == 0 else BLOCKS - 1 - step
            start_o[stream, b] = state
            decay_o[stream, b] = jnp.broadcast_to(decay, (8, INNER))
            states_ref, decays_ref, k = sources[b]
            d = decays_ref[k, 0:1, stream * INNER : (stream + 1) * INNER]
            state = d * state + states_ref[stream, k]
            decay = decay * d
        total_s[stream] = state
        decays.append(decay)
    rows = split_rows(decays)
    for s, ref in enumerate((p0, p1, p2, p3)):
        at = pl.multiple_of(lax.rem(meta[1] + s, 4) * QUARTER, QUARTER)
        ref[0:QUARTER, :] = total_s[0, pl.ds(at, QUARTER), :].astype(bf16)
        ref[QUARTER : 2 * QUARTER, :] = total_s[1, pl.ds(at, QUARTER), :].astype(bf16)
        ref[2 * QUARTER : PAY, :] = rows


def local_states(chunk, pieces, meta, dt_bias, rate, hs, w_f, w_r, wdt, conv_x, conv_bc, spread, others=()):
    count = COUNT[chunk]
    rows = count * BLOCK
    fixed = [*hs, w_f, w_r, wdt, conv_x, conv_bc, spread, *others]
    added = jax.ShapeDtypeStruct((2, count, NSTATE, INNER), f32)
    blockdec = jax.ShapeDtypeStruct((count, 8, 2 * INNER), f32)
    shapes = [
        jax.ShapeDtypeStruct((rows, MIX), bf16),
        jax.ShapeDtypeStruct((rows, MIX), bf16),
        jax.ShapeDtypeStruct((8, rows), f32),
        jax.ShapeDtypeStruct((8, rows), f32),
        jax.ShapeDtypeStruct((8, rows), f32),
    ]
    scratch = [
        pltpu.VMEM((MIX // 128, EDGE + BLOCK, 128), f32),
        pltpu.VMEM((MIX // 128, EDGE + BLOCK, 128), f32),
        pltpu.VMEM((count, 8, BLOCK), f32),
        pltpu.VMEM((count, 16, BLOCK), bf16),
    ]
    if chunk == 0:
        shapes += [added, blockdec]
    else:
        shapes += [
            jax.ShapeDtypeStruct((2, BLOCKS, NSTATE, INNER), f32),
            jax.ShapeDtypeStruct((2, BLOCKS, 8, INNER), f32),
        ] + [jax.ShapeDtypeStruct((PAY, INNER), bf16)] * 4
        scratch += [pltpu.VMEM(a.shape, f32) for a in (added, blockdec)]
        scratch += [pltpu.VMEM((2, NSTATE, INNER), f32)]
    return pl.pallas_call(
        functools.partial(k1_body, chunk),
        in_specs=[SMEM] * 4 + [VMEM] * len(fixed),
        out_specs=[VMEM] * len(shapes),
        out_shape=shapes,
        scratch_shapes=scratch,
        compiler_params=params(24),
        cost_estimate=cost(rows * 6e6, rows * 4000),
        name="local_states",
    )(pieces, meta, dt_bias, rate, *fixed)


def k2_body(
    chunk, base, count, pieces, meta, skip_gain, h0, h1, h2, h3, w_f, w_r, conv_x, conv_bc,
    xb_f, xb_r, cum_i, dt_i, c_f, c_r, y_f, y_r, z_f, z_r, sf, sr, open_mask,
):
    ends = bounds_of(pieces)
    row_at = lax.broadcasted_iota(jnp.int32, (BLOCK, BLOCK), 0)
    col_at = lax.broadcasted_iota(jnp.int32, (BLOCK, BLOCK), 1)
    half = BLOCK // 2

    open_mask[0] = jnp.where(row_at >= col_at, 0.0, FAR)
    open_mask[1] = jnp.where(row_at <= col_at, 0.0, FAR)

    def mix(step, masked):
        g = step + base
        first = meta[0] + block_of(chunk, g) * BLOCK
        here, there = rows_at(step), rows_at(g)
        window = load_window((h0, h1, h2, h3), chunk, g)
        masks = None
        if masked:
            seg = seg_rows(ends, first)
            masks = (seg == seg[3:4, :]).astype(f32).T
            together = seg.T[:, 3:4] == seg[3:4, :]
            open_mask[2] = jnp.where(together & (row_at >= col_at), 0.0, FAR)
            open_mask[3] = jnp.where(together & (row_at <= col_at), 0.0, FAR)
        proj_f = jnp.dot(window[: EDGE + BLOCK], w_f[...], preferred_element_type=f32)
        proj_r = jnp.dot(window[EDGE:], w_r[...], preferred_element_type=f32)
        keep_rounded(sf, proj_f)
        keep_rounded(sr, proj_r)
        z_f[here, :] = silu(proj_f[EDGE:, NSTATE:].astype(bf16).astype(f32))
        z_r[here, :] = silu(proj_r[0:BLOCK, NSTATE:].astype(bf16).astype(f32))
        taps = tap_rows(conv_x, conv_bc)[3]
        cum = cum_i[:, there]
        cum_t = cum.T
        log_dt = jnp.log(dt_i[:, there]) - cum
        lane_head = lax.broadcasted_iota(jnp.int32, (BLOCK, INNER), 1) // HEAD_DIM
        skip = per_head(skip_gain, (1, INNER), 1, HEAD_DIM)
        for stream, xb, scratch, c_ref, y_ref in ((0, xb_f, sf, c_f, y_f), (1, xb_r, sr, c_r, y_r)):
            c_rows = conv_tile(scratch, 0, taps, stream == 1, masks)
            c_ref[here, :] = c_rows
            x = xb[there, 0:INNER]
            b = xb[there, INNER:MIX]
            heads = [jnp.where(lane_head == h, x, jnp.zeros_like(x)) for h in range(HEADS_HERE)]
            for part in range(2):
                rows = slice(part * half, (part + 1) * half)
                if stream == 0:
                    cols = slice(0, half) if part == 0 else slice(0, BLOCK)
                else:
                    cols = slice(0, BLOCK) if part == 0 else slice(half, BLOCK)
                scores = lax.dot_general(
                    c_rows[rows, :], b[cols, :], (((1,), (1,)), ((), ())), preferred_element_type=f32
                )
                mask = open_mask[(2 if masked else 0) + stream, rows, cols]
                total = x[rows, :].astype(f32) * skip
                for h in range(HEADS_HERE):
                    at = stream * HEADS_HERE + h
                    gap = (cum_t[rows, at : at + 1] + log_dt[at : at + 1, cols]) + mask
                    weight = (jnp.exp(gap) * scores).astype(bf16)
                    total = total + jnp.dot(weight, heads[h][cols, :], preferred_element_type=f32)
                at = pl.multiple_of(step * BLOCK + part * half, half)
                y_ref[pl.ds(at, half), :] = total

    @pl.loop(0, count)
    def _(step):
        crosses = has_boundary(ends, meta[0] + block_of(chunk, step + base) * BLOCK)
        pl.when(crosses)(lambda: mix(step, True))
        pl.when(jnp.logical_not(crosses))(lambda: mix(step, False))


def intra(chunk, base, count, pieces, meta, skip_gain, hs, w_f, w_r, conv_x, conv_bc, xb_f, xb_r, cum, dt):
    rows = count * BLOCK
    arrays = [*hs, w_f, w_r, conv_x, conv_bc, xb_f, xb_r, cum, dt]
    return pl.pallas_call(
        functools.partial(k2_body, chunk, base, count),
        in_specs=[SMEM] * 3 + [VMEM] * len(arrays),
        out_specs=[VMEM] * 6,
        out_shape=[jax.ShapeDtypeStruct((rows, NSTATE), bf16)] * 2
        + [jax.ShapeDtypeStruct((rows, INNER), f32)] * 4,
        scratch_shapes=[
            pltpu.VMEM((1, EDGE + BLOCK, 128), f32),
            pltpu.VMEM((1, EDGE + BLOCK, 128), f32),
            pltpu.VMEM((4, BLOCK, BLOCK), f32),
        ],
        compiler_params=params(16),
        cost_estimate=cost(rows * 5e6, rows * 5000),
        name="intra",
    )(pieces, meta, skip_gain, *arrays)


def state_rows(ref, stream):
    return ref[stream * QUARTER : (stream + 1) * QUARTER, :].astype(f32)


def put_payload(ref, states, decays):
    for stream in range(2):
        ref[stream * QUARTER : (stream + 1) * QUARTER, :] = states[stream].astype(bf16)
    ref[2 * QUARTER : PAY, :] = split_rows(decays)


def group_body(meta, own, r1, r2, r3, pre_s, pre_a, pay, stage):
    me = meta[1]
    for s, ref in enumerate((own, r1, r2, r3)):
        stage[lax.rem(me - s + 4, 4)] = ref[...]
    states, decays = [], []
    for stream in range(2):
        state = jnp.zeros((QUARTER, INNER), f32)
        decay = jnp.ones((1, INNER), f32)
        for step in range(4):
            k = step if stream == 0 else 3 - step
            pre_s[k, stream] = state
            pre_a[k, stream] = jnp.broadcast_to(decay, (8, INNER))
            one = stage[k]
            d = decays_of(one[2 * QUARTER :])[stream]
            state = d * state + one[stream * QUARTER : (stream + 1) * QUARTER].astype(f32)
            decay = decay * d
        states.append(state)
        decays.append(decay)
    put_payload(pay, states, decays)


def before_digit(place, stream, got):
    low_s, low_a = jnp.zeros((QUARTER, INNER), f32), jnp.ones((1, INNER), f32)
    for s in (1, 2, 3):
        there = s <= place
        state, decay = got[s if stream == 0 else 4 - s]
        low_s = jnp.where(there, low_s + low_a * state, low_s)
        low_a = jnp.where(there, low_a * decay, low_a)
    return low_s, low_a


def middle_body(meta, own, r1, r2, r3, low_o, low_ao, pay):
    digit = meta[2]
    states, decays = [], []
    rows = [decays_of(r[2 * QUARTER : PAY, :]) for r in (own, r1, r2, r3)]
    for stream in range(2):
        got = [(state_rows(r, stream), rows[s][stream]) for s, r in enumerate((own, r1, r2, r3))]
        place = digit if stream == 0 else 3 - digit
        low_s, low_a = before_digit(place, stream, got)
        low_o[stream] = low_s
        low_ao[stream] = jnp.broadcast_to(low_a, (8, INNER))
        total_s, total_a = got[0][1] * low_s + got[0][0], got[0][1] * low_a
        for s in (3, 2, 1):
            there = s > place
            state, decay = got[s if stream == 0 else 4 - s]
            total_s = jnp.where(there, decay * total_s + state, total_s)
            total_a = jnp.where(there, decay * total_a, total_a)
        states.append(total_s)
        decays.append(total_a)
    put_payload(pay, states, decays)


def top_body(meta, r1, r2, r3, low_i, low_ai, pre_s, pre_a, *outs):
    digit = meta[3]
    rows = [None] + [decays_of(r[2 * QUARTER : PAY, :]) for r in (r1, r2, r3)]
    for stream in range(2):
        got = [None] + [
            (state_rows(r, stream), rows[s + 1][stream]) for s, r in enumerate((r1, r2, r3))
        ]
        place = digit if stream == 0 else 3 - digit
        top_s, _ = before_digit(place, stream, got)
        group_s = low_ai[stream, 0:1, :] * top_s + low_i[stream]
        for s, ref in enumerate(outs):
            k = lax.rem(meta[1] + s, 4)
            member = pre_a[k, stream][0:1, :] * group_s + pre_s[k, stream]
            ref[stream * QUARTER : (stream + 1) * QUARTER, :] = member.astype(bf16)


def small_call(body, name, meta, arrays, shapes, scratch=()):
    return pl.pallas_call(
        body,
        in_specs=[SMEM] + [VMEM] * len(arrays),
        out_specs=[VMEM] * len(shapes),
        out_shape=shapes,
        scratch_shapes=list(scratch),
        compiler_params=params(6),
        cost_estimate=cost(2e6, 1e6),
        name=name,
    )(meta, *arrays)


PAYLOAD = jax.ShapeDtypeStruct((PAY, INNER), bf16)


def join_group(meta, arrays):
    shapes = [
        jax.ShapeDtypeStruct((4, 2, QUARTER, INNER), f32),
        jax.ShapeDtypeStruct((4, 2, 8, INNER), f32),
        PAYLOAD,
    ]
    return small_call(group_body, "join_group", meta, arrays, shapes, [pltpu.VMEM((4, PAY, INNER), bf16)])


def join_middle(meta, arrays):
    shapes = [
        jax.ShapeDtypeStruct((2, QUARTER, INNER), f32),
        jax.ShapeDtypeStruct((2, 8, INNER), f32),
        PAYLOAD,
    ]
    return small_call(middle_body, "join_middle", meta, arrays, shapes)


def join_top(meta, arrays):
    shapes = [jax.ShapeDtypeStruct((2 * QUARTER, INNER), bf16)] * 4
    return small_call(top_body, "join_top", meta, arrays, shapes)


def k3_body(meta, *refs):
    parts, refs = refs[: 6 * len(PARTS)], refs[6 * len(PARTS) :]
    fs, (starts, decays, q0, q1, q2, q3, gain, spread, g_f, g_r, sums, s_in) = refs[:2], refs[2:]
    for s, ref in enumerate((q0, q1, q2, q3)):
        at = pl.multiple_of(lax.rem(meta[1] - s + 4, 4) * QUARTER, QUARTER)
        for stream in range(2):
            s_in[stream, pl.ds(at, QUARTER), :] = state_rows(ref, stream)
    for part, (chunk, base, count) in enumerate(PARTS):
        c, y, z = (parts[6 * part + n : 6 * part + n + 2] for n in (0, 2, 4))
        for at in range(count):
            k = base + at
            b = block_of(chunk, k)
            to = slice(b * BLOCK, (b + 1) * BLOCK)
            rows = slice(at * BLOCK, (at + 1) * BLOCK)
            wide = rows_to_cols(fs[chunk][:, k * BLOCK : (k + 1) * BLOCK], spread[...])
            for stream, g_ref in ((0, g_f), (1, g_r)):
                state = starts[stream, b] + decays[stream, b, 0:1, :] * s_in[stream]
                carried = jnp.dot(c[stream][rows, :], state.astype(bf16), preferred_element_type=f32)
                mixed = y[stream][rows, :] + carried * wide[:, stream * INNER : (stream + 1) * INNER]
                gated = mixed * z[stream][rows, :]
                square = gated * gated
                sums[stream : stream + 1, to] = jnp.sum(
                    (square[:, 0:128] + square[:, 128:256]).T, axis=0, keepdims=True
                )
                g_ref[to, :] = (gated * gain[...]).astype(bf16)


def gate(meta, locals_, fs, starts, decays, quarters, gain, spread):
    m = BLOCKS * BLOCK
    arrays = [*locals_, *fs, starts, decays, *quarters, gain, spread]
    return pl.pallas_call(
        k3_body,
        in_specs=[SMEM] + [VMEM] * len(arrays),
        out_specs=[VMEM] * 3,
        out_shape=[
            jax.ShapeDtypeStruct((m, INNER), bf16),
            jax.ShapeDtypeStruct((m, INNER), bf16),
            jax.ShapeDtypeStruct((2, m), f32),
        ],
        scratch_shapes=[pltpu.VMEM((2, NSTATE, INNER), f32)],
        compiler_params=params(12),
        cost_estimate=cost(m * 5e5, m * 6000),
        name="gate",
    )(meta, *arrays)


def k4_body(half, g_f, g_r, s0, s1, s2, s3, w_f, w_r, spread, o0, o1, o2, o3):
    for k in range(HERE):
        rows = slice((half * HERE + k) * BLOCK, (half * HERE + k + 1) * BLOCK)
        total = (s0[:, rows] + s1[:, rows]) + (s2[:, rows] + s3[:, rows])
        scale = lax.rsqrt(total / E + EPSILON)
        scale = jnp.concatenate([scale, jnp.zeros((6, BLOCK), f32)], axis=0)
        wide = rows_to_cols(scale, spread[...])
        out_f = jnp.dot(g_f[rows, :], w_f[...], preferred_element_type=f32)
        out_r = jnp.dot(g_r[rows, :], w_r[...], preferred_element_type=f32)
        for s, ref in enumerate((o0, o1, o2, o3)):
            cols = slice(s * 128, (s + 1) * 128)
            part = out_f[:, cols] * wide[:, 0:128] + out_r[:, cols] * wide[:, 128:256]
            ref[k * BLOCK : (k + 1) * BLOCK, :] = part.astype(ref.dtype)


def project_out(half, kinds, g_f, g_r, sums, w_f, w_r, spread):
    m = HERE * BLOCK
    arrays = [g_f, g_r, *sums, w_f, w_r, spread]
    return pl.pallas_call(
        functools.partial(k4_body, half),
        in_specs=[VMEM] * len(arrays),
        out_specs=[VMEM] * 4,
        out_shape=[jax.ShapeDtypeStruct((m, 128), kind) for kind in kinds],
        compiler_params=params(12),
        cost_estimate=cost(m * 1e6, m * 3000),
        name="project_out",
    )(*arrays)


def join_body(a1, b1, a2, b2, o1, o2):
    o1[...] = (a1[...] + b1[...].astype(f32)).astype(bf16)
    o2[...] = (a2[...] + b2[...].astype(f32)).astype(bf16)


def join_shares(a1, b1, a2, b2):
    arrays = (a1, b1, a2, b2)
    shapes = [jax.ShapeDtypeStruct(a1.shape, bf16)] * 2
    return pl.pallas_call(
        join_body,
        in_specs=[VMEM] * len(arrays),
        out_specs=[VMEM] * len(shapes),
        out_shape=shapes,
        compiler_params=params(8),
        cost_estimate=cost(1e6, 3e6),
        name="join_shares",
    )(*arrays)


def last_body(a0, a1, a2, b0, b1, b2, out):
    for k, (own, one, other) in enumerate(((a0, a1, a2), (b0, b1, b2))):
        @pl.when(pl.program_id(0) == k)
        def _():
            out[...] = (own[...] + one[...].astype(f32) + other[...].astype(f32)).astype(bf16)


def last_sum(*arrays):
    m = HERE * BLOCK
    return pl.pallas_call(
        last_body,
        grid=(2,),
        in_specs=[whole(a.shape) for a in arrays],
        out_specs=pl.BlockSpec((m, 128), lambda g: (g, 0)),
        out_shape=jax.ShapeDtypeStruct((2 * m, 128), bf16),
        compiler_params=params(8),
        cost_estimate=cost(1e6, 3e6),
        name="last_sum",
    )(*arrays)


def orders(mp, n_mp, width):
    here = width // n_mp
    shape = (width, width)
    row = lax.broadcasted_iota(jnp.int32, shape, 0)
    col = lax.broadcasted_iota(jnp.int32, shape, 1)
    place = lax.rem(mp - row // here + n_mp, n_mp) * here + lax.rem(row, here)
    goal = lax.rem(mp + col // here, n_mp) * here + lax.rem(col, here)
    return [
        keep.astype(f32).astype(bf16)
        for keep in (place == col, width - 1 - place == col, goal == row, width - 1 - goal == row)
    ]


def prepare_body(n_mp, mp, w, o_f, o_r, o_dt, q_f, q_r):
    pick_f, pick_r, _, _ = orders(mp[0], n_mp, w.shape[0])
    moved = [jnp.dot(pick, w[...], preferred_element_type=f32) for pick in (pick_f, pick_r)]
    for rows, first, second in ((moved[0], o_f, q_f), (moved[1], o_r, q_r)):
        first[...] = rows[:, 0:MIX].astype(bf16)
        second[...] = rows[:, MIX : 2 * MIX].astype(bf16)
    lane = lax.broadcasted_iota(jnp.int32, (w.shape[0], 128), 1)
    steps = jnp.where(lane < HEADS_HERE, moved[0][:, 2 * MIX :], moved[1][:, 2 * MIX :])
    o_dt[...] = steps.T[0:8, :].astype(bf16)


def prepare_out_body(n_mp, mp, w_out, p_f, p_r):
    _, _, out_f, out_r = orders(mp[0], n_mp, w_out.shape[1])
    p_f[...] = jnp.dot(w_out[...], out_f, preferred_element_type=f32).astype(bf16)
    p_r[...] = jnp.dot(w_out[...], out_r, preferred_element_type=f32).astype(bf16)


def prepare(body, name, n_mp, mp, w, shapes):
    return pl.pallas_call(
        functools.partial(body, n_mp),
        in_specs=[SMEM, VMEM],
        out_specs=[VMEM] * len(shapes),
        out_shape=[jax.ShapeDtypeStruct(a, bf16) for a in shapes],
        compiler_params=params(16),
        cost_estimate=cost(1e9, 3e6),
        name=name,
    )(mp, w)


def row_spread():
    out = np.zeros((16, 256), np.float32)
    for part in range(2):
        out[part * 8, 0:128] = 1.0
        out[part * 8 + 1, 128:256] = 1.0
    return out


def around(array, axis, count, shift):
    return lax.ppermute(array, axis, [(i, (i + shift) % count) for i in range(count)])


def digit_perm(count, stride, shift):
    pairs = []
    for i in range(count):
        d = (i // stride) % 4
        pairs.append((i, i + (((d + shift) % 4) - d) * stride))
    return pairs


def shards(
    hidden, w_x, w_z, w_bc, w_dt, conv_x, conv_bc, dt_bias, decay_rate, skip_gain, norm_gain, w_out,
    piece_lengths,
):
    rows = hidden.shape[0]
    ctx, mp = lax.axis_index("ctx"), lax.axis_index("mp")
    n_ctx, n_mp = lax.axis_size("ctx"), lax.axis_size("mp")

    run, last = BLOCK, (1 + COUNT[0]) * BLOCK
    middle = hidden[run - EDGE : last + EDGE]
    hs_0 = [middle] + [around(middle, "mp", n_mp, s) for s in range(1, n_mp)]
    low = lax.ppermute(hidden[rows - EDGE :], "ctx", [(i, i + 1) for i in range(n_ctx - 1)])
    high = lax.ppermute(hidden[:EDGE], "ctx", [(i + 1, i) for i in range(n_ctx - 1)])
    outer = jnp.concatenate([low, hidden[: run + EDGE], hidden[last - EDGE :], high], axis=0)

    hs_1 = [outer] + [around(outer, "mp", n_mp, s) for s in range(1, n_mp)]
    width = w_x.shape[0]
    place = mp[None].astype(jnp.int32)
    spare = jnp.zeros((width, 128 - 2 * HEADS_HERE), bf16)
    w_1f, w_1r, wdt, w_2f, w_2r = prepare(
        prepare_body, "prepare", n_mp, place, jnp.concatenate([w_x, w_bc, w_z, w_dt, w_dt, spare], axis=1),
        [(width, MIX), (width, MIX), (8, width), (width, MIX), (width, MIX)],
    )

    gain = norm_gain[None, :]
    spread = jnp.asarray(head_spread(), bf16)
    spread_rows = jnp.asarray(row_spread(), bf16)
    meta = jnp.stack([ctx * rows, ctx % 4, (ctx // 4) % 4, (ctx // 16) % 4]).astype(jnp.int32)

    first = (piece_lengths, meta, dt_bias, decay_rate)
    weights_1 = (w_1f, w_1r, wdt, conv_x, conv_bc, spread)
    weights_2 = (w_2f, w_2r, conv_x, conv_bc)

    xb_f, xb_r, cum, dt, fs_0, *middle_states = local_states(0, *first, hs_0, *weights_1)
    arguments = [(piece_lengths, meta, skip_gain, hs_0, *weights_2, xb_f, xb_r, cum, dt)]
    done = []

    def beside(part, received):
        new = intra(*PARTS[part], *arguments[PARTS[part][0]])
        received, new = lax.optimization_barrier((received, tuple(new)))
        done.extend(new)
        return received

    xb_f, xb_r, cum, dt, fs_1, starts, decays, *pays = local_states(
        1, *first, hs_1, *weights_1, middle_states
    )
    pays, late, late_place = lax.optimization_barrier((pays, w_out, place))
    w_of, w_or = prepare(prepare_out_body, "prepare_out", n_mp, late_place, late, [w_out.shape] * 2)
    arguments.append((piece_lengths, meta, skip_gain, hs_1, *weights_2, xb_f, xb_r, cum, dt))

    def moved(arrays, stride):
        return [lax.ppermute(a, "ctx", digit_perm(n_ctx, stride, s)) for s, a in zip((1, 2, 3), arrays)]

    pre_s, pre_a, pay = join_group(meta, [pays[0]] + beside(0, moved(pays[1:], 1)))
    low_s, low_a, top = join_middle(meta, [pay] + beside(1, moved([pay] * 3, 4)))
    back = join_top(meta, moved([top] * 3, 16) + [low_s, low_a, pre_s, pre_a])
    quarters = [back[0]] + beside(2, moved(back[1:], 1))

    g_f, g_r, sums = gate(
        meta, done, (fs_0, fs_1), starts, decays, quarters, gain, spread
    )
    all_sums = [sums] + [around(sums, "mp", n_mp, s) for s in range(1, n_mp)]
    tail = (g_f, g_r, all_sums, w_of, w_or, spread_rows)
    own_a, up_a, far_a, down_a = project_out(0, (f32, f32, bf16, bf16), *tail)
    far_a = around(far_a, "mp", n_mp, 1)
    own_b, up_b, far_b, down_b = project_out(1, (f32, bf16, bf16, f32), *tail)
    far_b = around(far_b, "mp", n_mp, n_mp - 1)
    down_a, up_b = around(down_a, "mp", n_mp, n_mp - 1), around(up_b, "mp", n_mp, 1)
    up_a, down_b = join_shares(up_a, far_a, down_b, far_b)
    up_a, down_b = around(up_a, "mp", n_mp, 1), around(down_b, "mp", n_mp, n_mp - 1)
    return last_sum(own_a, down_a, up_a, own_b, up_b, down_b)


def solution(mesh):
    return jax.shard_map(
        shards,
        mesh=mesh,
        in_specs=(
            P("ctx", "mp"),
            P(None, "mp"),
            P(None, "mp"),
            P(),
            P(None, "mp"),
            P(None, "mp"),
            P(),
            P("mp"),
            P("mp"),
            P("mp"),
            P("mp"),
            P("mp", None),
            P(),
        ),
        out_specs=P("ctx", "mp"),
        check_vma=False,
    )
```

```python
import functools

import jax
import jax.numpy as jnp
import numpy as np
from jax import lax
from jax.experimental import pallas as pl
from jax.experimental.pallas import tpu as pltpu
from jax.sharding import PartitionSpec as P

E = 1024
HEAD_DIM = 64
NSTATE = 128
BLOCK = 256
HEADS_HERE = 4
INNER = HEADS_HERE * HEAD_DIM
PIECES = 16
EPSILON = 1e-05
FAR = -1e30
EDGE = 16
MIX = INNER + NSTATE
QUARTER = NSTATE // 4
COUNT = (5, 3)
BLOCKS = 8
HERE = BLOCKS // 2
PARTS = ((0, 0, 2), (0, 2, 3), (1, 0, 2), (1, 2, 1))
PAY = 2 * QUARTER + 16

bf16 = jnp.bfloat16
f32 = jnp.float32


def head_spread():
    out = np.zeros((16, 2 * INNER), np.float32)
    for part in range(2):
        for stream in range(2):
            for h in range(HEADS_HERE):
                first = stream * INNER + h * HEAD_DIM
                out[part * 8 + stream * 4 + h, first : first + HEAD_DIM] = 1.0
    return out


def whole(shape):
    return pl.BlockSpec(shape, lambda *_: (0,) * len(shape))


SMEM = pl.BlockSpec(memory_space=pltpu.SMEM)
VMEM = pl.BlockSpec(memory_space=pltpu.VMEM)


def rows_at(g):
    return pl.ds(pl.multiple_of(g * BLOCK, BLOCK), BLOCK)


def params(mib):
    return pltpu.CompilerParams(vmem_limit_bytes=mib * 1024 * 1024)


def cost(flops, nbytes):
    return pl.CostEstimate(flops=int(flops), bytes_accessed=int(nbytes), transcendentals=0)


def bounds_of(pieces_ref):
    total = pieces_ref[0]
    ends = [total]
    for k in range(1, PIECES):
        total = total + pieces_ref[k]
        ends.append(total)
    return ends


def seg_rows(ends, first):
    shape = (8, BLOCK)
    pos = (
        first - 3 + lax.broadcasted_iota(jnp.int32, shape, 0)
        + lax.broadcasted_iota(jnp.int32, shape, 1)
    )
    seg = jnp.zeros(shape, jnp.int32)
    for end in ends:
        seg = seg + (pos >= end).astype(jnp.int32)
    return seg.astype(f32)


def has_boundary(ends, first):
    found = jnp.int32(0)
    for end in ends:
        found = found + ((end > first - 3) & (end <= first + BLOCK + 2)).astype(jnp.int32)
    return found > 0


def split2(rows):
    high = rows.astype(bf16)
    return jnp.concatenate([high, (rows - high.astype(f32)).astype(bf16)], axis=0)


def rows_to_cols(rows, spread):
    return lax.dot_general(
        split2(rows), spread, (((0,), (0,)), ((), ())), preferred_element_type=f32
    )


def row_of(chunk, g):
    return EDGE + g * BLOCK + (0 if chunk == 0 else (g + 2) // 3 * 2 * EDGE)


def block_of(chunk, g):
    return g + 1 if chunk == 0 else g + (g + 2) // 3 * COUNT[0]


def load_window(hs, chunk, g):
    at = pl.multiple_of(row_of(chunk, g) - EDGE, EDGE)
    return jnp.concatenate([h[pl.ds(at, BLOCK + 2 * EDGE), :] for h in hs], axis=1)


def silu(v):
    half = 0.5 * v
    return half + half * jnp.tanh(half)


def tap_rows(conv_x, conv_bc):
    return [conv_x[:, 0:128], conv_x[:, 128:256], conv_bc[:, 0:128], conv_bc[:, 128:256]]


def conv_tile(scratch, tile, taps, reverse, masks):
    total = None
    for back in range(4):
        first = back if reverse else EDGE - back
        term = scratch[tile, pl.ds(first, BLOCK), :] * taps[3 - back : 4 - back, :]
        if masks is not None and back:
            row = 3 + back if reverse else 3 - back
            term = term * masks[:, row : row + 1]
        total = term if total is None else total + term
    return silu(total).astype(bf16)


def keep_rounded(scratch, proj):
    for tile in range(scratch.shape[0]):
        scratch[tile] = proj[:, tile * 128 : (tile + 1) * 128].astype(bf16).astype(f32)


def per_head(scalars, shape, axis, width):
    head = lax.broadcasted_iota(jnp.int32, shape, axis) // width % HEADS_HERE
    out = jnp.full(shape, scalars[0], f32)
    for h in range(1, HEADS_HERE):
        out = jnp.where(head == h, scalars[h], out)
    return out


def split_rows(decays):
    at = lax.broadcasted_iota(jnp.int32, (16, INNER), 0)
    out = jnp.zeros((16, INNER), f32)
    for k, decay in enumerate(decays):
        high = decay.astype(bf16).astype(f32)
        out = jnp.where(at == 2 * k, high, jnp.where(at == 2 * k + 1, decay - high, out))
    return out.astype(bf16)


def decays_of(rows):
    wide = rows.astype(f32)
    return [wide[2 * k : 2 * k + 1, :] + wide[2 * k + 1 : 2 * k + 2, :] for k in range(2)]


def row_quantities(
    chunk, ends, origin, hs, wdt, dt_bias, rate, spread, cum_o, dt_o, fs_o, same_s, te_s, blockdec
):
    raw = []
    for b in range(COUNT[chunk]):
        at = row_of(chunk, b)
        block = jnp.concatenate([h[at : at + BLOCK, :] for h in hs], axis=1)
        raw.append(
            lax.dot_general(wdt[...], block, (((1,), (1,)), ((), ())), preferred_element_type=f32)
        )
    shape = (8 * COUNT[chunk], BLOCK)
    v = jnp.concatenate(raw, axis=0).astype(bf16).astype(f32) + per_head(dt_bias, shape, 0, 1)
    dt = jnp.maximum(v, 0.0) + jnp.log1p(jnp.exp(-jnp.abs(v)))
    logd = -dt * per_head(rate, shape, 0, 1)
    high = logd.astype(bf16)
    rest = logd - high.astype(f32)
    middle = rest.astype(bf16)
    low = (rest - middle.astype(f32)).astype(bf16)
    row_at = lax.broadcasted_iota(jnp.int32, (BLOCK, BLOCK), 0)
    col_at = lax.broadcasted_iota(jnp.int32, (BLOCK, BLOCK), 1)
    summed = []
    for keep in (row_at <= col_at, row_at >= col_at):
        ones = keep.astype(f32).astype(bf16)
        summed.append(sum(jnp.dot(p, ones, preferred_element_type=f32) for p in (low, middle, high)))
    forward = lax.broadcasted_iota(jnp.int32, (8, BLOCK), 0) < HEADS_HERE
    spread_f = spread[0:8, :].astype(f32)
    for b in range(COUNT[chunk]):
        rows = slice(b * 8, (b + 1) * 8)
        cols = slice(b * BLOCK, (b + 1) * BLOCK)
        cum = jnp.where(forward, summed[0][rows], summed[1][rows])
        dt_b = dt[rows]
        seg = seg_rows(ends, origin + block_of(chunk, b) * BLOCK)
        same_s[b] = (seg == seg[3:4, :]).astype(f32)
        own = jnp.broadcast_to(seg[3:4, :], (8, BLOCK))
        seg_end = jnp.where(forward, seg[3:4, BLOCK - 1 : BLOCK], seg[3:4, 0:1])
        seg_in = jnp.where(forward, seg[2:3, 0:1], seg[4:5, BLOCK - 1 : BLOCK])
        total = jnp.where(forward, cum[:, BLOCK - 1 : BLOCK], cum[:, 0:1])
        to_end = jnp.exp(total - cum) * (own == seg_end).astype(f32) * dt_b
        block_decay = jnp.exp(total) * (seg_end == seg_in).astype(f32)
        cum_o[:, cols] = cum
        dt_o[:, cols] = dt_b
        fs_o[:, cols] = jnp.exp(cum) * (own == seg_in).astype(f32)
        te_s[b] = split2(to_end)
        decay_row = jnp.sum(
            jnp.concatenate([block_decay, block_decay], axis=1) * spread_f, axis=0, keepdims=True
        )
        blockdec[b] = jnp.broadcast_to(decay_row, (8, 2 * INNER))


def k1_body(chunk, pieces, meta, dt_bias, rate, h0, h1, h2, h3, w_f, w_r, wdt, conv_x, conv_bc, spread, *rest):
    if chunk == 0:
        xb_f, xb_r, cum_o, dt_o, fs_o, added, blockdec, sf, sr, same_s, te_s = rest
    else:
        added_0, blockdec_0, *rest = rest
        xb_f, xb_r, cum_o, dt_o, fs_o, start_o, decay_o, p0, p1, p2, p3 = rest[:11]
        sf, sr, same_s, te_s, added, blockdec, total_s = rest[11:]
    ends = bounds_of(pieces)
    hs = (h0, h1, h2, h3)
    row_quantities(
        chunk, ends, meta[0], hs, wdt, dt_bias, rate, spread, cum_o, dt_o, fs_o, same_s, te_s, blockdec
    )

    def states(g, masked):
        window = load_window(hs, chunk, g)
        masks = same_s[g].T if masked else None
        taps = tap_rows(conv_x, conv_bc)
        wide = lax.dot_general(
            te_s[g], spread[...], (((0,), (0,)), ((), ())), preferred_element_type=f32
        )
        keep_rounded(sf, jnp.dot(window[: EDGE + BLOCK], w_f[...], preferred_element_type=f32))
        keep_rounded(sr, jnp.dot(window[EDGE:], w_r[...], preferred_element_type=f32))
        rows = rows_at(g)
        for stream, scratch, ref in ((0, sf, xb_f), (1, sr, xb_r)):
            scaled = []
            for tile in (0, 1):
                x = conv_tile(scratch, tile, taps[tile], stream == 1, masks)
                ref[rows, tile * 128 : (tile + 1) * 128] = x
                at = stream * INNER + tile * 128
                scaled.append((x.astype(f32) * wide[:, at : at + 128]).astype(bf16))
            b = conv_tile(scratch, 2, taps[2], stream == 1, masks)
            ref[rows, INNER:MIX] = b
            added[stream, g] = lax.dot_general(
                b, jnp.concatenate(scaled, axis=1), (((0,), (0,)), ((), ())), preferred_element_type=f32
            )

    @pl.loop(0, COUNT[chunk])
    def _(g):
        crosses = has_boundary(ends, meta[0] + block_of(chunk, g) * BLOCK)
        pl.when(crosses)(lambda: states(g, True))
        pl.when(jnp.logical_not(crosses))(lambda: states(g, False))

    if chunk == 0:
        return
    sources = {block_of(0, k): (added_0, blockdec_0, k) for k in range(COUNT[0])}
    sources.update({block_of(1, k): (added, blockdec, k) for k in range(COUNT[1])})
    decays = []
    for stream in range(2):
        state = jnp.zeros((NSTATE, INNER), f32)
        decay = jnp.ones((1, INNER), f32)
        for step in range(BLOCKS):
            b = step if stream == 0 else BLOCKS - 1 - step
            start_o[stream, b] = state
            decay_o[stream, b] = jnp.broadcast_to(decay, (8, INNER))
            states_ref, decays_ref, k = sources[b]
            d = decays_ref[k, 0:1, stream * INNER : (stream + 1) * INNER]
            state = d * state + states_ref[stream, k]
            decay = decay * d
        total_s[stream] = state
        decays.append(decay)
    rows = split_rows(decays)
    for s, ref in enumerate((p0, p1, p2, p3)):
        at = pl.multiple_of(lax.rem(meta[1] + s, 4) * QUARTER, QUARTER)
        ref[0:QUARTER, :] = total_s[0, pl.ds(at, QUARTER), :].astype(bf16)
        ref[QUARTER : 2 * QUARTER, :] = total_s[1, pl.ds(at, QUARTER), :].astype(bf16)
        ref[2 * QUARTER : PAY, :] = rows


def local_states(chunk, pieces, meta, dt_bias, rate, hs, w_f, w_r, wdt, conv_x, conv_bc, spread, others=()):
    count = COUNT[chunk]
    rows = count * BLOCK
    fixed = [*hs, w_f, w_r, wdt, conv_x, conv_bc, spread, *others]
    added = jax.ShapeDtypeStruct((2, count, NSTATE, INNER), f32)
    blockdec = jax.ShapeDtypeStruct((count, 8, 2 * INNER), f32)
    shapes = [
        jax.ShapeDtypeStruct((rows, MIX), bf16),
        jax.ShapeDtypeStruct((rows, MIX), bf16),
        jax.ShapeDtypeStruct((8, rows), f32),
        jax.ShapeDtypeStruct((8, rows), f32),
        jax.ShapeDtypeStruct((8, rows), f32),
    ]
    scratch = [
        pltpu.VMEM((MIX // 128, EDGE + BLOCK, 128), f32),
        pltpu.VMEM((MIX // 128, EDGE + BLOCK, 128), f32),
        pltpu.VMEM((count, 8, BLOCK), f32),
        pltpu.VMEM((count, 16, BLOCK), bf16),
    ]
    if chunk == 0:
        shapes += [added, blockdec]
    else:
        shapes += [
            jax.ShapeDtypeStruct((2, BLOCKS, NSTATE, INNER), f32),
            jax.ShapeDtypeStruct((2, BLOCKS, 8, INNER), f32),
        ] + [jax.ShapeDtypeStruct((PAY, INNER), bf16)] * 4
        scratch += [pltpu.VMEM(a.shape, f32) for a in (added, blockdec)]
        scratch += [pltpu.VMEM((2, NSTATE, INNER), f32)]
    return pl.pallas_call(
        functools.partial(k1_body, chunk),
        in_specs=[SMEM] * 4 + [VMEM] * len(fixed),
        out_specs=[VMEM] * len(shapes),
        out_shape=shapes,
        scratch_shapes=scratch,
        compiler_params=params(24),
        cost_estimate=cost(rows * 6e6, rows * 4000),
        name="local_states",
    )(pieces, meta, dt_bias, rate, *fixed)


def k2_body(
    chunk, base, count, pieces, meta, skip_gain, h0, h1, h2, h3, w_f, w_r, conv_x, conv_bc,
    xb_f, xb_r, cum_i, dt_i, c_f, c_r, y_f, y_r, z_f, z_r, sf, sr, open_mask,
):
    ends = bounds_of(pieces)
    row_at = lax.broadcasted_iota(jnp.int32, (BLOCK, BLOCK), 0)
    col_at = lax.broadcasted_iota(jnp.int32, (BLOCK, BLOCK), 1)
    half = BLOCK // 2

    open_mask[0] = jnp.where(row_at >= col_at, 0.0, FAR)
    open_mask[1] = jnp.where(row_at <= col_at, 0.0, FAR)

    def mix(step, masked):
        g = step + base
        first = meta[0] + block_of(chunk, g) * BLOCK
        here, there = rows_at(step), rows_at(g)
        window = load_window((h0, h1, h2, h3), chunk, g)
        masks = None
        if masked:
            seg = seg_rows(ends, first)
            masks = (seg == seg[3:4, :]).astype(f32).T
            together = seg.T[:, 3:4] == seg[3:4, :]
            open_mask[2] = jnp.where(together & (row_at >= col_at), 0.0, FAR)
            open_mask[3] = jnp.where(together & (row_at <= col_at), 0.0, FAR)
        proj_f = jnp.dot(window[: EDGE + BLOCK], w_f[...], preferred_element_type=f32)
        proj_r = jnp.dot(window[EDGE:], w_r[...], preferred_element_type=f32)
        keep_rounded(sf, proj_f)
        keep_rounded(sr, proj_r)
        z_f[here, :] = silu(proj_f[EDGE:, NSTATE:].astype(bf16).astype(f32))
        z_r[here, :] = silu(proj_r[0:BLOCK, NSTATE:].astype(bf16).astype(f32))
        taps = tap_rows(conv_x, conv_bc)[3]
        cum = cum_i[:, there]
        cum_t = cum.T
        log_dt = jnp.log(dt_i[:, there]) - cum
        lane_head = lax.broadcasted_iota(jnp.int32, (BLOCK, INNER), 1) // HEAD_DIM
        skip = per_head(skip_gain, (1, INNER), 1, HEAD_DIM)
        for stream, xb, scratch, c_ref, y_ref in ((0, xb_f, sf, c_f, y_f), (1, xb_r, sr, c_r, y_r)):
            c_rows = conv_tile(scratch, 0, taps, stream == 1, masks)
            c_ref[here, :] = c_rows
            x = xb[there, 0:INNER]
            b = xb[there, INNER:MIX]
            heads = [jnp.where(lane_head == h, x, jnp.zeros_like(x)) for h in range(HEADS_HERE)]
            for part in range(2):
                rows = slice(part * half, (part + 1) * half)
                if stream == 0:
                    cols = slice(0, half) if part == 0 else slice(0, BLOCK)
                else:
                    cols = slice(0, BLOCK) if part == 0 else slice(half, BLOCK)
                scores = lax.dot_general(
                    c_rows[rows, :], b[cols, :], (((1,), (1,)), ((), ())), preferred_element_type=f32
                )
                mask = open_mask[(2 if masked else 0) + stream, rows, cols]
                total = x[rows, :].astype(f32) * skip
                for h in range(HEADS_HERE):
                    at = stream * HEADS_HERE + h
                    gap = (cum_t[rows, at : at + 1] + log_dt[at : at + 1, cols]) + mask
                    weight = (jnp.exp(gap) * scores).astype(bf16)
                    total = total + jnp.dot(weight, heads[h][cols, :], preferred_element_type=f32)
                at = pl.multiple_of(step * BLOCK + part * half, half)
                y_ref[pl.ds(at, half), :] = total

    @pl.loop(0, count)
    def _(step):
        crosses = has_boundary(ends, meta[0] + block_of(chunk, step + base) * BLOCK)
        pl.when(crosses)(lambda: mix(step, True))
        pl.when(jnp.logical_not(crosses))(lambda: mix(step, False))


def intra(chunk, base, count, pieces, meta, skip_gain, hs, w_f, w_r, conv_x, conv_bc, xb_f, xb_r, cum, dt):
    rows = count * BLOCK
    arrays = [*hs, w_f, w_r, conv_x, conv_bc, xb_f, xb_r, cum, dt]
    return pl.pallas_call(
        functools.partial(k2_body, chunk, base, count),
        in_specs=[SMEM] * 3 + [VMEM] * len(arrays),
        out_specs=[VMEM] * 6,
        out_shape=[jax.ShapeDtypeStruct((rows, NSTATE), bf16)] * 2
        + [jax.ShapeDtypeStruct((rows, INNER), f32)] * 4,
        scratch_shapes=[
            pltpu.VMEM((1, EDGE + BLOCK, 128), f32),
            pltpu.VMEM((1, EDGE + BLOCK, 128), f32),
            pltpu.VMEM((4, BLOCK, BLOCK), f32),
        ],
        compiler_params=params(16),
        cost_estimate=cost(rows * 5e6, rows * 5000),
        name="intra",
    )(pieces, meta, skip_gain, *arrays)


def state_rows(ref, stream):
    return ref[stream * QUARTER : (stream + 1) * QUARTER, :].astype(f32)


def put_payload(ref, states, decays):
    for stream in range(2):
        ref[stream * QUARTER : (stream + 1) * QUARTER, :] = states[stream].astype(bf16)
    ref[2 * QUARTER : PAY, :] = split_rows(decays)


def group_body(meta, own, r1, r2, r3, pre_s, pre_a, pay, stage):
    me = meta[1]
    for s, ref in enumerate((own, r1, r2, r3)):
        stage[lax.rem(me - s + 4, 4)] = ref[...]
    states, decays = [], []
    for stream in range(2):
        state = jnp.zeros((QUARTER, INNER), f32)
        decay = jnp.ones((1, INNER), f32)
        for step in range(4):
            k = step if stream == 0 else 3 - step
            pre_s[k, stream] = state
            pre_a[k, stream] = jnp.broadcast_to(decay, (8, INNER))
            one = stage[k]
            d = decays_of(one[2 * QUARTER :])[stream]
            state = d * state + one[stream * QUARTER : (stream + 1) * QUARTER].astype(f32)
            decay = decay * d
        states.append(state)
        decays.append(decay)
    put_payload(pay, states, decays)


def before_digit(place, stream, got):
    low_s, low_a = jnp.zeros((QUARTER, INNER), f32), jnp.ones((1, INNER), f32)
    for s in (1, 2, 3):
        there = s <= place
        state, decay = got[s if stream == 0 else 4 - s]
        low_s = jnp.where(there, low_s + low_a * state, low_s)
        low_a = jnp.where(there, low_a * decay, low_a)
    return low_s, low_a


def middle_body(meta, own, r1, r2, r3, low_o, low_ao, pay):
    digit = meta[2]
    states, decays = [], []
    rows = [decays_of(r[2 * QUARTER : PAY, :]) for r in (own, r1, r2, r3)]
    for stream in range(2):
        got = [(state_rows(r, stream), rows[s][stream]) for s, r in enumerate((own, r1, r2, r3))]
        place = digit if stream == 0 else 3 - digit
        low_s, low_a = before_digit(place, stream, got)
        low_o[stream] = low_s
        low_ao[stream] = jnp.broadcast_to(low_a, (8, INNER))
        total_s, total_a = got[0][1] * low_s + got[0][0], got[0][1] * low_a
        for s in (3, 2, 1):
            there = s > place
            state, decay = got[s if stream == 0 else 4 - s]
            total_s = jnp.where(there, decay * total_s + state, total_s)
            total_a = jnp.where(there, decay * total_a, total_a)
        states.append(total_s)
        decays.append(total_a)
    put_payload(pay, states, decays)


def top_body(meta, r1, r2, r3, low_i, low_ai, pre_s, pre_a, *outs):
    digit = meta[3]
    rows = [None] + [decays_of(r[2 * QUARTER : PAY, :]) for r in (r1, r2, r3)]
    for stream in range(2):
        got = [None] + [
            (state_rows(r, stream), rows[s + 1][stream]) for s, r in enumerate((r1, r2, r3))
        ]
        place = digit if stream == 0 else 3 - digit
        top_s, _ = before_digit(place, stream, got)
        group_s = low_ai[stream, 0:1, :] * top_s + low_i[stream]
        for s, ref in enumerate(outs):
            k = lax.rem(meta[1] + s, 4)
            member = pre_a[k, stream][0:1, :] * group_s + pre_s[k, stream]
            ref[stream * QUARTER : (stream + 1) * QUARTER, :] = member.astype(bf16)


def small_call(body, name, meta, arrays, shapes, scratch=()):
    return pl.pallas_call(
        body,
        in_specs=[SMEM] + [VMEM] * len(arrays),
        out_specs=[VMEM] * len(shapes),
        out_shape=shapes,
        scratch_shapes=list(scratch),
        compiler_params=params(6),
        cost_estimate=cost(2e6, 1e6),
        name=name,
    )(meta, *arrays)


PAYLOAD = jax.ShapeDtypeStruct((PAY, INNER), bf16)


def join_group(meta, arrays):
    shapes = [
        jax.ShapeDtypeStruct((4, 2, QUARTER, INNER), f32),
        jax.ShapeDtypeStruct((4, 2, 8, INNER), f32),
        PAYLOAD,
    ]
    return small_call(group_body, "join_group", meta, arrays, shapes, [pltpu.VMEM((4, PAY, INNER), bf16)])


def join_middle(meta, arrays):
    shapes = [
        jax.ShapeDtypeStruct((2, QUARTER, INNER), f32),
        jax.ShapeDtypeStruct((2, 8, INNER), f32),
        PAYLOAD,
    ]
    return small_call(middle_body, "join_middle", meta, arrays, shapes)


def join_top(meta, arrays):
    shapes = [jax.ShapeDtypeStruct((2 * QUARTER, INNER), bf16)] * 4
    return small_call(top_body, "join_top", meta, arrays, shapes)


def k3_body(meta, *refs):
    parts, refs = refs[: 6 * len(PARTS)], refs[6 * len(PARTS) :]
    fs, (starts, decays, q0, q1, q2, q3, gain, spread, g_f, g_r, sums, s_in) = refs[:2], refs[2:]
    for s, ref in enumerate((q0, q1, q2, q3)):
        at = pl.multiple_of(lax.rem(meta[1] - s + 4, 4) * QUARTER, QUARTER)
        for stream in range(2):
            s_in[stream, pl.ds(at, QUARTER), :] = state_rows(ref, stream)
    for part, (chunk, base, count) in enumerate(PARTS):
        c, y, z = (parts[6 * part + n : 6 * part + n + 2] for n in (0, 2, 4))
        for at in range(count):
            k = base + at
            b = block_of(chunk, k)
            to = slice(b * BLOCK, (b + 1) * BLOCK)
            rows = slice(at * BLOCK, (at + 1) * BLOCK)
            wide = rows_to_cols(fs[chunk][:, k * BLOCK : (k + 1) * BLOCK], spread[...])
            for stream, g_ref in ((0, g_f), (1, g_r)):
                state = starts[stream, b] + decays[stream, b, 0:1, :] * s_in[stream]
                carried = jnp.dot(c[stream][rows, :], state.astype(bf16), preferred_element_type=f32)
                mixed = y[stream][rows, :] + carried * wide[:, stream * INNER : (stream + 1) * INNER]
                gated = mixed * z[stream][rows, :]
                square = gated * gated
                sums[stream : stream + 1, to] = jnp.sum(
                    (square[:, 0:128] + square[:, 128:256]).T, axis=0, keepdims=True
                )
                g_ref[to, :] = (gated * gain[...]).astype(bf16)


def gate(meta, locals_, fs, starts, decays, quarters, gain, spread):
    m = BLOCKS * BLOCK
    arrays = [*locals_, *fs, starts, decays, *quarters, gain, spread]
    return pl.pallas_call(
        k3_body,
        in_specs=[SMEM] + [VMEM] * len(arrays),
        out_specs=[VMEM] * 3,
        out_shape=[
            jax.ShapeDtypeStruct((m, INNER), bf16),
            jax.ShapeDtypeStruct((m, INNER), bf16),
            jax.ShapeDtypeStruct((2, m), f32),
        ],
        scratch_shapes=[pltpu.VMEM((2, NSTATE, INNER), f32)],
        compiler_params=params(12),
        cost_estimate=cost(m * 5e5, m * 6000),
        name="gate",
    )(meta, *arrays)


def k4_body(half, g_f, g_r, s0, s1, s2, s3, w_f, w_r, spread, o0, o1, o2, o3):
    for k in range(HERE):
        rows = slice((half * HERE + k) * BLOCK, (half * HERE + k + 1) * BLOCK)
        total = (s0[:, rows] + s1[:, rows]) + (s2[:, rows] + s3[:, rows])
        scale = lax.rsqrt(total / E + EPSILON)
        scale = jnp.concatenate([scale, jnp.zeros((6, BLOCK), f32)], axis=0)
        wide = rows_to_cols(scale, spread[...])
        out_f = jnp.dot(g_f[rows, :], w_f[...], preferred_element_type=f32)
        out_r = jnp.dot(g_r[rows, :], w_r[...], preferred_element_type=f32)
        for s, ref in enumerate((o0, o1, o2, o3)):
            cols = slice(s * 128, (s + 1) * 128)
            part = out_f[:, cols] * wide[:, 0:128] + out_r[:, cols] * wide[:, 128:256]
            ref[k * BLOCK : (k + 1) * BLOCK, :] = part.astype(ref.dtype)


def project_out(half, kinds, g_f, g_r, sums, w_f, w_r, spread):
    m = HERE * BLOCK
    arrays = [g_f, g_r, *sums, w_f, w_r, spread]
    return pl.pallas_call(
        functools.partial(k4_body, half),
        in_specs=[VMEM] * len(arrays),
        out_specs=[VMEM] * 4,
        out_shape=[jax.ShapeDtypeStruct((m, 128), kind) for kind in kinds],
        compiler_params=params(12),
        cost_estimate=cost(m * 1e6, m * 3000),
        name="project_out",
    )(*arrays)


def join_body(a1, b1, a2, b2, o1, o2):
    o1[...] = (a1[...] + b1[...].astype(f32)).astype(bf16)
    o2[...] = (a2[...] + b2[...].astype(f32)).astype(bf16)


def join_shares(a1, b1, a2, b2):
    arrays = (a1, b1, a2, b2)
    shapes = [jax.ShapeDtypeStruct(a1.shape, bf16)] * 2
    return pl.pallas_call(
        join_body,
        in_specs=[VMEM] * len(arrays),
        out_specs=[VMEM] * len(shapes),
        out_shape=shapes,
        compiler_params=params(8),
        cost_estimate=cost(1e6, 3e6),
        name="join_shares",
    )(*arrays)


def last_body(a0, a1, a2, b0, b1, b2, out):
    for k, (own, one, other) in enumerate(((a0, a1, a2), (b0, b1, b2))):
        @pl.when(pl.program_id(0) == k)
        def _():
            out[...] = (own[...] + one[...].astype(f32) + other[...].astype(f32)).astype(bf16)


def last_sum(*arrays):
    m = HERE * BLOCK
    return pl.pallas_call(
        last_body,
        grid=(2,),
        in_specs=[whole(a.shape) for a in arrays],
        out_specs=pl.BlockSpec((m, 128), lambda g: (g, 0)),
        out_shape=jax.ShapeDtypeStruct((2 * m, 128), bf16),
        compiler_params=params(8),
        cost_estimate=cost(1e6, 3e6),
        name="last_sum",
    )(*arrays)


def orders(mp, n_mp, width):
    here = width // n_mp
    shape = (width, width)
    row = lax.broadcasted_iota(jnp.int32, shape, 0)
    col = lax.broadcasted_iota(jnp.int32, shape, 1)
    place = lax.rem(mp - row // here + n_mp, n_mp) * here + lax.rem(row, here)
    goal = lax.rem(mp + col // here, n_mp) * here + lax.rem(col, here)
    return [
        keep.astype(f32).astype(bf16)
        for keep in (place == col, width - 1 - place == col, goal == row, width - 1 - goal == row)
    ]


def prepare_body(n_mp, mp, w, o_f, o_r, o_dt, q_f, q_r):
    pick_f, pick_r, _, _ = orders(mp[0], n_mp, w.shape[0])
    moved = [jnp.dot(pick, w[...], preferred_element_type=f32) for pick in (pick_f, pick_r)]
    for rows, first, second in ((moved[0], o_f, q_f), (moved[1], o_r, q_r)):
        first[...] = rows[:, 0:MIX].astype(bf16)
        second[...] = rows[:, MIX : 2 * MIX].astype(bf16)
    lane = lax.broadcasted_iota(jnp.int32, (w.shape[0], 128), 1)
    steps = jnp.where(lane < HEADS_HERE, moved[0][:, 2 * MIX :], moved[1][:, 2 * MIX :])
    o_dt[...] = steps.T[0:8, :].astype(bf16)


def prepare_out_body(n_mp, mp, w_out, p_f, p_r):
    _, _, out_f, out_r = orders(mp[0], n_mp, w_out.shape[1])
    p_f[...] = jnp.dot(w_out[...], out_f, preferred_element_type=f32).astype(bf16)
    p_r[...] = jnp.dot(w_out[...], out_r, preferred_element_type=f32).astype(bf16)


def prepare(body, name, n_mp, mp, w, shapes):
    return pl.pallas_call(
        functools.partial(body, n_mp),
        in_specs=[SMEM, VMEM],
        out_specs=[VMEM] * len(shapes),
        out_shape=[jax.ShapeDtypeStruct(a, bf16) for a in shapes],
        compiler_params=params(16),
        cost_estimate=cost(1e9, 3e6),
        name=name,
    )(mp, w)


def row_spread():
    out = np.zeros((16, 256), np.float32)
    for part in range(2):
        out[part * 8, 0:128] = 1.0
        out[part * 8 + 1, 128:256] = 1.0
    return out


def around(array, axis, count, shift):
    return lax.ppermute(array, axis, [(i, (i + shift) % count) for i in range(count)])


def digit_perm(count, stride, shift):
    pairs = []
    for i in range(count):
        d = (i // stride) % 4
        pairs.append((i, i + (((d + shift) % 4) - d) * stride))
    return pairs


def shards(
    hidden, w_x, w_z, w_bc, w_dt, conv_x, conv_bc, dt_bias, decay_rate, skip_gain, norm_gain, w_out,
    piece_lengths,
):
    rows = hidden.shape[0]
    ctx, mp = lax.axis_index("ctx"), lax.axis_index("mp")
    n_ctx, n_mp = lax.axis_size("ctx"), lax.axis_size("mp")

    run, last = BLOCK, (1 + COUNT[0]) * BLOCK
    middle = hidden[run - EDGE : last + EDGE]
    hs_0 = [middle] + [around(middle, "mp", n_mp, s) for s in range(1, n_mp)]
    low = lax.ppermute(hidden[rows - EDGE :], "ctx", [(i, i + 1) for i in range(n_ctx - 1)])
    high = lax.ppermute(hidden[:EDGE], "ctx", [(i + 1, i) for i in range(n_ctx - 1)])
    outer = jnp.concatenate([low, hidden[: run + EDGE], hidden[last - EDGE :], high], axis=0)

    hs_1 = [outer] + [around(outer, "mp", n_mp, s) for s in range(1, n_mp)]
    width = w_x.shape[0]
    place = mp[None].astype(jnp.int32)
    spare = jnp.zeros((width, 128 - 2 * HEADS_HERE), bf16)
    w_1f, w_1r, wdt, w_2f, w_2r = prepare(
        prepare_body, "prepare", n_mp, place, jnp.concatenate([w_x, w_bc, w_z, w_dt, w_dt, spare], axis=1),
        [(width, MIX), (width, MIX), (8, width), (width, MIX), (width, MIX)],
    )

    gain = norm_gain[None, :]
    spread = jnp.asarray(head_spread(), bf16)
    spread_rows = jnp.asarray(row_spread(), bf16)
    meta = jnp.stack([ctx * rows, ctx % 4, (ctx // 4) % 4, (ctx // 16) % 4]).astype(jnp.int32)

    first = (piece_lengths, meta, dt_bias, decay_rate)
    weights_1 = (w_1f, w_1r, wdt, conv_x, conv_bc, spread)
    weights_2 = (w_2f, w_2r, conv_x, conv_bc)

    xb_f, xb_r, cum, dt, fs_0, *middle_states = local_states(0, *first, hs_0, *weights_1)
    arguments = [(piece_lengths, meta, skip_gain, hs_0, *weights_2, xb_f, xb_r, cum, dt)]
    done = []

    def beside(part, received):
        new = intra(*PARTS[part], *arguments[PARTS[part][0]])
        received, new = lax.optimization_barrier((received, tuple(new)))
        done.extend(new)
        return received

    hs_1 = beside(0, tuple(hs_1))
    xb_f, xb_r, cum, dt, fs_1, starts, decays, *pays = local_states(
        1, *first, hs_1, *weights_1, middle_states
    )
    pays, late, late_place = lax.optimization_barrier((pays, w_out, place))
    w_of, w_or = prepare(prepare_out_body, "prepare_out", n_mp, late_place, late, [w_out.shape] * 2)
    arguments.append((piece_lengths, meta, skip_gain, hs_1, *weights_2, xb_f, xb_r, cum, dt))

    def moved(arrays, stride):
        return [lax.ppermute(a, "ctx", digit_perm(n_ctx, stride, s)) for s, a in zip((1, 2, 3), arrays)]

    pre_s, pre_a, pay = join_group(meta, [pays[0]] + moved(pays[1:], 1))
    low_s, low_a, top = join_middle(meta, [pay] + beside(1, moved([pay] * 3, 4)))
    back = join_top(meta, beside(2, moved([top] * 3, 16)) + [low_s, low_a, pre_s, pre_a])
    quarters = [back[0]] + beside(3, moved(back[1:], 1))

    g_f, g_r, sums = gate(
        meta, done, (fs_0, fs_1), starts, decays, quarters, gain, spread
    )
    all_sums = [sums] + [around(sums, "mp", n_mp, s) for s in range(1, n_mp)]
    tail = (g_f, g_r, all_sums, w_of, w_or, spread_rows)
    own_a, up_a, far_a, down_a = project_out(0, (f32, f32, bf16, bf16), *tail)
    far_a = around(far_a, "mp", n_mp, 1)
    own_b, up_b, far_b, down_b = project_out(1, (f32, bf16, bf16, f32), *tail)
    far_b = around(far_b, "mp", n_mp, n_mp - 1)
    down_a, up_b = around(down_a, "mp", n_mp, n_mp - 1), around(up_b, "mp", n_mp, 1)
    up_a, down_b = join_shares(up_a, far_a, down_b, far_b)
    up_a, down_b = around(up_a, "mp", n_mp, 1), around(down_b, "mp", n_mp, n_mp - 1)
    return last_sum(own_a, down_a, up_a, own_b, up_b, down_b)


def solution(mesh):
    return jax.shard_map(
        shards,
        mesh=mesh,
        in_specs=(
            P("ctx", "mp"),
            P(None, "mp"),
            P(None, "mp"),
            P(),
            P(None, "mp"),
            P(None, "mp"),
            P(),
            P("mp"),
            P("mp"),
            P("mp"),
            P("mp"),
            P("mp", None),
            P(),
        ),
        out_specs=P("ctx", "mp"),
        check_vma=False,
    )
```
